128 devices in a mesh: nodes: 32 (over y, z, core), feat: 4 (over x).
Axes of the slice: x: 4, y: 4, z: 4, core: 2. Of those that a mesh axis runs over, the one named last changes fastest.
Arguments:
- features: bfloat16 [131072, 1024], P('nodes', 'feat'), may hold values from -6 to 6
- pair_count: int32 [32, 32], P('nodes'), may hold values from 1 to 2, as said below
- send_blocks: int32 [32, 32, 2], P('nodes'), may hold values from 0 to 31
- tile_src: int32 [1024, 4], P('nodes'), may hold values from 0 to 63, as said below
- tiles: bfloat16 [1024, 4, 128, 128], P('nodes'), may hold values from -0.25 to 0.25
- labels: int32 [131072], P('nodes'), may hold values from 0 to 15
- w_first: bfloat16 [1024, 1024], P('feat'), may hold values from -0.1875 to 0.1875
- b_first: float32 [1024], P('feat'), may hold values from -3 to 3
- w_second: bfloat16 [1024, 16], P('feat'), may hold values from -0.1875 to 0.1875
Outputs:
- grad_first: float32 [1024, 1024], P('feat', 'nodes')
- grad_bias: float32 [1024], P('feat')
- grad_second: float32 [1024, 16], P('feat')
The draws below stay inside these ranges and needn't reach their ends.
Inputs may be any that keep to these rules, and one draw needn't show every extreme that they name: pair_count[p, p] is 2 for every p. `tile_src`: the 32 rows of one partition name every slot 0 to 63 at least once.
All inputs are finite; a program needn't handle non-finite values.
Results may differ from the reference program's by a relative error of at most 0.015.
The reference program's roundings to bfloat16 on the way count: a program that leaves them out, or rounds other values in their place, can miss the bound.
Values may be sent and summed in bfloat16 or wider, within the bound.
No kernel may reach another device: no remote copies, remote signals or barrier semaphores. Data moves between devices by JAX's collectives and lax.ppermute only.
A program may use at most 128 MiB of HBM per device.

```python
import jax
import jax.numpy as jnp
from jax import lax

D = 1024
H = 1024
C = 16
BLK = 128
SLOTS = 2
PARTS_SIZE = 32
NB = 32
TPB = 4
NBLK = 1024
NODES = 131072


def draw_pair_count(key, part):
    key = jax.random.fold_in(key, 11)
    counts = jax.random.randint(key, (PARTS_SIZE, PARTS_SIZE), 1, SLOTS + 1)
    diag = jnp.arange(PARTS_SIZE)[:, None] == jnp.arange(PARTS_SIZE)[None, :]
    return jnp.where(diag, SLOTS, counts).astype(jnp.int32)


def draw_tile_src(key, part):
    key = jax.random.fold_in(key, 23)
    keys = jax.random.split(key, PARTS_SIZE)

    def single(sub):
        order = jax.random.permutation(sub, NB * TPB)
        return (order % (PARTS_SIZE * SLOTS)).reshape(NB, TPB)
    return jax.vmap(single)(keys).reshape(NBLK, TPB).astype(jnp.int32)


def set_ends(result, rng, smallest, high):
    longest = result.shape.index(max(result.shape))
    spots = []
    for shift in (0, 1):
        where = [jax.random.randint(jax.random.fold_in(rng, axis), (), 0, length) for axis, length in enumerate(result.shape)]
        where[longest] = (where[longest] + shift) % result.shape[longest]
        spots.append(tuple(where))
    return result.at[spots[0]].set(smallest).at[spots[1]].set(high)


def block_scale(rng, extent, shards, low, top_value):
    def one(axis_at, parts):
        heights = jax.random.uniform(jax.random.fold_in(jax.random.fold_in(rng, 6), axis_at), (parts,), jnp.float32, low / len(shards), top_value / len(shards))
        return jnp.repeat(jnp.exp(heights), extent[axis_at] // parts).reshape((-1,) + (1,) * (len(extent) - axis_at - 1))

    loudness = one(*shards[0])
    for cut in shards[1:]:
        loudness = loudness * one(*cut)
    return loudness


def gaussian(key, extent, deviation, reach, pieces=(), kind=jnp.bfloat16):
    factor_of = block_scale(key, extent, pieces, -0.22, 0.18) if pieces else 1.0
    result = jax.random.normal(key, extent, jnp.float32) * deviation * factor_of
    return jnp.minimum(jnp.maximum(result, -reach), reach).astype(kind)


def setup_inputs(seed: int = 0) -> dict:
    streams_of = jax.random.split(jax.random.key(seed), 10)
    return {
        "features": gaussian(streams_of[0], (NODES, D), 1.0, 6.0, ((0, 32), (1, 4))),
        "pair_count": draw_pair_count(jax.random.fold_in(streams_of[9], 71), 0),
        "send_blocks": set_ends(jax.random.randint(streams_of[2], (PARTS_SIZE, PARTS_SIZE, SLOTS), 0, NB), jax.random.fold_in(streams_of[2], 1), 0, NB - 1).astype(jnp.int32),
        "tile_src": draw_tile_src(jax.random.fold_in(streams_of[9], 71), 0),
        "tiles": gaussian(streams_of[4], (NBLK, TPB, BLK, BLK), (TPB * BLK) ** -0.5, 0.25, ((0, 32),)),
        "labels": set_ends(jax.random.randint(streams_of[5], (NODES,), 0, C), jax.random.fold_in(streams_of[5], 1), 0, C - 1).astype(jnp.int32),
        "w_first": gaussian(streams_of[6], (D, H), D ** -0.5, 0.1875, ((0, 4),)),
        "b_first": gaussian(streams_of[7], (H,), 0.5, 3.0, ((0, 4),), jnp.float32),
        "w_second": gaussian(streams_of[8], (H, C), H ** -0.5, 0.1875, ((0, 4),)),
    }


def reference(features, pair_count, send_blocks, tile_src, tiles, labels, w_first, b_first, w_second):
    high = lax.Precision.HIGHEST
    part_ids = jnp.arange(PARTS_SIZE, dtype=jnp.int32)
    tiles_part = tiles.reshape(PARTS_SIZE, NB, TPB, BLK, BLK)
    source_part = tile_src.reshape(PARTS_SIZE, NB, TPB)

    def weights_of(p):
        slot = source_part[p] % SLOTS
        owner = source_part[p] // SLOTS
        live = (slot < pair_count[p][owner]).astype(jnp.float32)
        return tiles_part[p].astype(jnp.float32) * live[:, :, None, None]

    def incoming(field, p):
        blocks = send_blocks[:, p, :]
        received = field[part_ids[:, None], blocks]
        width = field.shape[-1]
        return received.reshape(PARTS_SIZE * SLOTS, BLK, width)[source_part[p]]
    field_one = features.reshape(PARTS_SIZE, NB, BLK, D)

    def first_agg(p):
        source = incoming(field_one, p).astype(jnp.float32)
        summed = jnp.einsum('btij,btjf->bif', weights_of(p), source, precision=high)
        return (field_one[p].astype(jnp.float32) + summed).astype(jnp.bfloat16)
    agg_first = lax.map(first_agg, part_ids).reshape(NODES, D)
    pre = jnp.dot(agg_first, w_first, preferred_element_type=jnp.float32) + b_first
    hidden = jnp.maximum(pre, 0.0).astype(jnp.bfloat16)
    proj = jnp.dot(hidden, w_second, preferred_element_type=jnp.float32)
    field_two = proj.reshape(PARTS_SIZE, NB, BLK, C)

    def second_agg(p):
        source = incoming(field_two, p)
        return field_two[p] + jnp.einsum('btij,btjf->bif', weights_of(p), source, precision=high)
    logits = lax.map(second_agg, part_ids).reshape(NODES, C)
    expo = jnp.exp(logits)
    probs = expo / lax.optimization_barrier(jnp.sum(expo, axis=1, keepdims=True))
    onehot = (labels[:, None] == jnp.arange(C, dtype=jnp.int32)[None, :]).astype(jnp.float32)
    dlog = (probs - onehot) / jnp.sqrt(jnp.float32(NODES))
    dlog_b = dlog.astype(jnp.bfloat16).reshape(PARTS_SIZE, NB, BLK, C)

    def back_step(total, p):
        contrib = jnp.einsum('btij,bif->btjf', weights_of(p), dlog_b[p].astype(jnp.float32), precision=high)
        slotsum = jnp.zeros((PARTS_SIZE * SLOTS, BLK, C), jnp.float32)
        slotsum = slotsum.at[source_part[p].reshape(-1)].add(contrib.reshape(NB * TPB, BLK, C))
        total = total.at[part_ids[:, None], send_blocks[:, p, :]].add(slotsum.reshape(PARTS_SIZE, SLOTS, BLK, C))
        return (total, 0)
    spread, unused = lax.scan(back_step, jnp.zeros((PARTS_SIZE, NB, BLK, C), jnp.float32), part_ids)
    dproj = dlog + spread.reshape(NODES, C)
    dproj_b = dproj.astype(jnp.bfloat16)
    grad_second = jnp.dot(hidden.T, dproj_b, preferred_element_type=jnp.float32)
    dhid = jnp.dot(dproj_b, w_second.T, preferred_element_type=jnp.float32)
    dpre = jnp.where(pre > 0, dhid, jnp.float32(0.0))
    grad_bias = lax.optimization_barrier(jnp.sum(dpre, axis=0))
    grad_first = jnp.dot(agg_first.T, dpre.astype(jnp.bfloat16), preferred_element_type=jnp.float32)
    return (grad_first, grad_bias, grad_second)
```

```python
import functools
import math

import jax
import jax.numpy as jnp
from jax import lax
from jax.experimental import pallas as pl
from jax.experimental.pallas import tpu as pltpu
from jax.sharding import PartitionSpec as P

F32 = jnp.float32
BF16 = jnp.bfloat16
NT = (((1,), (1,)), ((), ()))
NN = (((1,), (0,)), ((), ()))
BLK = 128
MIB = 1 << 20


def params(mib):
    return pltpu.CompilerParams(vmem_limit_bytes=mib * MIB)


def cost(flops, nbytes):
    return pl.CostEstimate(flops=flops, bytes_accessed=nbytes, transcendentals=0)


def dot(a, b, dims):
    return lax.dot_general(a, b, dims, preferred_element_type=F32)


def pick_kernel(chunk, table, features, out, sems):
    slots = out.shape[0]

    def copy(k):
        rows = pl.ds(pl.multiple_of(table[k] * BLK, BLK), BLK)
        return pltpu.make_async_copy(
            features.at[rows, pl.ds(chunk * BLK, BLK)], out.at[k], sems.at[k]
        )

    @pl.loop(0, slots)
    def _(k):
        copy(k).start()

    @pl.loop(0, slots)
    def _(k):
        copy(k).wait()


def pick(features, table, chunk):
    slots = table.shape[0]
    return pl.pallas_call(
        functools.partial(pick_kernel, chunk),
        grid_spec=pltpu.PrefetchScalarGridSpec(
            num_scalar_prefetch=1,
            grid=(),
            in_specs=[pl.BlockSpec(memory_space=pl.ANY)],
            out_specs=pl.BlockSpec(memory_space=pl.ANY),
            scratch_shapes=[pltpu.SemaphoreType.DMA((slots,))],
        ),
        out_shape=jax.ShapeDtypeStruct((slots, BLK, BLK), BF16),
        compiler_params=params(4),
        cost_estimate=cost(0, 4 * MIB),
        name="pick",
    )(table, features)


def agg_kernel(src, counts, me, arrived, tiles, own, o0, o1, o2, o3, buf):
    group, per = tiles.shape[0], tiles.shape[1]
    g = pl.program_id(0)
    first = lax.rem(me[0] + g, pl.num_programs(0)) * group

    for b in range(group):
        rows, weights = [], []
        for t in range(per):
            slot = src[(first + b) * per + t]
            live = lax.rem(slot, 2) < counts[lax.div(slot, 2)]
            rows.append(arrived[slot])
            weights.append(tiles[b, t] * jnp.where(live, 1.0, 0.0).astype(BF16))
        total = dot(jnp.concatenate(weights, 1), jnp.concatenate(rows, 0), NN)
        mine = own[pl.ds(b * BLK, BLK), :].astype(F32)
        buf[pl.ds(b * BLK, BLK), :] = (mine + total).astype(BF16)
    for k, out in enumerate((o0, o1, o2, o3)):

        @pl.when(g == k)
        def _():
            out[...] = buf[...]


def aggregate(src, counts, me, arrived, tiles, features, chunk, nfeat):
    nblocks, per = tiles.shape[:2]
    group = nblocks // nfeat
    piece = jax.ShapeDtypeStruct((group * BLK, BLK), BF16)
    turn = lambda g, m: lax.rem(m[0] + g, nfeat)
    return pl.pallas_call(
        agg_kernel,
        grid_spec=pltpu.PrefetchScalarGridSpec(
            num_scalar_prefetch=3,
            grid=(nfeat,),
            in_specs=[
                pl.BlockSpec(arrived.shape, lambda g, s, c, m: (0, 0, 0)),
                pl.BlockSpec((group, per, BLK, BLK), lambda g, s, c, m: (turn(g, m), 0, 0, 0)),
                pl.BlockSpec((group * BLK, BLK), lambda g, s, c, m: (turn(g, m), chunk)),
            ],
            out_specs=[pl.BlockSpec(piece.shape, lambda g, s, c, m: (0, 0))] * nfeat,
            scratch_shapes=[pltpu.VMEM(piece.shape, BF16)],
        ),
        out_shape=[piece] * nfeat,
        compiler_params=params(20),
        cost_estimate=cost(nblocks * per * 2 * BLK**3, 8 * MIB),
        name="aggregate",
    )(src, counts, me, arrived, tiles, features)


def dense_kernel(nfeat, *refs):
    pieces, rest = refs[: 2 * nfeat], refs[2 * nfeat :]
    weights, (bias, second, hidden, proj) = rest[:nfeat], rest[nfeat:]
    pre = bias[...] + dot(
        weights[0][...], jnp.concatenate([pieces[0][...], pieces[nfeat][...]], 1), NT
    )
    for k in range(1, nfeat):
        pre += dot(
            weights[k][...], jnp.concatenate([pieces[k][...], pieces[nfeat + k][...]], 1), NT
        )
    hid = jnp.maximum(pre, 0.0).astype(BF16)
    hidden[...] = hid
    out = dot(second[...], hid, NN)
    for b in range(proj.shape[0]):
        proj[b] = out[:, b * BLK : (b + 1) * BLK]


def dense(pieces, weights, bias, second):
    nodes, nfeat = pieces[0].shape[0], len(weights)
    hid, width = weights[0].shape
    grades = second.shape[0]
    step = 256
    return pl.pallas_call(
        functools.partial(dense_kernel, nfeat),
        grid=(nodes // step,),
        in_specs=[pl.BlockSpec((step, BLK), lambda g: (g, 0))] * (2 * nfeat)
        + [pl.BlockSpec((hid, width), lambda g: (0, 0))] * nfeat
        + [
            pl.BlockSpec((hid, 1), lambda g: (0, 0)),
            pl.BlockSpec((grades, hid), lambda g: (0, 0)),
        ],
        out_specs=[
            pl.BlockSpec((hid, step), lambda g: (0, g)),
            pl.BlockSpec((step // BLK, grades, BLK), lambda g: (g, 0, 0)),
        ],
        out_shape=[
            jax.ShapeDtypeStruct((hid, nodes), BF16),
            jax.ShapeDtypeStruct((nodes // BLK, grades, BLK), F32),
        ],
        compiler_params=params(28),
        cost_estimate=cost(2 * nodes * hid * width * nfeat, 7 * MIB),
        name="dense",
    )(*pieces, *weights, bias, second)


def spread_kernel(table, me, p0, p1, p2, p3, whole, out):
    nfeat, group = 4, p0.shape[0]
    for k, piece in enumerate((p0, p1, p2, p3)):
        owner = lax.rem(me[0] + nfeat - k, nfeat)
        whole[pl.ds(owner * group, group)] = piece[...]

    @pl.loop(0, out.shape[0], unroll=8)
    def _(k):
        out[k] = whole[table[k]]


def spread(table, me, pieces):
    group, grades, _ = pieces[0].shape
    slots = table.shape[0]
    vmem = pl.BlockSpec(memory_space=pltpu.VMEM)
    return pl.pallas_call(
        spread_kernel,
        grid_spec=pltpu.PrefetchScalarGridSpec(
            num_scalar_prefetch=2,
            grid=(),
            in_specs=[vmem] * 4,
            out_specs=[vmem] * 2,
        ),
        out_shape=[
            jax.ShapeDtypeStruct((group * 4, grades, BLK), F32),
            jax.ShapeDtypeStruct((slots, grades, BLK), F32),
        ],
        compiler_params=params(4),
        cost_estimate=cost(0, MIB),
        name="spread",
    )(table, me, *pieces)


def logits_kernel(scale, src, counts, me, arrived, own, labels, tiles, dlog_out, slots_out, parts, sums):
    group, per = tiles.shape[0], tiles.shape[1]
    nslots, grades, _ = arrived.shape
    mine = dlog_out.shape[0]
    g = pl.program_id(0)

    @pl.when(g == 0)
    def _():
        sums[...] = jnp.zeros_like(sums)

        @pl.loop(0, nslots, unroll=4)
        def _(k):
            x = arrived[k]
            for i in range(3):
                y = x.astype(BF16)
                parts[k, pl.ds(i * grades, grades), :] = y
                x = x - y.astype(F32)

    for b in range(group):
        block = g * group + b
        slots, lives, rows = [], [], []
        for t in range(per):
            slot = src[block * per + t]
            live = jnp.where(lax.rem(slot, 2) < counts[lax.div(slot, 2)], 1.0, 0.0)
            slots.append(slot)
            lives.append(live)
            rows.append(parts[slot] * live.astype(BF16))
        weights = jnp.concatenate([tiles[b, t] for t in range(per)], 1)
        triple = dot(jnp.concatenate(rows, 1), weights, NT)
        logits = own[b] + (
            triple[:grades] + (triple[grades : 2 * grades] + triple[2 * grades :])
        )
        expo = jnp.exp(logits)
        probs = expo / jnp.sum(expo, axis=0, keepdims=True)
        grade = lax.broadcasted_iota(jnp.int32, (grades, BLK), 0)
        onehot = jnp.where(labels[pl.ds(b, 1), :] == grade, 1.0, 0.0)
        dlog = (probs - onehot) * scale

        @pl.when(lax.div(block, mine) == me[0])
        def _():
            dlog_out[lax.rem(block, mine)] = dlog

        back = dot(dlog.astype(BF16), weights, NN)
        for t in range(per):
            sums[slots[t]] += back[:, t * BLK : (t + 1) * BLK] * lives[t]

    @pl.when(g == pl.num_programs(0) - 1)
    def _():
        slots_out[...] = sums[...].astype(BF16)


def logits_back(src, counts, me, arrived, own, labels, tiles, scale, nfeat):
    nblocks, per = tiles.shape[:2]
    nslots, grades, _ = arrived.shape
    group = 8
    whole = lambda g, s, c, m: (0, 0, 0)
    return pl.pallas_call(
        functools.partial(logits_kernel, scale),
        grid_spec=pltpu.PrefetchScalarGridSpec(
            num_scalar_prefetch=3,
            grid=(nblocks // group,),
            in_specs=[
                pl.BlockSpec(arrived.shape, whole),
                pl.BlockSpec((group, grades, BLK), lambda g, s, c, m: (g, 0, 0)),
                pl.BlockSpec((group, BLK), lambda g, s, c, m: (g, 0)),
                pl.BlockSpec((group, per, BLK, BLK), lambda g, s, c, m: (g, 0, 0, 0)),
            ],
            out_specs=[
                pl.BlockSpec((nblocks // nfeat, grades, BLK), whole),
                pl.BlockSpec(arrived.shape, whole),
            ],
            scratch_shapes=[
                pltpu.VMEM((nslots, 3 * grades, BLK), BF16),
                pltpu.VMEM(arrived.shape, F32),
            ],
        ),
        out_shape=[
            jax.ShapeDtypeStruct((nblocks // nfeat, grades, BLK), F32),
            jax.ShapeDtypeStruct(arrived.shape, BF16),
        ],
        compiler_params=params(20),
        cost_estimate=cost(nblocks * per * 2 * 64 * BLK**2, 6 * MIB),
        name="logits",
    )(src, counts, me, arrived, own, labels, tiles)


def grads_kernel(nfeat, table, me, returned, dlog, hidden, second, *refs):
    pieces = refs[: 2 * nfeat]
    big = refs[2 * nfeat]
    small = refs[2 * nfeat + 1 : 3 * nfeat + 1]
    total, dproj, buf = refs[3 * nfeat + 1 :]
    group, grades, _ = dlog.shape
    g = pl.program_id(0)
    width = hidden.shape[0]

    @pl.when(g == 0)
    def _():
        total[pl.ds(0, group)] = dlog[...]

        @pl.loop(0, returned.shape[0], unroll=8)
        def _(k):
            at = table[k] - me[0] * group
            at = jnp.where((at >= 0) & (at < group), at, group)
            total[at] += returned[k].astype(F32)

        for b in range(group):
            dproj[:, b * BLK : (b + 1) * BLK] = total[b].astype(BF16)

    active = hidden[...]
    dproj_b = dproj[...]
    dpre = jnp.where(active > 0, dot(second[...], dproj_b, NN), 0.0)
    buf[pl.ds(0, grades), :] = dot(dproj_b, active, NT)
    part = dpre[:, :BLK]
    for i in range(1, dpre.shape[1] // BLK):
        part += dpre[:, i * BLK : (i + 1) * BLK]
    buf[pl.ds(grades, 8), :] = jnp.broadcast_to(
        jnp.sum(part.T, axis=0, keepdims=True), (8, width)
    )
    dpre_b = dpre.astype(BF16)
    for k in range(nfeat):
        owner = lax.rem(me[0] + nfeat - k, nfeat)
        both = jnp.concatenate([pieces[k][...], pieces[nfeat + k][...]], 1)
        grad = dot(dpre_b, both, NN).astype(BF16)
        big[:, owner] = grad.reshape(big.shape[0], big.shape[2], big.shape[3])
    for k in range(nfeat):

        @pl.when(g == k)
        def _():
            small[k][...] = buf[...]


def gradients(table, me, returned, dlog, hidden, second, pieces, parts):
    nfeat = len(pieces) // 2
    hid, nodes = hidden.shape
    group, grades, _ = dlog.shape
    width = hid // nfeat
    per = parts // nfeat
    turn = lambda g, m: lax.rem(m[0] + nfeat - g, nfeat)
    whole3 = lambda g, t, m: (0, 0, 0)
    whole2 = lambda g, t, m: (0, 0)
    small = jax.ShapeDtypeStruct((grades + 8, width), F32)
    return pl.pallas_call(
        functools.partial(grads_kernel, nfeat),
        grid_spec=pltpu.PrefetchScalarGridSpec(
            num_scalar_prefetch=2,
            grid=(nfeat,),
            in_specs=[
                pl.BlockSpec(returned.shape, whole3),
                pl.BlockSpec(dlog.shape, whole3),
                pl.BlockSpec((width, nodes), lambda g, t, m: (turn(g, m), 0)),
                pl.BlockSpec((width, grades), lambda g, t, m: (turn(g, m), 0)),
            ]
            + [pl.BlockSpec((nodes, BLK), whole2)] * (2 * nfeat),
            out_specs=[
                pl.BlockSpec(
                    (per, nfeat, hid // parts, width), lambda g, t, m: (turn(g, m), 0, 0, 0)
                )
            ]
            + [pl.BlockSpec(small.shape, whole2)] * nfeat,
            scratch_shapes=[
                pltpu.VMEM((group + 1, grades, BLK), F32),
                pltpu.VMEM((grades, nodes), BF16),
                pltpu.VMEM(small.shape, F32),
            ],
        ),
        out_shape=[jax.ShapeDtypeStruct((parts, nfeat, hid // parts, width), BF16)]
        + [small] * nfeat,
        compiler_params=params(32),
        cost_estimate=cost(2 * nodes * hid * hid, 8 * MIB),
        name="gradients",
    )(table, me, returned, dlog, hidden, second, *pieces)


def total_kernel(arrived, out, acc):
    g = pl.program_id(0)

    @pl.when(g == 0)
    def _():
        acc[...] = jnp.zeros_like(acc)

    total = arrived[0].astype(F32)
    for i in range(1, arrived.shape[0]):
        total += arrived[i].astype(F32)
    acc[...] += total

    @pl.when(g == pl.num_programs(0) - 1)
    def _():
        out[...] = acc[...].T


def total(arrived):
    n, cols, rows = arrived.shape
    step = 16
    return pl.pallas_call(
        total_kernel,
        grid=(n // step,),
        in_specs=[pl.BlockSpec((step, cols, rows), lambda g: (g, 0, 0))],
        out_specs=pl.BlockSpec((rows, cols), lambda g: (0, 0)),
        out_shape=jax.ShapeDtypeStruct((rows, cols), F32),
        scratch_shapes=[pltpu.VMEM((cols, rows), F32)],
        compiler_params=params(8),
        cost_estimate=cost(0, 2 * MIB),
        name="total",
    )(arrived)


def shards(features, pair_count, send_blocks, tile_src, tiles, labels, w_first, b_first, w_second):
    nblocks = tile_src.shape[0]
    parts = lax.axis_size("nodes")
    nfeat = lax.axis_size("feat")
    slots = send_blocks.shape[2]
    grades = w_second.shape[1]
    hid = w_first.shape[1]
    axis = lax.axis_index("feat").astype(jnp.int32)
    me = axis.reshape(1)
    table = send_blocks.reshape(parts * slots)
    src = tile_src.reshape(-1)
    counts = pair_count.reshape(-1)

    def ahead(x, k):
        return lax.ppermute(x, "feat", [(i, (i + k) % nfeat) for i in range(nfeat)])

    def swap(x):
        shaped = x.reshape(parts, slots, *x.shape[1:])
        moved = lax.all_to_all(shaped, "nodes", split_axis=0, concat_axis=0, tiled=True)
        return moved.reshape(x.shape)

    arrived = [swap(pick(features, table, c)) for c in range(2)]

    flat = w_first.T
    weights = [flat] + [ahead(flat, k) for k in range(1, nfeat)]
    consts = jnp.concatenate(
        [w_second.T.astype(F32), jnp.broadcast_to(b_first[None], (8, b_first.shape[0]))], 0
    )
    turned = [consts] + [ahead(consts, k) for k in range(1, nfeat)]
    ring = jnp.stack([turned[k] for k in (3, 2, 1, 0, 3, 2, 1)])
    ordered = lax.dynamic_slice_in_dim(ring, nfeat - 1 - axis, nfeat, 0)
    second_t = ordered[:, :grades].transpose(1, 0, 2).reshape(grades, hid).astype(BF16)
    bias = ordered[:, grades].reshape(hid, 1)
    second = second_t.T

    pieces = []
    for c in range(2):
        made = aggregate(src, counts, me, arrived[c], tiles, features, c, nfeat)
        pieces += [made[0]] + [ahead(made[k], k) for k in range(1, nfeat)]
    hidden, proj = dense(pieces, weights, bias, second_t)

    projs = [proj] + [ahead(proj, k) for k in range(1, nfeat)]
    own, send = spread(table, me, projs)
    scale = 1.0 / math.sqrt(nblocks * BLK * parts)
    dlog, slotsum = logits_back(
        src, counts, me, swap(send), own, labels.reshape(nblocks, BLK), tiles, scale, nfeat
    )
    big, *small = gradients(
        table, me, swap(slotsum), dlog, hidden, second, pieces, parts
    )
    moved = lax.all_to_all(
        big.reshape(parts * nfeat, *big.shape[2:]),
        ("nodes", "feat"),
        split_axis=0,
        concat_axis=0,
        tiled=True,
    )
    rest = small[0]
    for k in range(1, nfeat):
        rest = rest + ahead(small[k], nfeat - k)
    for bit in (1, 2, 4, 8, 16):
        rest = rest + lax.ppermute(rest, "nodes", [(i, i ^ bit) for i in range(parts)])
    return total(moved), rest[grades], rest[:grades].T


def solution(mesh):
    placed = (
        P("nodes", "feat"),
        P("nodes", None),
        P("nodes", None, None),
        P("nodes", None),
        P("nodes", None, None, None),
        P("nodes"),
        P("feat", None),
        P("feat"),
        P("feat", None),
    )
    return jax.shard_map(
        shards,
        mesh=mesh,
        in_specs=placed,
        out_specs=(P("feat", "nodes"), P("feat"), P("feat", None)),
        check_vma=False,
    )
```

```python
import functools
import math

import jax
import jax.numpy as jnp
from jax import lax
from jax.experimental import pallas as pl
from jax.experimental.pallas import tpu as pltpu
from jax.sharding import PartitionSpec as P

F32 = jnp.float32
BF16 = jnp.bfloat16
NT = (((1,), (1,)), ((), ()))
NN = (((1,), (0,)), ((), ()))
BLK = 128
MIB = 1 << 20


def params(mib):
    return pltpu.CompilerParams(vmem_limit_bytes=mib * MIB)


def cost(flops, nbytes):
    return pl.CostEstimate(flops=flops, bytes_accessed=nbytes, transcendentals=0)


def dot(a, b, dims):
    return lax.dot_general(a, b, dims, preferred_element_type=F32)


def pick_kernel(chunk, table, features, out, sem):
    slots = out.shape[0]

    @pl.loop(0, slots, unroll=8)
    def _(k):
        rows = pl.ds(pl.multiple_of(table[k] * BLK, BLK), BLK)
        pltpu.make_async_copy(
            features.at[rows, pl.ds(chunk * BLK, BLK)], out.at[k], sem
        ).start()

    pltpu.make_async_copy(out, out, sem).wait()


def pick(features, table, chunk):
    slots = table.shape[0]
    return pl.pallas_call(
        functools.partial(pick_kernel, chunk),
        grid_spec=pltpu.PrefetchScalarGridSpec(
            num_scalar_prefetch=1,
            grid=(),
            in_specs=[pl.BlockSpec(memory_space=pltpu.HBM)],
            out_specs=pl.BlockSpec(memory_space=pltpu.HBM),
            scratch_shapes=[pltpu.SemaphoreType.DMA],
        ),
        out_shape=pltpu.HBM((slots, BLK, BLK), BF16),
        compiler_params=params(4),
        cost_estimate=cost(0, 4 * MIB),
        name="pick",
    )(table, features)


def stage_kernel(x, out, sem):
    copy = pltpu.make_async_copy(x, out, sem)
    copy.start()
    copy.wait()


def stage(x):
    return pl.pallas_call(
        stage_kernel,
        in_specs=[pl.BlockSpec(memory_space=pltpu.HBM)],
        out_specs=pl.BlockSpec(memory_space=pltpu.VMEM),
        out_shape=pltpu.VMEM(x.shape, x.dtype),
        scratch_shapes=[pltpu.SemaphoreType.DMA],
        compiler_params=params(4),
        cost_estimate=cost(0, x.size * 2),
        name="stage",
    )(x)


def agg_kernel(which, group, nfeat, src, counts, me, arrived, tiles, own, *outs):
    per = tiles.shape[1]
    for k, out in zip(which, outs):
        first = lax.rem(me[0] + k, nfeat) * group
        for b in range(group):
            rows, weights = [], []
            for t in range(per):
                slot = src[(first + b) * per + t]
                live = lax.rem(slot, 2) < counts[lax.div(slot, 2)]
                rows.append(arrived[slot])
                weights.append(tiles[first + b, t] * jnp.where(live, 1.0, 0.0).astype(BF16))
            total = dot(jnp.concatenate(weights, 1), jnp.concatenate(rows, 0), NN)
            at = pl.ds(pl.multiple_of((first + b) * BLK, BLK), BLK)
            out[pl.ds(b * BLK, BLK), :] = (own[at, :].astype(F32) + total).astype(BF16)


def aggregate(src, counts, me, arrived, tiles, features, chunk, nfeat, which):
    nblocks, per = tiles.shape[:2]
    group = nblocks // nfeat
    piece = jax.ShapeDtypeStruct((group * BLK, BLK), BF16)
    vmem = pl.BlockSpec(memory_space=pltpu.VMEM)
    return pl.pallas_call(
        functools.partial(agg_kernel, which, group, nfeat),
        grid_spec=pltpu.PrefetchScalarGridSpec(
            num_scalar_prefetch=3,
            grid=(1,),
            in_specs=[
                vmem,
                vmem,
                pl.BlockSpec((nblocks * BLK, BLK), lambda g, s, c, m: (0, chunk)),
            ],
            out_specs=[vmem] * len(which),
        ),
        out_shape=[piece] * len(which),
        compiler_params=params(12),
        cost_estimate=cost(len(which) * group * per * 2 * BLK**3, 8 * MIB),
        name="aggregate",
    )(src, counts, me, arrived, tiles, features)


def early_kernel(own, p0, p1, p2, p3, w0, w1, w2, w3, bias, pre):
    first = jnp.concatenate([p0[...], own[...]], 1)
    later = jnp.concatenate([p1[...], p2[...], p3[...]], 1)
    weights = jnp.concatenate([w1[:, :BLK], w2[:, :BLK], w3[:, :BLK]], 1)
    pre[...] = (bias[...] + dot(w0[...], first, NT)) + dot(weights, later, NT)


def early(own, pieces, weights, bias):
    nodes = own.shape[0]
    hid, width = weights[0].shape
    step = 256
    return pl.pallas_call(
        early_kernel,
        grid=(nodes // step,),
        in_specs=[pl.BlockSpec((step, BLK), lambda g: (g, 0))] * 5
        + [pl.BlockSpec((hid, width), lambda g: (0, 0))] * 4
        + [pl.BlockSpec((hid, 1), lambda g: (0, 0))],
        out_specs=pl.BlockSpec((hid, step), lambda g: (0, g)),
        out_shape=jax.ShapeDtypeStruct((hid, nodes), F32),
        compiler_params=params(20),
        cost_estimate=cost(2 * nodes * hid * 5 * BLK, 7 * MIB),
        name="early",
    )(own, *pieces, *weights, bias)


def dense_kernel(pre, p1, p2, p3, w1, w2, w3, second, hidden, proj):
    later = jnp.concatenate([p1[...], p2[...], p3[...]], 1)
    weights = jnp.concatenate([w1[:, BLK:], w2[:, BLK:], w3[:, BLK:]], 1)
    hid = jnp.maximum(pre[...] + dot(weights, later, NT), 0.0).astype(BF16)
    hidden[...] = hid
    out = dot(second[...], hid, NN)
    for b in range(proj.shape[0]):
        proj[b] = out[:, b * BLK : (b + 1) * BLK]


def dense(pre, pieces, weights, second):
    hid, nodes = pre.shape
    width = weights[0].shape[1]
    grades = second.shape[0]
    step = 256
    return pl.pallas_call(
        dense_kernel,
        grid=(nodes // step,),
        in_specs=[pl.BlockSpec((hid, step), lambda g: (0, g))]
        + [pl.BlockSpec((step, BLK), lambda g: (g, 0))] * 3
        + [pl.BlockSpec((hid, width), lambda g: (0, 0))] * 3
        + [pl.BlockSpec((grades, hid), lambda g: (0, 0))],
        out_specs=[
            pl.BlockSpec((hid, step), lambda g: (0, g)),
            pl.BlockSpec((step // BLK, grades, BLK), lambda g: (g, 0, 0)),
        ],
        out_shape=[
            jax.ShapeDtypeStruct((hid, nodes), BF16),
            jax.ShapeDtypeStruct((nodes // BLK, grades, BLK), F32),
        ],
        compiler_params=params(20),
        cost_estimate=cost(2 * nodes * hid * 3 * BLK, 9 * MIB),
        name="dense",
    )(pre, *pieces, *weights, second)


def spread_kernel(table, me, p0, p1, p2, p3, whole, out):
    nfeat, group = 4, p0.shape[0]
    for k, piece in enumerate((p0, p1, p2, p3)):
        owner = lax.rem(me[0] + nfeat - k, nfeat)
        whole[pl.ds(owner * group, group)] = piece[...]

    @pl.loop(0, out.shape[0], unroll=8)
    def _(k):
        out[k] = whole[table[k]]


def spread(table, me, pieces):
    group, grades, _ = pieces[0].shape
    slots = table.shape[0]
    vmem = pl.BlockSpec(memory_space=pltpu.VMEM)
    return pl.pallas_call(
        spread_kernel,
        grid_spec=pltpu.PrefetchScalarGridSpec(
            num_scalar_prefetch=2,
            grid=(),
            in_specs=[vmem] * 4,
            out_specs=[vmem] * 2,
        ),
        out_shape=[
            jax.ShapeDtypeStruct((group * 4, grades, BLK), F32),
            jax.ShapeDtypeStruct((slots, grades, BLK), F32),
        ],
        compiler_params=params(4),
        cost_estimate=cost(0, MIB),
        name="spread",
    )(table, me, *pieces)


def logits_kernel(
    scale, src, counts, me, arrived, own, labels, tiles, dlog_out, slots_out, parts, field, grad_b, sums
):
    nblocks, per = tiles.shape[:2]
    nslots, grades, _ = arrived.shape
    mine = dlog_out.shape[0]

    def live_of(slot):
        return jnp.where(lax.rem(slot, 2) < counts[lax.div(slot, 2)], 1.0, 0.0)

    x = arrived[...]
    for i in range(3):
        y = x.astype(BF16)
        parts[:, i * grades : (i + 1) * grades, :] = y
        x = x - y.astype(F32)

    @pl.loop(0, nblocks, unroll=8)
    def _(b):
        rows, weights = [], []
        for t in range(per):
            slot = src[b * per + t]
            rows.append(parts[slot] * live_of(slot).astype(BF16))
            weights.append(tiles[b, t])
        triple = dot(jnp.concatenate(rows, 1), jnp.concatenate(weights, 1), NT)
        field[b] = own[b] + (
            triple[:grades] + (triple[grades : 2 * grades] + triple[2 * grades :])
        )

    expo = jnp.exp(field[...])
    probs = expo / jnp.sum(expo, axis=1, keepdims=True)
    grade = lax.broadcasted_iota(jnp.int32, field.shape, 1)
    onehot = jnp.where(labels[...] == grade, 1.0, 0.0)
    dlog = (probs - onehot) * scale
    field[...] = dlog
    grad_b[...] = dlog.astype(BF16)
    dlog_out[...] = field[pl.ds(me[0] * mine, mine)]
    sums[...] = jnp.zeros_like(sums)

    @pl.loop(0, nblocks, unroll=8)
    def _(b):
        back = dot(grad_b[b], jnp.concatenate([tiles[b, t] for t in range(per)], 1), NN)
        for t in range(per):
            slot = src[b * per + t]
            sums[slot] += back[:, t * BLK : (t + 1) * BLK] * live_of(slot)

    slots_out[...] = sums[...].astype(BF16)


def logits_back(src, counts, me, arrived, own, labels, tiles, scale, nfeat):
    nblocks, per = tiles.shape[:2]
    nslots, grades, _ = arrived.shape
    vmem = pl.BlockSpec(memory_space=pltpu.VMEM)
    return pl.pallas_call(
        functools.partial(logits_kernel, scale),
        grid_spec=pltpu.PrefetchScalarGridSpec(
            num_scalar_prefetch=3,
            grid=(),
            in_specs=[vmem] * 4,
            out_specs=[vmem] * 2,
            scratch_shapes=[
                pltpu.VMEM((nslots, 3 * grades, BLK), BF16),
                pltpu.VMEM((nblocks, grades, BLK), F32),
                pltpu.VMEM((nblocks, grades, BLK), BF16),
                pltpu.VMEM(arrived.shape, F32),
            ],
        ),
        out_shape=[
            jax.ShapeDtypeStruct((nblocks // nfeat, grades, BLK), F32),
            jax.ShapeDtypeStruct(arrived.shape, BF16),
        ],
        compiler_params=params(8),
        cost_estimate=cost(nblocks * per * 2 * 64 * BLK**2, 6 * MIB),
        name="logits",
    )(src, counts, me, arrived, own, labels, tiles)


def small_kernel(table, me, returned, dlog, hidden, second, dpre_out, *refs):
    small, (total, dproj, buf) = refs[:-3], refs[-3:]
    group, grades, _ = dlog.shape
    g = pl.program_id(0)
    width = hidden.shape[0]

    @pl.when(g == 0)
    def _():
        total[pl.ds(0, group)] = dlog[...]
        buf[...] = jnp.zeros_like(buf)

        @pl.loop(0, returned.shape[0], unroll=8)
        def _(k):
            at = table[k] - me[0] * group
            at = jnp.where((at >= 0) & (at < group), at, group)
            total[at] += returned[k].astype(F32)

        for b in range(group):
            dproj[:, b * BLK : (b + 1) * BLK] = total[b].astype(BF16)

    active = hidden[...]
    dproj_b = dproj[...]
    dpre = jnp.where(active > 0, dot(second[...], dproj_b, NN), 0.0)
    dpre_out[...] = dpre.astype(BF16)
    buf[pl.ds(0, grades), :] = dot(dproj_b, active, NT)
    part = dpre[:, :BLK]
    for i in range(1, dpre.shape[1] // BLK):
        part += dpre[:, i * BLK : (i + 1) * BLK]
    buf[pl.ds(grades, 8), :] = jnp.broadcast_to(
        jnp.sum(part.T, axis=0, keepdims=True), (8, width)
    )
    for k, out in enumerate(small):

        @pl.when(g == k)
        def _():
            out[...] = buf[...]


def small_gradients(table, me, returned, dlog, hidden, second, nfeat):
    hid, nodes = hidden.shape
    group, grades, _ = dlog.shape
    width = hid // nfeat
    turn = lambda g, m: lax.rem(m[0] + nfeat - g, nfeat)
    whole3 = lambda g, t, m: (0, 0, 0)
    small = jax.ShapeDtypeStruct((32, width), F32)
    return pl.pallas_call(
        small_kernel,
        grid_spec=pltpu.PrefetchScalarGridSpec(
            num_scalar_prefetch=2,
            grid=(nfeat,),
            in_specs=[
                pl.BlockSpec(returned.shape, whole3),
                pl.BlockSpec(dlog.shape, whole3),
                pl.BlockSpec((width, nodes), lambda g, t, m: (turn(g, m), 0)),
                pl.BlockSpec((width, grades), lambda g, t, m: (turn(g, m), 0)),
            ],
            out_specs=[pl.BlockSpec((width, nodes), lambda g, t, m: (turn(g, m), 0))]
            + [pl.BlockSpec(small.shape, lambda g, t, m: (0, 0))] * nfeat,
            scratch_shapes=[
                pltpu.VMEM((group + 1, grades, BLK), F32),
                pltpu.VMEM((grades, nodes), BF16),
                pltpu.VMEM(small.shape, F32),
            ],
        ),
        out_shape=[jax.ShapeDtypeStruct((hid, nodes), BF16)] + [small] * nfeat,
        compiler_params=params(16),
        cost_estimate=cost(2 * nodes * hid * 256, 4 * MIB),
        name="small_gradients",
    )(table, me, returned, dlog, hidden, second)


def big_kernel(me, dpre, *refs):
    pieces, out = refs[:-1], refs[-1]
    nfeat = len(pieces) // 2
    for k in range(nfeat):

        @pl.when(pl.program_id(0) == k)
        def _():
            both = jnp.concatenate([pieces[k][...], pieces[nfeat + k][...]], 1)
            grad = dot(dpre[...], both, NN).astype(BF16)
            out[...] = grad.reshape(out.shape)


def big_gradient(me, dpre, pieces, parts):
    nfeat = len(pieces) // 2
    hid, nodes = dpre.shape
    whole = lambda g, m: (0, 0)
    return pl.pallas_call(
        big_kernel,
        grid_spec=pltpu.PrefetchScalarGridSpec(
            num_scalar_prefetch=1,
            grid=(nfeat,),
            in_specs=[pl.BlockSpec((hid, nodes), whole)]
            + [pl.BlockSpec((nodes, BLK), whole)] * (2 * nfeat),
            out_specs=pl.BlockSpec(
                (parts, 1, hid // parts, 2 * BLK),
                lambda g, m: (0, lax.rem(m[0] + nfeat - g, nfeat), 0, 0),
            ),
        ),
        out_shape=pltpu.HBM((parts, nfeat, hid // parts, 2 * BLK), BF16),
        compiler_params=params(24),
        cost_estimate=cost(2 * nodes * hid * hid, 6 * MIB),
        name="big_gradient",
    )(me, dpre, *pieces)


def total_kernel(arrived, out, acc):
    g = pl.program_id(0)

    @pl.when(g == 0)
    def _():
        acc[...] = jnp.zeros_like(acc)

    total = arrived[0].astype(F32)
    for i in range(1, arrived.shape[0]):
        total += arrived[i].astype(F32)
    acc[...] += total

    @pl.when(g == pl.num_programs(0) - 1)
    def _():
        out[...] = acc[...]


def total(arrived):
    n, cols, rows = arrived.shape
    step = n // 8
    return pl.pallas_call(
        total_kernel,
        grid=(n // step,),
        in_specs=[pl.BlockSpec((step, cols, rows), lambda g: (g, 0, 0))],
        out_specs=pl.BlockSpec((cols, rows), lambda g: (0, 0)),
        out_shape=jax.ShapeDtypeStruct((cols, rows), F32),
        scratch_shapes=[pltpu.VMEM((cols, rows), F32)],
        compiler_params=params(8),
        cost_estimate=cost(0, 2 * MIB),
        name="total",
    )(arrived)


def shards(features, pair_count, send_blocks, tile_src, tiles, labels, w_first, b_first, w_second):
    nblocks = tile_src.shape[0]
    parts = lax.axis_size("nodes")
    nfeat = lax.axis_size("feat")
    slots = send_blocks.shape[2]
    grades = w_second.shape[1]
    hid = w_first.shape[1]
    axis = lax.axis_index("feat").astype(jnp.int32)
    me = axis.reshape(1)
    table = send_blocks.reshape(parts * slots)
    src = tile_src.reshape(-1)
    counts = pair_count.reshape(-1)

    def ahead(x, k):
        return lax.ppermute(x, "feat", [(i, (i + k) % nfeat) for i in range(nfeat)])

    def swap(x):
        shaped = x.reshape(parts, slots, *x.shape[1:])
        moved = lax.all_to_all(shaped, "nodes", split_axis=0, concat_axis=0, tiled=True)
        return moved.reshape(x.shape)

    arrived = [swap(pick(features, table, c)) for c in range(2)]

    flat = w_first.T
    weights = [flat] + [ahead(flat, k) for k in range(1, nfeat)]
    consts = jnp.concatenate(
        [w_second.T.astype(F32), jnp.broadcast_to(b_first[None], (8, b_first.shape[0]))], 0
    )
    turned = [consts] + [ahead(consts, k) for k in range(1, nfeat)]
    ring = jnp.stack([turned[k] for k in (3, 2, 1, 0, 3, 2, 1)])
    ordered = lax.dynamic_slice_in_dim(ring, nfeat - 1 - axis, nfeat, 0)
    second_t = ordered[:, :grades].transpose(1, 0, 2).reshape(grades, hid).astype(BF16)
    bias = ordered[:, grades].reshape(hid, 1)
    second = second_t.T

    staged = stage(tiles)
    others = (2, 1, 3)
    make = functools.partial(aggregate, src, counts, me)
    first = [None] * nfeat
    *sent, first[0] = make(arrived[0], staged, features, 0, nfeat, others + (0,))
    for k, piece in zip(others, sent):
        first[k] = ahead(piece, k)
    last = [None] * nfeat
    for k, piece in zip(others, make(arrived[1], staged, features, 1, nfeat, others)):
        last[k] = ahead(piece, k)
    (last[0],) = make(arrived[1], staged, features, 1, nfeat, (0,))
    pre = early(last[0], first, weights, bias)
    hidden, proj = dense(pre, last[1:], weights[1:], second_t)

    projs = [proj] + [ahead(proj, k) for k in range(1, nfeat)]
    own, send = spread(table, me, projs)
    scale = 1.0 / math.sqrt(nblocks * BLK * parts)
    dlog, slotsum = logits_back(
        src, counts, me, swap(send), own, labels.reshape(nblocks, 1, BLK), staged, scale, nfeat
    )
    dpre, *small = small_gradients(table, me, swap(slotsum), dlog, hidden, second, nfeat)
    rest = small[0]
    for k in range(1, nfeat):
        rest = rest + ahead(small[k], nfeat - k)
    everyone = lax.all_gather(rest, "nodes", axis=0)
    big = big_gradient(me, dpre, first + last, parts)
    moved = lax.all_to_all(
        big.reshape(parts * nfeat, *big.shape[2:]),
        ("nodes", "feat"),
        split_axis=0,
        concat_axis=0,
        tiled=True,
    )
    rest = total(everyone)
    return total(moved).T, rest[grades], rest[:grades].T


def solution(mesh):
    placed = (
        P("nodes", "feat"),
        P("nodes", None),
        P("nodes", None, None),
        P("nodes", None),
        P("nodes", None, None, None),
        P("nodes"),
        P("feat", None),
        P("feat"),
        P("feat", None),
    )
    return jax.shard_map(
        shards,
        mesh=mesh,
        in_specs=placed,
        out_specs=(P("feat", "nodes"), P("feat"), P("feat", None)),
        check_vma=False,
    )
```

```python
import functools
import math

import jax
import jax.numpy as jnp
from jax import lax
from jax.experimental import pallas as pl
from jax.experimental.pallas import tpu as pltpu
from jax.sharding import PartitionSpec as P

F32 = jnp.float32
BF16 = jnp.bfloat16
NT = (((1,), (1,)), ((), ()))
NN = (((1,), (0,)), ((), ()))
BLK = 128
MIB = 1 << 20


def params(mib):
    return pltpu.CompilerParams(vmem_limit_bytes=mib * MIB)


def cost(flops, nbytes):
    return pl.CostEstimate(flops=flops, bytes_accessed=nbytes, transcendentals=0)


def dot(a, b, dims):
    return lax.dot_general(a, b, dims, preferred_element_type=F32)


def in_hbm(x):
    return pltpu.with_memory_space_constraint(x, pltpu.HBM)


def pick_kernel(chunk, table, features, out, sem):
    slots = out.shape[0]

    @pl.loop(0, slots, unroll=8)
    def _(k):
        rows = pl.ds(pl.multiple_of(table[k] * BLK, BLK), BLK)
        pltpu.make_async_copy(
            features.at[rows, pl.ds(chunk * BLK, BLK)], out.at[k], sem
        ).start()

    pltpu.make_async_copy(out, out, sem).wait()


def pick(features, table, chunk):
    slots = table.shape[0]
    return pl.pallas_call(
        functools.partial(pick_kernel, chunk),
        grid_spec=pltpu.PrefetchScalarGridSpec(
            num_scalar_prefetch=1,
            grid=(),
            in_specs=[pl.BlockSpec(memory_space=pltpu.HBM)],
            out_specs=pl.BlockSpec(memory_space=pltpu.HBM),
            scratch_shapes=[pltpu.SemaphoreType.DMA],
        ),
        out_shape=pltpu.HBM((slots, BLK, BLK), BF16),
        compiler_params=params(4),
        cost_estimate=cost(0, 4 * MIB),
        name="pick",
    )(table, in_hbm(features))


def agg_kernel(which, chunk, nfeat, src, counts, me, arrived_hbm, tiles_hbm, features, *refs):
    outs, (arrived, tiles, own, sems) = refs[: len(which)], refs[len(which) :]
    group, per = tiles.shape[1:3]
    moves = [pltpu.make_async_copy(arrived_hbm, arrived, sems.at[0])]
    firsts = [lax.rem(me[0] + k, nfeat) * group for k in which]
    for i, first in enumerate(firsts):
        rows = pl.ds(pl.multiple_of(first * BLK, BLK), group * BLK)
        moves.append(
            pltpu.make_async_copy(tiles_hbm.at[pl.ds(first, group)], tiles.at[i], sems.at[1 + 2 * i])
        )
        moves.append(
            pltpu.make_async_copy(
                features.at[rows, pl.ds(chunk * BLK, BLK)], own.at[i], sems.at[2 + 2 * i]
            )
        )
    for move in moves:
        move.start()
    moves[0].wait()
    for i, (first, out) in enumerate(zip(firsts, outs)):
        moves[1 + 2 * i].wait()
        moves[2 + 2 * i].wait()
        for b in range(group):
            rows, weights = [], []
            for t in range(per):
                slot = src[(first + b) * per + t]
                live = lax.rem(slot, 2) < counts[lax.div(slot, 2)]
                rows.append(arrived[slot])
                weights.append(tiles[i, b, t] * jnp.where(live, 1.0, 0.0).astype(BF16))
            total = dot(jnp.concatenate(weights, 1), jnp.concatenate(rows, 0), NN)
            at = pl.ds(b * BLK, BLK)
            out[at, :] = (own[i, at, :].astype(F32) + total).astype(BF16)


def aggregate(src, counts, me, arrived, tiles, features, chunk, nfeat, which):
    nblocks, per = tiles.shape[:2]
    group = nblocks // nfeat
    piece = jax.ShapeDtypeStruct((group * BLK, BLK), BF16)
    hbm = pl.BlockSpec(memory_space=pltpu.HBM)
    return pl.pallas_call(
        functools.partial(agg_kernel, which, chunk, nfeat),
        grid_spec=pltpu.PrefetchScalarGridSpec(
            num_scalar_prefetch=3,
            grid=(),
            in_specs=[hbm] * 3,
            out_specs=[pl.BlockSpec(memory_space=pltpu.VMEM)] * len(which),
            scratch_shapes=[
                pltpu.VMEM(arrived.shape, BF16),
                pltpu.VMEM((len(which), group, per, BLK, BLK), BF16),
                pltpu.VMEM((len(which), group * BLK, BLK), BF16),
                pltpu.SemaphoreType.DMA((1 + 2 * len(which),)),
            ],
        ),
        out_shape=[piece] * len(which),
        compiler_params=params(14),
        cost_estimate=cost(len(which) * group * per * 2 * BLK**3, 8 * MIB),
        name="aggregate",
    )(src, counts, me, in_hbm(arrived), in_hbm(tiles), in_hbm(features))


def dense_kernel(nfeat, *refs):
    pieces, (weights, bias, second, hidden, proj) = refs[: 2 * nfeat], refs[2 * nfeat :]
    order = [pieces[i * nfeat + k][...] for k in range(nfeat) for i in range(2)]
    pre = dot(weights[...], jnp.concatenate(order, 1), NT)
    hid = jnp.maximum(pre + bias[...], 0.0).astype(BF16)
    hidden[...] = hid
    out = dot(second[...], hid, NN)
    for b in range(proj.shape[0]):
        proj[b] = out[:, b * BLK : (b + 1) * BLK]


def dense(pieces, weights, bias, second):
    nodes, nfeat = pieces[0].shape[0], len(pieces) // 2
    hid, width = weights.shape
    grades = second.shape[0]
    step = 256
    return pl.pallas_call(
        functools.partial(dense_kernel, nfeat),
        grid=(nodes // step,),
        in_specs=[pl.BlockSpec((step, BLK), lambda g: (g, 0))] * (2 * nfeat)
        + [
            pl.BlockSpec((hid, width), lambda g: (0, 0)),
            pl.BlockSpec((hid, 1), lambda g: (0, 0)),
            pl.BlockSpec((grades, hid), lambda g: (0, 0)),
        ],
        out_specs=[
            pl.BlockSpec((hid, step), lambda g: (0, g)),
            pl.BlockSpec((step // BLK, grades, BLK), lambda g: (g, 0, 0)),
        ],
        out_shape=[
            jax.ShapeDtypeStruct((hid, nodes), BF16),
            jax.ShapeDtypeStruct((nodes // BLK, grades, BLK), F32),
        ],
        compiler_params=params(20),
        cost_estimate=cost(2 * nodes * hid * width, 7 * MIB),
        name="dense",
    )(*pieces, weights, bias, second)


def spread_kernel(table, me, p0, p1, p2, p3, whole, out):
    nfeat, group = 4, p0.shape[0]
    for k, piece in enumerate((p0, p1, p2, p3)):
        owner = lax.rem(me[0] + nfeat - k, nfeat)
        whole[pl.ds(owner * group, group)] = piece[...]

    @pl.loop(0, out.shape[0], unroll=8)
    def _(k):
        out[k] = whole[table[k]]


def spread(table, me, pieces):
    group, grades, _ = pieces[0].shape
    slots = table.shape[0]
    vmem = pl.BlockSpec(memory_space=pltpu.VMEM)
    return pl.pallas_call(
        spread_kernel,
        grid_spec=pltpu.PrefetchScalarGridSpec(
            num_scalar_prefetch=2,
            grid=(),
            in_specs=[vmem] * 4,
            out_specs=[vmem] * 2,
        ),
        out_shape=[
            jax.ShapeDtypeStruct((group * 4, grades, BLK), F32),
            jax.ShapeDtypeStruct((slots, grades, BLK), F32),
        ],
        compiler_params=params(4),
        cost_estimate=cost(0, MIB),
        name="spread",
    )(table, me, *pieces)


def logits_kernel(
    scale, src, counts, me, arrived, own, labels, tiles, dlog_out, slots_out, parts, field, grad_b, sums
):
    nblocks, per = tiles.shape[:2]
    nslots, grades, _ = arrived.shape
    mine = dlog_out.shape[0]

    def live_of(slot):
        return jnp.where(lax.rem(slot, 2) < counts[lax.div(slot, 2)], 1.0, 0.0)

    x = arrived[...]
    for i in range(3):
        y = x.astype(BF16)
        parts[:, i * grades : (i + 1) * grades, :] = y
        x = x - y.astype(F32)

    @pl.loop(0, nblocks, unroll=8)
    def _(b):
        rows, weights = [], []
        for t in range(per):
            slot = src[b * per + t]
            rows.append(parts[slot] * live_of(slot).astype(BF16))
            weights.append(tiles[b, t])
        triple = dot(jnp.concatenate(rows, 1), jnp.concatenate(weights, 1), NT)
        field[b] = own[b] + (
            triple[:grades] + (triple[grades : 2 * grades] + triple[2 * grades :])
        )

    expo = jnp.exp(field[...])
    probs = expo / jnp.sum(expo, axis=1, keepdims=True)
    grade = lax.broadcasted_iota(jnp.int32, field.shape, 1)
    onehot = jnp.where(labels[...] == grade, 1.0, 0.0)
    dlog = (probs - onehot) * scale
    field[...] = dlog
    grad_b[...] = dlog.astype(BF16)
    dlog_out[...] = field[pl.ds(me[0] * mine, mine)]
    sums[...] = jnp.zeros_like(sums)

    @pl.loop(0, nblocks, unroll=8)
    def _(b):
        back = dot(grad_b[b], jnp.concatenate([tiles[b, t] for t in range(per)], 1), NN)
        for t in range(per):
            slot = src[b * per + t]
            sums[slot] += back[:, t * BLK : (t + 1) * BLK] * live_of(slot)

    slots_out[...] = sums[...].astype(BF16)


def logits_back(src, counts, me, arrived, own, labels, tiles, scale, nfeat):
    nblocks, per = tiles.shape[:2]
    nslots, grades, _ = arrived.shape
    vmem = pl.BlockSpec(memory_space=pltpu.VMEM)
    return pl.pallas_call(
        functools.partial(logits_kernel, scale),
        grid_spec=pltpu.PrefetchScalarGridSpec(
            num_scalar_prefetch=3,
            grid=(),
            in_specs=[vmem] * 4,
            out_specs=[vmem] * 2,
            scratch_shapes=[
                pltpu.VMEM((nslots, 3 * grades, BLK), BF16),
                pltpu.VMEM((nblocks, grades, BLK), F32),
                pltpu.VMEM((nblocks, grades, BLK), BF16),
                pltpu.VMEM(arrived.shape, F32),
            ],
        ),
        out_shape=[
            jax.ShapeDtypeStruct((nblocks // nfeat, grades, BLK), F32),
            jax.ShapeDtypeStruct(arrived.shape, BF16),
        ],
        compiler_params=params(8),
        cost_estimate=cost(nblocks * per * 2 * 64 * BLK**2, 6 * MIB),
        name="logits",
    )(src, counts, me, arrived, own, labels, tiles)


def small_kernel(table, me, returned, dlog, hidden, second, dpre_out, *refs):
    small, (total, dproj, buf) = refs[:-3], refs[-3:]
    group, grades, _ = dlog.shape
    g = pl.program_id(0)
    width = hidden.shape[0]

    @pl.when(g == 0)
    def _():
        total[pl.ds(0, group)] = dlog[...]

        @pl.loop(0, returned.shape[0], unroll=8)
        def _(k):
            at = table[k] - me[0] * group
            at = jnp.where((at >= 0) & (at < group), at, group)
            total[at] += returned[k].astype(F32)

        for b in range(group):
            dproj[:, b * BLK : (b + 1) * BLK] = total[b].astype(BF16)

    active = hidden[...]
    dproj_b = dproj[...]
    dpre = jnp.where(active > 0, dot(second[...], dproj_b, NN), 0.0)
    dpre_out[...] = dpre.astype(BF16)
    buf[pl.ds(0, grades), :] = dot(dproj_b, active, NT)
    part = dpre[:, :BLK]
    for i in range(1, dpre.shape[1] // BLK):
        part += dpre[:, i * BLK : (i + 1) * BLK]
    buf[pl.ds(grades, 8), :] = jnp.broadcast_to(
        jnp.sum(part.T, axis=0, keepdims=True), (8, width)
    )
    for k, out in enumerate(small):

        @pl.when(g == k)
        def _():
            out[...] = buf[...]


def small_gradients(table, me, returned, dlog, hidden, second, nfeat):
    hid, nodes = hidden.shape
    group, grades, _ = dlog.shape
    width = hid // nfeat
    turn = lambda g, m: lax.rem(m[0] + nfeat - g, nfeat)
    whole3 = lambda g, t, m: (0, 0, 0)
    small = jax.ShapeDtypeStruct((grades + 8, width), F32)
    return pl.pallas_call(
        small_kernel,
        grid_spec=pltpu.PrefetchScalarGridSpec(
            num_scalar_prefetch=2,
            grid=(nfeat,),
            in_specs=[
                pl.BlockSpec(returned.shape, whole3),
                pl.BlockSpec(dlog.shape, whole3),
                pl.BlockSpec((width, nodes), lambda g, t, m: (turn(g, m), 0)),
                pl.BlockSpec((width, grades), lambda g, t, m: (turn(g, m), 0)),
            ],
            out_specs=[pl.BlockSpec((width, nodes), lambda g, t, m: (turn(g, m), 0))]
            + [pl.BlockSpec(small.shape, lambda g, t, m: (0, 0))] * nfeat,
            scratch_shapes=[
                pltpu.VMEM((group + 1, grades, BLK), F32),
                pltpu.VMEM((grades, nodes), BF16),
                pltpu.VMEM(small.shape, F32),
            ],
        ),
        out_shape=[pltpu.HBM((hid, nodes), BF16)] + [small] * nfeat,
        compiler_params=params(16),
        cost_estimate=cost(2 * nodes * hid * 256, 4 * MIB),
        name="small_gradients",
    )(table, me, returned, dlog, hidden, second)


def big_kernel(me, dpre, *refs):
    pieces, out = refs[:-1], refs[-1]
    nfeat = len(pieces) // 2
    for k in range(nfeat):
        owner = lax.rem(me[0] + nfeat - k, nfeat)
        both = jnp.concatenate([pieces[k][...], pieces[nfeat + k][...]], 1)
        grad = dot(dpre[...], both, NN).astype(BF16)
        out[:, owner] = grad.reshape(out.shape[0], out.shape[2], out.shape[3])


def big_gradient(me, dpre, pieces, parts):
    nfeat = len(pieces) // 2
    hid, nodes = dpre.shape
    steps = 2
    return pl.pallas_call(
        big_kernel,
        grid_spec=pltpu.PrefetchScalarGridSpec(
            num_scalar_prefetch=1,
            grid=(steps,),
            in_specs=[pl.BlockSpec((hid // steps, nodes), lambda g, m: (g, 0))]
            + [pl.BlockSpec((nodes, BLK), lambda g, m: (0, 0))] * (2 * nfeat),
            out_specs=pl.BlockSpec(
                (parts // steps, nfeat, hid // parts, 2 * BLK), lambda g, m: (g, 0, 0, 0)
            ),
        ),
        out_shape=pltpu.HBM((parts, nfeat, hid // parts, 2 * BLK), BF16),
        compiler_params=params(24),
        cost_estimate=cost(2 * nodes * hid * hid, 6 * MIB),
        name="big_gradient",
    )(me, in_hbm(dpre), *pieces)


def total_kernel(arrived, out, acc):
    g = pl.program_id(0)

    @pl.when(g == 0)
    def _():
        acc[...] = jnp.zeros_like(acc)

    total = arrived[0].astype(F32)
    for i in range(1, arrived.shape[0]):
        total += arrived[i].astype(F32)
    acc[...] += total

    @pl.when(g == pl.num_programs(0) - 1)
    def _():
        out[...] = acc[...]


def total(arrived):
    n, cols, rows = arrived.shape
    step = n // 8
    return pl.pallas_call(
        total_kernel,
        grid=(n // step,),
        in_specs=[pl.BlockSpec((step, cols, rows), lambda g: (g, 0, 0))],
        out_specs=pl.BlockSpec((cols, rows), lambda g: (0, 0)),
        out_shape=jax.ShapeDtypeStruct((cols, rows), F32),
        scratch_shapes=[pltpu.VMEM((cols, rows), F32)],
        compiler_params=params(8),
        cost_estimate=cost(0, 2 * MIB),
        name="total",
    )(arrived)


def shards(features, pair_count, send_blocks, tile_src, tiles, labels, w_first, b_first, w_second):
    nblocks = tile_src.shape[0]
    parts = lax.axis_size("nodes")
    nfeat = lax.axis_size("feat")
    slots = send_blocks.shape[2]
    grades = w_second.shape[1]
    hid = w_first.shape[1]
    axis = lax.axis_index("feat").astype(jnp.int32)
    me = axis.reshape(1)
    table = send_blocks.reshape(parts * slots)
    src = tile_src.reshape(-1)
    counts = pair_count.reshape(-1)

    def ahead(x, k):
        return lax.ppermute(x, "feat", [(i, (i + k) % nfeat) for i in range(nfeat)])

    def swap(x):
        shaped = x.reshape(parts, slots, *x.shape[1:])
        moved = lax.all_to_all(shaped, "nodes", split_axis=0, concat_axis=0, tiled=True)
        return moved.reshape(x.shape)

    arrived = [swap(pick(features, table, 0))]
    send = pick(features, table, 1)

    flat = w_first.T
    weights = jnp.concatenate([flat] + [ahead(flat, k) for k in range(1, nfeat)], 1)
    consts = jnp.concatenate(
        [w_second.T.astype(F32), jnp.broadcast_to(b_first[None], (8, b_first.shape[0]))], 0
    )
    turned = [consts] + [ahead(consts, k) for k in range(1, nfeat)]
    ring = jnp.stack([turned[k] for k in (3, 2, 1, 0, 3, 2, 1)])
    ordered = lax.dynamic_slice_in_dim(ring, nfeat - 1 - axis, nfeat, 0)
    second_t = ordered[:, :grades].transpose(1, 0, 2).reshape(grades, hid).astype(BF16)
    bias = ordered[:, grades].reshape(hid, 1)
    second = second_t.T

    send, weights, bias, second_t, second = lax.optimization_barrier(
        (send, weights, bias, second_t, second)
    )
    arrived.append(swap(send))
    others = (2, 1, 3)
    make = functools.partial(aggregate, src, counts, me)
    first = [None] * nfeat
    *sent, first[0] = make(arrived[0], tiles, features, 0, nfeat, others + (0,))
    for k, piece in zip(others, sent):
        first[k] = ahead(piece, k)
    last = [None] * nfeat
    for k, piece in zip(others, make(arrived[1], tiles, features, 1, nfeat, others)):
        last[k] = ahead(piece, k)
    (last[0],) = make(arrived[1], tiles, features, 1, nfeat, (0,))
    hidden, proj = dense(first + last, weights, bias, second_t)

    projs = [proj] + [ahead(proj, k) for k in range(1, nfeat)]
    own, send = spread(table, me, projs)
    scale = 1.0 / math.sqrt(nblocks * BLK * parts)
    dlog, slotsum = logits_back(
        src, counts, me, swap(send), own, labels.reshape(nblocks, 1, BLK), tiles, scale, nfeat
    )
    dpre, *small = small_gradients(table, me, swap(slotsum), dlog, hidden, second, nfeat)
    rest = small[0]
    for k in range(1, nfeat):
        rest = rest + ahead(small[k], nfeat - k)
    big = big_gradient(me, dpre, first + last, parts)
    moved = lax.all_to_all(
        big.reshape(parts * nfeat, *big.shape[2:]),
        ("nodes", "feat"),
        split_axis=0,
        concat_axis=0,
        tiled=True,
    )
    for group in ((1, 2, 3, 4, 5, 6, 7), (8, 16, 24)):
        terms = [rest] + [
            lax.ppermute(rest, "nodes", [(i, i ^ d) for i in range(parts)]) for d in group
        ]
        while len(terms) > 1:
            terms = [a + b for a, b in zip(terms[::2], terms[1::2])]
        (rest,) = terms
    return total(moved).T, rest[grades], rest[:grades].T


def solution(mesh):
    placed = (
        P("nodes", "feat"),
        P("nodes", None),
        P("nodes", None, None),
        P("nodes", None),
        P("nodes", None, None, None),
        P("nodes"),
        P("feat", None),
        P("feat"),
        P("feat", None),
    )
    return jax.shard_map(
        shards,
        mesh=mesh,
        in_specs=placed,
        out_specs=(P("feat", "nodes"), P("feat"), P("feat", None)),
        check_vma=False,
    )
```

```python
import functools
import math

import jax
import jax.numpy as jnp
from jax import lax
from jax.experimental import pallas as pl
from jax.experimental.pallas import tpu as pltpu
from jax.sharding import PartitionSpec as P

F32 = jnp.float32
BF16 = jnp.bfloat16
NT = (((1,), (1,)), ((), ()))
NN = (((1,), (0,)), ((), ()))
BLK = 128
MIB = 1 << 20


def params(mib):
    return pltpu.CompilerParams(vmem_limit_bytes=mib * MIB)


def cost(flops, nbytes):
    return pl.CostEstimate(flops=flops, bytes_accessed=nbytes, transcendentals=0)


def dot(a, b, dims):
    return lax.dot_general(a, b, dims, preferred_element_type=F32)


def in_hbm(x):
    return pltpu.with_memory_space_constraint(x, pltpu.HBM)


def pick_kernel(chunk, table, features, out, held, sems):
    slots = out.shape[0]
    load = pltpu.make_async_copy(features.at[:, pl.ds(chunk * BLK, BLK)], held, sems.at[0])
    load.start()
    load.wait()

    @pl.loop(0, slots, unroll=8)
    def _(k):
        rows = pl.ds(pl.multiple_of(table[k] * BLK, BLK), BLK)
        pltpu.make_async_copy(held.at[rows], out.at[k], sems.at[1]).start()

    pltpu.make_async_copy(out, out, sems.at[1]).wait()


def pick(features, table, chunk):
    slots = table.shape[0]
    return pl.pallas_call(
        functools.partial(pick_kernel, chunk),
        grid_spec=pltpu.PrefetchScalarGridSpec(
            num_scalar_prefetch=1,
            grid=(),
            in_specs=[pl.BlockSpec(memory_space=pltpu.HBM)],
            out_specs=pl.BlockSpec(memory_space=pltpu.HBM),
            scratch_shapes=[
                pltpu.VMEM((features.shape[0], BLK), BF16),
                pltpu.SemaphoreType.DMA((2,)),
            ],
        ),
        out_shape=pltpu.HBM((slots, BLK, BLK), BF16),
        compiler_params=params(4),
        cost_estimate=cost(0, 4 * MIB),
        name="pick",
    )(table, in_hbm(features))


def agg_kernel(which, chunk, nfeat, src, counts, me, arrived_hbm, tiles_hbm, features, *refs):
    outs, (arrived, tiles, own, sems) = refs[: len(which)], refs[len(which) :]
    group, per = tiles.shape[1:3]
    moves = [pltpu.make_async_copy(arrived_hbm, arrived, sems.at[0])]
    firsts = [lax.rem(me[0] + k, nfeat) * group for k in which]
    for i, first in enumerate(firsts):
        rows = pl.ds(pl.multiple_of(first * BLK, BLK), group * BLK)
        moves.append(
            pltpu.make_async_copy(tiles_hbm.at[pl.ds(first, group)], tiles.at[i], sems.at[1 + 2 * i])
        )
        moves.append(
            pltpu.make_async_copy(
                features.at[rows, pl.ds(chunk * BLK, BLK)], own.at[i], sems.at[2 + 2 * i]
            )
        )
    for move in moves:
        move.start()
    moves[0].wait()
    for i, (first, out) in enumerate(zip(firsts, outs)):
        moves[1 + 2 * i].wait()
        moves[2 + 2 * i].wait()
        for b in range(group):
            rows, weights = [], []
            for t in range(per):
                slot = src[(first + b) * per + t]
                live = lax.rem(slot, 2) < counts[lax.div(slot, 2)]
                rows.append(arrived[slot])
                weights.append(tiles[i, b, t] * jnp.where(live, 1.0, 0.0).astype(BF16))
            total = dot(jnp.concatenate(weights, 1), jnp.concatenate(rows, 0), NN)
            at = pl.ds(b * BLK, BLK)
            out[at, :] = (own[i, at, :].astype(F32) + total).astype(BF16)


def aggregate(src, counts, me, arrived, tiles, features, chunk, nfeat, which):
    nblocks, per = tiles.shape[:2]
    group = nblocks // nfeat
    piece = jax.ShapeDtypeStruct((group * BLK, BLK), BF16)
    hbm = pl.BlockSpec(memory_space=pltpu.HBM)
    return pl.pallas_call(
        functools.partial(agg_kernel, which, chunk, nfeat),
        grid_spec=pltpu.PrefetchScalarGridSpec(
            num_scalar_prefetch=3,
            grid=(),
            in_specs=[hbm] * 3,
            out_specs=[pl.BlockSpec(memory_space=pltpu.VMEM)] * len(which),
            scratch_shapes=[
                pltpu.VMEM(arrived.shape, BF16),
                pltpu.VMEM((len(which), group, per, BLK, BLK), BF16),
                pltpu.VMEM((len(which), group * BLK, BLK), BF16),
                pltpu.SemaphoreType.DMA((1 + 2 * len(which),)),
            ],
        ),
        out_shape=[piece] * len(which),
        compiler_params=params(14),
        cost_estimate=cost(len(which) * group * per * 2 * BLK**3, 8 * MIB),
        name="aggregate",
    )(src, counts, me, in_hbm(arrived), in_hbm(tiles), in_hbm(features))


def dense_kernel(nfeat, *refs):
    pieces, (weights, bias, second, hidden, proj) = refs[: 2 * nfeat], refs[2 * nfeat :]
    order = [pieces[i * nfeat + k][...] for k in range(nfeat) for i in range(2)]
    pre = dot(weights[...], jnp.concatenate(order, 1), NT)
    hid = jnp.maximum(pre + bias[...], 0.0).astype(BF16)
    hidden[...] = hid
    out = dot(second[...], hid, NN)
    for b in range(proj.shape[0]):
        proj[b] = out[:, b * BLK : (b + 1) * BLK]


def dense(pieces, weights, bias, second):
    nodes, nfeat = pieces[0].shape[0], len(pieces) // 2
    hid, width = weights.shape
    grades = second.shape[0]
    step = 256
    return pl.pallas_call(
        functools.partial(dense_kernel, nfeat),
        grid=(nodes // step,),
        in_specs=[pl.BlockSpec((step, BLK), lambda g: (g, 0))] * (2 * nfeat)
        + [
            pl.BlockSpec((hid, width), lambda g: (0, 0)),
            pl.BlockSpec((hid, 1), lambda g: (0, 0)),
            pl.BlockSpec((grades, hid), lambda g: (0, 0)),
        ],
        out_specs=[
            pl.BlockSpec((hid, step), lambda g: (0, g)),
            pl.BlockSpec((step // BLK, grades, BLK), lambda g: (g, 0, 0)),
        ],
        out_shape=[
            jax.ShapeDtypeStruct((hid, nodes), BF16),
            jax.ShapeDtypeStruct((nodes // BLK, grades, BLK), F32),
        ],
        compiler_params=params(20),
        cost_estimate=cost(2 * nodes * hid * width, 7 * MIB),
        name="dense",
    )(*pieces, weights, bias, second)


def spread_kernel(table, me, p0, p1, p2, p3, whole, out):
    nfeat, group = 4, p0.shape[0]
    for k, piece in enumerate((p0, p1, p2, p3)):
        owner = lax.rem(me[0] + nfeat - k, nfeat)
        whole[pl.ds(owner * group, group)] = piece[...]

    @pl.loop(0, out.shape[0], unroll=8)
    def _(k):
        out[k] = whole[table[k]]


def spread(table, me, pieces):
    group, grades, _ = pieces[0].shape
    slots = table.shape[0]
    vmem = pl.BlockSpec(memory_space=pltpu.VMEM)
    return pl.pallas_call(
        spread_kernel,
        grid_spec=pltpu.PrefetchScalarGridSpec(
            num_scalar_prefetch=2,
            grid=(),
            in_specs=[vmem] * 4,
            out_specs=[vmem] * 2,
        ),
        out_shape=[
            jax.ShapeDtypeStruct((group * 4, grades, BLK), F32),
            jax.ShapeDtypeStruct((slots, grades, BLK), F32),
        ],
        compiler_params=params(4),
        cost_estimate=cost(0, MIB),
        name="spread",
    )(table, me, *pieces)


def logits_kernel(
    scale, src, counts, me, arrived, own, labels, tiles, dlog_out, slots_out, parts, field, grad_b, sums
):
    nblocks, per = tiles.shape[:2]
    nslots, grades, _ = arrived.shape
    mine = dlog_out.shape[0]

    def live_of(slot):
        return jnp.where(lax.rem(slot, 2) < counts[lax.div(slot, 2)], 1.0, 0.0)

    x = arrived[...]
    for i in range(3):
        y = x.astype(BF16)
        parts[:, i * grades : (i + 1) * grades, :] = y
        x = x - y.astype(F32)

    @pl.loop(0, nblocks, unroll=8)
    def _(b):
        rows, weights = [], []
        for t in range(per):
            slot = src[b * per + t]
            rows.append(parts[slot] * live_of(slot).astype(BF16))
            weights.append(tiles[b, t])
        triple = dot(jnp.concatenate(rows, 1), jnp.concatenate(weights, 1), NT)
        field[b] = own[b] + (
            triple[:grades] + (triple[grades : 2 * grades] + triple[2 * grades :])
        )

    expo = jnp.exp(field[...])
    probs = expo / jnp.sum(expo, axis=1, keepdims=True)
    grade = lax.broadcasted_iota(jnp.int32, field.shape, 1)
    onehot = jnp.where(labels[...] == grade, 1.0, 0.0)
    dlog = (probs - onehot) * scale
    field[...] = dlog
    grad_b[...] = dlog.astype(BF16)
    dlog_out[...] = field[pl.ds(me[0] * mine, mine)]
    sums[...] = jnp.zeros_like(sums)

    @pl.loop(0, nblocks, unroll=8)
    def _(b):
        back = dot(grad_b[b], jnp.concatenate([tiles[b, t] for t in range(per)], 1), NN)
        for t in range(per):
            slot = src[b * per + t]
            sums[slot] += back[:, t * BLK : (t + 1) * BLK] * live_of(slot)

    slots_out[...] = sums[...].astype(BF16)


def logits_back(src, counts, me, arrived, own, labels, tiles, scale, nfeat):
    nblocks, per = tiles.shape[:2]
    nslots, grades, _ = arrived.shape
    vmem = pl.BlockSpec(memory_space=pltpu.VMEM)
    return pl.pallas_call(
        functools.partial(logits_kernel, scale),
        grid_spec=pltpu.PrefetchScalarGridSpec(
            num_scalar_prefetch=3,
            grid=(),
            in_specs=[vmem] * 4,
            out_specs=[vmem] * 2,
            scratch_shapes=[
                pltpu.VMEM((nslots, 3 * grades, BLK), BF16),
                pltpu.VMEM((nblocks, grades, BLK), F32),
                pltpu.VMEM((nblocks, grades, BLK), BF16),
                pltpu.VMEM(arrived.shape, F32),
            ],
        ),
        out_shape=[
            jax.ShapeDtypeStruct((nblocks // nfeat, grades, BLK), F32),
            jax.ShapeDtypeStruct(arrived.shape, BF16),
        ],
        compiler_params=params(8),
        cost_estimate=cost(nblocks * per * 2 * 64 * BLK**2, 6 * MIB),
        name="logits",
    )(src, counts, me, arrived, own, labels, tiles)


def small_kernel(table, me, returned, dlog, hidden, second, dpre_out, *refs):
    small, (total, dproj, buf) = refs[:-3], refs[-3:]
    group, grades, _ = dlog.shape
    g = pl.program_id(0)
    width = hidden.shape[0]

    @pl.when(g == 0)
    def _():
        total[pl.ds(0, group)] = dlog[...]

        @pl.loop(0, returned.shape[0], unroll=8)
        def _(k):
            at = table[k] - me[0] * group
            at = jnp.where((at >= 0) & (at < group), at, group)
            total[at] += returned[k].astype(F32)

        for b in range(group):
            dproj[:, b * BLK : (b + 1) * BLK] = total[b].astype(BF16)

    active = hidden[...]
    dproj_b = dproj[...]
    dpre = jnp.where(active > 0, dot(second[...], dproj_b, NN), 0.0)
    dpre_out[...] = dpre.astype(BF16)
    buf[pl.ds(0, grades), :] = dot(dproj_b, active, NT)
    part = dpre[:, :BLK]
    for i in range(1, dpre.shape[1] // BLK):
        part += dpre[:, i * BLK : (i + 1) * BLK]
    buf[pl.ds(grades, 8), :] = jnp.broadcast_to(
        jnp.sum(part.T, axis=0, keepdims=True), (8, width)
    )
    for k, out in enumerate(small):

        @pl.when(g == k)
        def _():
            out[...] = buf[...]


def small_gradients(table, me, returned, dlog, hidden, second, nfeat):
    hid, nodes = hidden.shape
    group, grades, _ = dlog.shape
    width = hid // nfeat
    turn = lambda g, m: lax.rem(m[0] + nfeat - g, nfeat)
    whole3 = lambda g, t, m: (0, 0, 0)
    small = jax.ShapeDtypeStruct((grades + 8, width), F32)
    return pl.pallas_call(
        small_kernel,
        grid_spec=pltpu.PrefetchScalarGridSpec(
            num_scalar_prefetch=2,
            grid=(nfeat,),
            in_specs=[
                pl.BlockSpec(returned.shape, whole3),
                pl.BlockSpec(dlog.shape, whole3),
                pl.BlockSpec((width, nodes), lambda g, t, m: (turn(g, m), 0)),
                pl.BlockSpec((width, grades), lambda g, t, m: (turn(g, m), 0)),
            ],
            out_specs=[pl.BlockSpec((width, nodes), lambda g, t, m: (turn(g, m), 0))]
            + [pl.BlockSpec(small.shape, lambda g, t, m: (0, 0))] * nfeat,
            scratch_shapes=[
                pltpu.VMEM((group + 1, grades, BLK), F32),
                pltpu.VMEM((grades, nodes), BF16),
                pltpu.VMEM(small.shape, F32),
            ],
        ),
        out_shape=[pltpu.HBM((hid, nodes), BF16)] + [small] * nfeat,
        compiler_params=params(16),
        cost_estimate=cost(2 * nodes * hid * 256, 4 * MIB),
        name="small_gradients",
    )(table, me, returned, dlog, hidden, second)


def big_kernel(me, dpre, *refs):
    pieces, out = refs[:-1], refs[-1]
    nfeat = len(pieces) // 2
    for k in range(nfeat):
        owner = lax.rem(me[0] + nfeat - k, nfeat)
        both = jnp.concatenate([pieces[k][...], pieces[nfeat + k][...]], 1)
        grad = dot(dpre[...], both, NN).astype(BF16)
        out[:, owner] = grad.reshape(out.shape[0], out.shape[2], out.shape[3])


def big_gradient(me, dpre, pieces, parts):
    nfeat = len(pieces) // 2
    hid, nodes = dpre.shape
    steps = 2
    return pl.pallas_call(
        big_kernel,
        grid_spec=pltpu.PrefetchScalarGridSpec(
            num_scalar_prefetch=1,
            grid=(steps,),
            in_specs=[pl.BlockSpec((hid // steps, nodes), lambda g, m: (g, 0))]
            + [pl.BlockSpec((nodes, BLK), lambda g, m: (0, 0))] * (2 * nfeat),
            out_specs=pl.BlockSpec(
                (parts // steps, nfeat, hid // parts, 2 * BLK), lambda g, m: (g, 0, 0, 0)
            ),
        ),
        out_shape=pltpu.HBM((parts, nfeat, hid // parts, 2 * BLK), BF16),
        compiler_params=params(24),
        cost_estimate=cost(2 * nodes * hid * hid, 6 * MIB),
        name="big_gradient",
    )(me, in_hbm(dpre), *pieces)


def total_kernel(nsmall, arrived, *refs):
    small, (out, second, bias, acc) = refs[:nsmall], refs[nsmall:]
    g = pl.program_id(0)

    @pl.when(g == 0)
    def _():
        acc[...] = jnp.zeros_like(acc)
        terms = [ref[...] for ref in small]
        while len(terms) > 1:
            terms = [a + b for a, b in zip(terms[::2], terms[1::2])]
        grades = second.shape[0]
        second[...] = terms[0][:grades]
        bias[...] = terms[0][grades : grades + 1]

    total = arrived[0].astype(F32)
    for i in range(1, arrived.shape[0]):
        total += arrived[i].astype(F32)
    acc[...] += total

    @pl.when(g == pl.num_programs(0) - 1)
    def _():
        out[...] = acc[...]


def total(arrived, small, grades):
    n, cols, rows = arrived.shape
    step = n // 8
    whole = lambda g: (0, 0)
    return pl.pallas_call(
        functools.partial(total_kernel, len(small)),
        grid=(n // step,),
        in_specs=[pl.BlockSpec((step, cols, rows), lambda g: (g, 0, 0))]
        + [pl.BlockSpec(small[0].shape, whole)] * len(small),
        out_specs=[
            pl.BlockSpec((cols, rows), whole),
            pl.BlockSpec((grades, rows), whole),
            pl.BlockSpec((1, rows), whole),
        ],
        out_shape=[
            jax.ShapeDtypeStruct((cols, rows), F32),
            jax.ShapeDtypeStruct((grades, rows), F32),
            jax.ShapeDtypeStruct((1, rows), F32),
        ],
        scratch_shapes=[pltpu.VMEM((cols, rows), F32)],
        compiler_params=params(8),
        cost_estimate=cost(0, 2 * MIB),
        name="total",
    )(arrived, *small)


def shards(features, pair_count, send_blocks, tile_src, tiles, labels, w_first, b_first, w_second):
    nblocks = tile_src.shape[0]
    parts = lax.axis_size("nodes")
    nfeat = lax.axis_size("feat")
    slots = send_blocks.shape[2]
    grades = w_second.shape[1]
    hid = w_first.shape[1]
    axis = lax.axis_index("feat").astype(jnp.int32)
    me = axis.reshape(1)
    table = send_blocks.reshape(parts * slots)
    src = tile_src.reshape(-1)
    counts = pair_count.reshape(-1)

    def ahead(x, k):
        return lax.ppermute(x, "feat", [(i, (i + k) % nfeat) for i in range(nfeat)])

    def swap(x):
        shaped = x.reshape(parts, slots, *x.shape[1:])
        moved = lax.all_to_all(shaped, "nodes", split_axis=0, concat_axis=0, tiled=True)
        return moved.reshape(x.shape)

    arrived = [swap(pick(features, table, 0))]
    send = pick(features, table, 1)

    flat = w_first.T
    weights = jnp.concatenate([flat] + [ahead(flat, k) for k in range(1, nfeat)], 1)
    consts = jnp.concatenate(
        [w_second.T.astype(F32), jnp.broadcast_to(b_first[None], (8, b_first.shape[0]))], 0
    )
    turned = [consts] + [ahead(consts, k) for k in range(1, nfeat)]
    ring = jnp.stack([turned[k] for k in (3, 2, 1, 0, 3, 2, 1)])
    ordered = lax.dynamic_slice_in_dim(ring, nfeat - 1 - axis, nfeat, 0)
    second_t = ordered[:, :grades].transpose(1, 0, 2).reshape(grades, hid).astype(BF16)
    bias = ordered[:, grades].reshape(hid, 1)
    second = second_t.T

    send, weights, bias, second_t, second = lax.optimization_barrier(
        (send, weights, bias, second_t, second)
    )
    arrived.append(swap(send))
    others = (2, 1, 3)
    make = functools.partial(aggregate, src, counts, me)
    first = [None] * nfeat
    *sent, first[0] = make(arrived[0], tiles, features, 0, nfeat, others + (0,))
    for k, piece in zip(others, sent):
        first[k] = ahead(piece, k)
    last = [None] * nfeat
    for k, piece in zip(others, make(arrived[1], tiles, features, 1, nfeat, others)):
        last[k] = ahead(piece, k)
    (last[0],) = make(arrived[1], tiles, features, 1, nfeat, (0,))
    hidden, proj = dense(first + last, weights, bias, second_t)

    projs = [proj] + [ahead(proj, k) for k in range(1, nfeat)]
    own, send = spread(table, me, projs)
    scale = 1.0 / math.sqrt(nblocks * BLK * parts)
    dlog, slotsum = logits_back(
        src, counts, me, swap(send), own, labels.reshape(nblocks, 1, BLK), tiles, scale, nfeat
    )
    dpre, *small = small_gradients(table, me, swap(slotsum), dlog, hidden, second, nfeat)
    rest = small[0]
    for k in range(1, nfeat):
        rest = rest + ahead(small[k], nfeat - k)
    big = big_gradient(me, dpre, first + last, parts)
    big, rest = lax.optimization_barrier((big, rest))
    moved = lax.all_to_all(
        big.reshape(parts * nfeat, *big.shape[2:]),
        ("nodes", "feat"),
        split_axis=0,
        concat_axis=0,
        tiled=True,
    )
    terms = [rest]
    for group in ((1, 2, 3, 4, 5, 6, 7), (8, 16, 24)):
        while len(terms) > 1:
            terms = [a + b for a, b in zip(terms[::2], terms[1::2])]
        terms += [
            lax.ppermute(terms[0], "nodes", [(i, i ^ d) for i in range(parts)]) for d in group
        ]
    grad_first, grad_second, grad_bias = total(moved, terms, grades)
    return grad_first.T, grad_bias.reshape(-1), grad_second.T


def solution(mesh):
    placed = (
        P("nodes", "feat"),
        P("nodes", None),
        P("nodes", None, None),
        P("nodes", None),
        P("nodes", None, None, None),
        P("nodes"),
        P("feat", None),
        P("feat"),
        P("feat", None),
    )
    return jax.shard_map(
        shards,
        mesh=mesh,
        in_specs=placed,
        out_specs=(P("feat", "nodes"), P("feat"), P("feat", None)),
        check_vma=False,
    )
```

```python
import functools
import math

import jax
import jax.numpy as jnp
from jax import lax
from jax.experimental import pallas as pl
from jax.experimental.pallas import tpu as pltpu
from jax.sharding import PartitionSpec as P

F32 = jnp.float32
BF16 = jnp.bfloat16
NT = (((1,), (1,)), ((), ()))
NN = (((1,), (0,)), ((), ()))
BLK = 128
MIB = 1 << 20


def params(mib):
    return pltpu.CompilerParams(vmem_limit_bytes=mib * MIB)


def cost(flops, nbytes):
    return pl.CostEstimate(flops=flops, bytes_accessed=nbytes, transcendentals=0)


def dot(a, b, dims):
    return lax.dot_general(a, b, dims, preferred_element_type=F32)


def tree(terms):
    while len(terms) > 1:
        terms = [a + b for a, b in zip(terms[::2], terms[1::2])]
    return terms[0]


def in_hbm(x):
    return pltpu.with_memory_space_constraint(x, pltpu.HBM)


def tree(terms):
    while len(terms) > 1:
        terms = [a + b for a, b in zip(terms[::2], terms[1::2])]
    return terms[0]


def in_hbm(x):
    return pltpu.with_memory_space_constraint(x, pltpu.HBM)


def in_vmem(x):
    return pltpu.with_memory_space_constraint(x, pltpu.VMEM)


def pick_kernel(table, features, out, held, sems):
    slots = out.shape[0]
    load = pltpu.make_async_copy(features, held, sems.at[0])
    load.start()
    load.wait()

    @pl.loop(0, slots, unroll=8)
    def _(k):
        rows = pl.ds(pl.multiple_of(table[k] * BLK, BLK), BLK)
        pltpu.make_async_copy(held.at[rows], out.at[k], sems.at[1]).start()

    pltpu.make_async_copy(out, out, sems.at[1]).wait()


def pick(features, table):
    slots = table.shape[0]
    return pl.pallas_call(
        pick_kernel,
        grid_spec=pltpu.PrefetchScalarGridSpec(
            num_scalar_prefetch=1,
            grid=(),
            in_specs=[pl.BlockSpec(memory_space=pltpu.HBM)],
            out_specs=pl.BlockSpec(memory_space=pltpu.HBM),
            scratch_shapes=[
                pltpu.VMEM(features.shape, BF16),
                pltpu.SemaphoreType.DMA((2,)),
            ],
        ),
        out_shape=pltpu.HBM((slots, BLK, features.shape[1]), BF16),
        compiler_params=params(6),
        cost_estimate=cost(0, 6 * MIB),
        name="pick",
    )(table, in_hbm(features))


def agg_kernel(which, nfeat, src, counts, me, arrived, tiles_hbm, features, after, *refs):
    outs, (tiles, own, sems) = refs[: len(which)], refs[len(which) :]
    group, per = tiles.shape[1:3]
    moves = []
    firsts = [lax.rem(me[0] + k, nfeat) * group for k in which]
    for i, first in enumerate(firsts):
        rows = pl.ds(pl.multiple_of(first * BLK, BLK), group * BLK)
        pair = (
            pltpu.make_async_copy(tiles_hbm.at[pl.ds(first, group)], tiles.at[i], sems.at[2 * i]),
            pltpu.make_async_copy(features.at[rows], own.at[i], sems.at[2 * i + 1]),
        )
        for move in pair:
            move.start()
        moves.append(pair)
    for i, (first, out) in enumerate(zip(firsts, outs)):
        for move in moves[i]:
            move.wait()
        for b in range(group):
            rows, weights = [], []
            for t in range(per):
                slot = src[(first + b) * per + t]
                live = lax.rem(slot, 2) < counts[lax.div(slot, 2)]
                rows.append(arrived[slot])
                weights.append(tiles[i, b, t] * jnp.where(live, 1.0, 0.0).astype(BF16))
            total = dot(jnp.concatenate(weights, 1), jnp.concatenate(rows, 0), NN)
            at = pl.ds(b * BLK, BLK)
            out[at, :] = (own[i, at, :].astype(F32) + total).astype(BF16)


def aggregate(src, counts, me, arrived, tiles, features, nfeat, which, after):
    nblocks, per = tiles.shape[:2]
    group = nblocks // nfeat
    width = features.shape[1]
    piece = jax.ShapeDtypeStruct((group * BLK, width), BF16)
    hbm = pl.BlockSpec(memory_space=pltpu.HBM)
    vmem = pl.BlockSpec(memory_space=pltpu.VMEM)
    return pl.pallas_call(
        functools.partial(agg_kernel, which, nfeat),
        grid_spec=pltpu.PrefetchScalarGridSpec(
            num_scalar_prefetch=3,
            grid=(),
            in_specs=[vmem, hbm, hbm, pl.BlockSpec(memory_space=pl.ANY)],
            out_specs=[vmem] * len(which),
            scratch_shapes=[
                pltpu.VMEM((len(which), group, per, BLK, BLK), BF16),
                pltpu.VMEM((len(which), group * BLK, width), BF16),
                pltpu.SemaphoreType.DMA((2 * len(which),)),
            ],
        ),
        out_shape=[piece] * len(which),
        compiler_params=params(12),
        cost_estimate=cost(len(which) * group * per * 2 * BLK * BLK * width, 8 * MIB),
        name="aggregate",
    )(src, counts, me, in_vmem(arrived), in_hbm(tiles), in_hbm(features), after)


def dense_kernel(nfeat, *refs):
    pieces, (weights, bias, second, hidden, proj) = refs[:nfeat], refs[nfeat:]
    pre = dot(weights[...], jnp.concatenate([piece[...] for piece in pieces], 1), NT)
    hid = jnp.maximum(pre + bias[...], 0.0).astype(BF16)
    hidden[...] = hid
    out = dot(second[...], hid, NN)
    for b in range(proj.shape[0]):
        proj[b] = out[:, b * BLK : (b + 1) * BLK]


def dense(pieces, weights, bias, second):
    nodes, width = pieces[0].shape
    nfeat = len(pieces)
    hid = weights.shape[0]
    grades = second.shape[0]
    step = 256
    return pl.pallas_call(
        functools.partial(dense_kernel, nfeat),
        grid=(nodes // step,),
        in_specs=[pl.BlockSpec((step, width), lambda g: (g, 0))] * nfeat
        + [
            pl.BlockSpec(weights.shape, lambda g: (0, 0)),
            pl.BlockSpec((hid, 1), lambda g: (0, 0)),
            pl.BlockSpec((grades, hid), lambda g: (0, 0)),
        ],
        out_specs=[
            pl.BlockSpec((hid, step), lambda g: (0, g)),
            pl.BlockSpec((step // BLK, grades, BLK), lambda g: (g, 0, 0)),
        ],
        out_shape=[
            jax.ShapeDtypeStruct((hid, nodes), BF16),
            jax.ShapeDtypeStruct((nodes // BLK, grades, BLK), F32),
        ],
        compiler_params=params(20),
        cost_estimate=cost(2 * nodes * hid * width * nfeat, 7 * MIB),
        name="dense",
    )(*pieces, weights, bias, second)


def spread_kernel(table, me, p0, p1, p2, p3, whole, out):
    nfeat, group = 4, p0.shape[0]
    for k, piece in enumerate((p0, p1, p2, p3)):
        owner = lax.rem(me[0] + nfeat - k, nfeat)
        whole[pl.ds(owner * group, group)] = piece[...]

    @pl.loop(0, out.shape[0], unroll=8)
    def _(k):
        out[k] = whole[table[k]]


def spread(table, me, pieces):
    group, grades, _ = pieces[0].shape
    slots = table.shape[0]
    vmem = pl.BlockSpec(memory_space=pltpu.VMEM)
    return pl.pallas_call(
        spread_kernel,
        grid_spec=pltpu.PrefetchScalarGridSpec(
            num_scalar_prefetch=2,
            grid=(),
            in_specs=[vmem] * 4,
            out_specs=[vmem] * 2,
        ),
        out_shape=[
            jax.ShapeDtypeStruct((group * 4, grades, BLK), F32),
            jax.ShapeDtypeStruct((slots, grades, BLK), F32),
        ],
        compiler_params=params(4),
        cost_estimate=cost(0, MIB),
        name="spread",
    )(table, me, *pieces)


def logits_kernel(
    scale, src, counts, me, arrived, own, labels, tiles, dlog_out, slots_out, parts, field, grad_b, sums
):
    nblocks, per = tiles.shape[:2]
    nslots, grades, _ = arrived.shape
    mine = dlog_out.shape[0]

    def live_of(slot):
        return jnp.where(lax.rem(slot, 2) < counts[lax.div(slot, 2)], 1.0, 0.0)

    x = arrived[...]
    for i in range(3):
        y = x.astype(BF16)
        parts[:, i * grades : (i + 1) * grades, :] = y
        x = x - y.astype(F32)

    @pl.loop(0, nblocks, unroll=8)
    def _(b):
        rows, weights = [], []
        for t in range(per):
            slot = src[b * per + t]
            rows.append(parts[slot] * live_of(slot).astype(BF16))
            weights.append(tiles[b, t])
        triple = dot(jnp.concatenate(rows, 1), jnp.concatenate(weights, 1), NT)
        field[b] = own[b] + (
            triple[:grades] + (triple[grades : 2 * grades] + triple[2 * grades :])
        )

    expo = jnp.exp(field[...])
    probs = expo / jnp.sum(expo, axis=1, keepdims=True)
    grade = lax.broadcasted_iota(jnp.int32, field.shape, 1)
    onehot = jnp.where(labels[...] == grade, 1.0, 0.0)
    dlog = (probs - onehot) * scale
    field[...] = dlog
    grad_b[...] = dlog.astype(BF16)
    dlog_out[...] = field[pl.ds(me[0] * mine, mine)]
    sums[...] = jnp.zeros_like(sums)

    @pl.loop(0, nblocks, unroll=8)
    def _(b):
        back = dot(grad_b[b], jnp.concatenate([tiles[b, t] for t in range(per)], 1), NN)
        for t in range(per):
            slot = src[b * per + t]
            sums[slot] += back[:, t * BLK : (t + 1) * BLK] * live_of(slot)

    slots_out[...] = sums[...].astype(BF16)


def logits_back(src, counts, me, arrived, own, labels, tiles, scale, nfeat):
    nblocks, per = tiles.shape[:2]
    nslots, grades, _ = arrived.shape
    vmem = pl.BlockSpec(memory_space=pltpu.VMEM)
    return pl.pallas_call(
        functools.partial(logits_kernel, scale),
        grid_spec=pltpu.PrefetchScalarGridSpec(
            num_scalar_prefetch=3,
            grid=(),
            in_specs=[vmem] * 4,
            out_specs=[vmem] * 2,
            scratch_shapes=[
                pltpu.VMEM((nslots, 3 * grades, BLK), BF16),
                pltpu.VMEM((nblocks, grades, BLK), F32),
                pltpu.VMEM((nblocks, grades, BLK), BF16),
                pltpu.VMEM(arrived.shape, F32),
            ],
        ),
        out_shape=[
            jax.ShapeDtypeStruct((nblocks // nfeat, grades, BLK), F32),
            jax.ShapeDtypeStruct(arrived.shape, BF16),
        ],
        compiler_params=params(8),
        cost_estimate=cost(nblocks * per * 2 * 64 * BLK**2, 6 * MIB),
        name="logits",
    )(src, counts, me, arrived, own, labels, tiles)


def small_kernel(table, me, returned, dlog, hidden, second, dpre_out, *refs):
    small, (total, dproj, buf) = refs[:-3], refs[-3:]
    group, grades, _ = dlog.shape
    g = pl.program_id(0)
    width = hidden.shape[0]

    @pl.when(g == 0)
    def _():
        total[pl.ds(0, group)] = dlog[...]

        @pl.loop(0, returned.shape[0], unroll=8)
        def _(k):
            at = table[k] - me[0] * group
            at = jnp.where((at >= 0) & (at < group), at, group)
            total[at] += returned[k].astype(F32)

        for b in range(group):
            dproj[:, b * BLK : (b + 1) * BLK] = total[b].astype(BF16)

    active = hidden[...]
    dproj_b = dproj[...]
    dpre = jnp.where(active > 0, dot(second[...], dproj_b, NN), 0.0)
    dpre_out[...] = dpre.astype(BF16)
    buf[pl.ds(0, grades), :] = dot(dproj_b, active, NT)
    part = dpre[:, :BLK]
    for i in range(1, dpre.shape[1] // BLK):
        part += dpre[:, i * BLK : (i + 1) * BLK]
    buf[pl.ds(grades, 8), :] = jnp.broadcast_to(
        jnp.sum(part.T, axis=0, keepdims=True), (8, width)
    )
    for k, out in enumerate(small):

        @pl.when(g == k)
        def _():
            out[...] = buf[...]


def small_gradients(table, me, returned, dlog, hidden, second, nfeat):
    hid, nodes = hidden.shape
    group, grades, _ = dlog.shape
    width = hid // nfeat
    turn = lambda g, m: lax.rem(m[0] + nfeat - g, nfeat)
    whole3 = lambda g, t, m: (0, 0, 0)
    small = jax.ShapeDtypeStruct((grades + 8, width), F32)
    return pl.pallas_call(
        small_kernel,
        grid_spec=pltpu.PrefetchScalarGridSpec(
            num_scalar_prefetch=2,
            grid=(nfeat,),
            in_specs=[
                pl.BlockSpec(returned.shape, whole3),
                pl.BlockSpec(dlog.shape, whole3),
                pl.BlockSpec((width, nodes), lambda g, t, m: (turn(g, m), 0)),
                pl.BlockSpec((width, grades), lambda g, t, m: (turn(g, m), 0)),
            ],
            out_specs=[pl.BlockSpec((width, nodes), lambda g, t, m: (turn(g, m), 0))]
            + [pl.BlockSpec(small.shape, lambda g, t, m: (0, 0))] * nfeat,
            scratch_shapes=[
                pltpu.VMEM((group + 1, grades, BLK), F32),
                pltpu.VMEM((grades, nodes), BF16),
                pltpu.VMEM(small.shape, F32),
            ],
        ),
        out_shape=[pltpu.HBM((hid, nodes), BF16)] + [small] * nfeat,
        compiler_params=params(16),
        cost_estimate=cost(2 * nodes * hid * 256, 4 * MIB),
        name="small_gradients",
    )(table, me, returned, dlog, hidden, second)


def big_kernel(me, dpre, *refs):
    pieces, out = refs[:-1], refs[-1]
    nfeat = len(pieces)
    for k, piece in enumerate(pieces):
        owner = lax.rem(me[0] + nfeat - k, nfeat)
        grad = dot(dpre[...], piece[...], NN).astype(BF16)
        out[:, owner] = grad.reshape(out.shape[0], out.shape[2], out.shape[3])


def big_gradient(me, dpre, pieces, parts):
    nfeat = len(pieces)
    hid, nodes = dpre.shape
    width = pieces[0].shape[1]
    steps = 2
    return pl.pallas_call(
        big_kernel,
        grid_spec=pltpu.PrefetchScalarGridSpec(
            num_scalar_prefetch=1,
            grid=(steps,),
            in_specs=[pl.BlockSpec((hid // steps, nodes), lambda g, m: (g, 0))]
            + [pl.BlockSpec((nodes, width), lambda g, m: (0, 0))] * nfeat,
            out_specs=pl.BlockSpec(
                (parts // steps, nfeat, hid // parts, width), lambda g, m: (g, 0, 0, 0)
            ),
        ),
        out_shape=pltpu.HBM((parts, nfeat, hid // parts, width), BF16),
        compiler_params=params(24),
        cost_estimate=cost(2 * nodes * hid * hid, 6 * MIB),
        name="big_gradient",
    )(me, in_hbm(dpre), *pieces)


def total_kernel(nsmall, arrived, *refs):
    small, (out, second, bias, acc) = refs[:nsmall], refs[nsmall:]
    g = pl.program_id(0)

    @pl.when(g == 0)
    def _():
        acc[...] = jnp.zeros_like(acc)
        whole = tree([ref[...] for ref in small])
        grades = second.shape[0]
        second[...] = whole[:grades]
        bias[...] = whole[grades : grades + 1]

    total = arrived[0].astype(F32)
    for i in range(1, arrived.shape[0]):
        total += arrived[i].astype(F32)
    acc[...] += total

    @pl.when(g == pl.num_programs(0) - 1)
    def _():
        out[...] = acc[...]


def total(arrived, small, grades):
    n, cols, rows = arrived.shape
    step = n // 8
    whole = lambda g: (0, 0)
    return pl.pallas_call(
        functools.partial(total_kernel, len(small)),
        grid=(n // step,),
        in_specs=[pl.BlockSpec((step, cols, rows), lambda g: (g, 0, 0))]
        + [pl.BlockSpec(small[0].shape, whole)] * len(small),
        out_specs=[
            pl.BlockSpec((cols, rows), whole),
            pl.BlockSpec((grades, rows), whole),
            pl.BlockSpec((1, rows), whole),
        ],
        out_shape=[
            jax.ShapeDtypeStruct((cols, rows), F32),
            jax.ShapeDtypeStruct((grades, rows), F32),
            jax.ShapeDtypeStruct((1, rows), F32),
        ],
        scratch_shapes=[pltpu.VMEM((cols, rows), F32)],
        compiler_params=params(8),
        cost_estimate=cost(0, 2 * MIB),
        name="total",
    )(arrived, *small)


def shards(features, pair_count, send_blocks, tile_src, tiles, labels, w_first, b_first, w_second):
    nblocks = tile_src.shape[0]
    parts = lax.axis_size("nodes")
    nfeat = lax.axis_size("feat")
    slots = send_blocks.shape[2]
    grades = w_second.shape[1]
    hid = w_first.shape[1]
    axis = lax.axis_index("feat").astype(jnp.int32)
    me = axis.reshape(1)
    table = send_blocks.reshape(parts * slots)
    src = tile_src.reshape(-1)
    counts = pair_count.reshape(-1)

    def ahead(x, k):
        return lax.ppermute(x, "feat", [(i, (i + k) % nfeat) for i in range(nfeat)])

    def swap(x):
        shaped = x.reshape(parts, slots, *x.shape[1:])
        moved = lax.all_to_all(shaped, "nodes", split_axis=0, concat_axis=0, tiled=True)
        return moved.reshape(x.shape)

    arrived = swap(pick(features, table))

    flat = w_first.T
    weights = jnp.concatenate([flat] + [ahead(flat, k) for k in range(1, nfeat)], 1)
    consts = jnp.concatenate(
        [w_second.T.astype(F32), jnp.broadcast_to(b_first[None], (8, b_first.shape[0]))], 0
    )
    turned = [consts] + [ahead(consts, k) for k in range(1, nfeat)]
    ring = jnp.stack([turned[k] for k in (3, 2, 1, 0, 3, 2, 1)])
    ordered = lax.dynamic_slice_in_dim(ring, nfeat - 1 - axis, nfeat, 0)
    second_t = ordered[:, :grades].transpose(1, 0, 2).reshape(grades, hid).astype(BF16)
    bias = ordered[:, grades].reshape(hid, 1)
    second = second_t.T

    arrived, weights, bias, second_t, second = lax.optimization_barrier(
        (arrived, weights, bias, second_t, second)
    )
    make = functools.partial(aggregate, src, counts, me, arrived, tiles, features, nfeat)
    (two,) = make((2,), features)
    one, three = make((1, 3), two)
    (own,) = make((0,), three)
    pieces = [own, ahead(one, 1), ahead(two, 2), ahead(three, 3)]
    hidden, proj = dense(pieces, weights, bias, second_t)

    projs = [proj] + [ahead(proj, k) for k in range(1, nfeat)]
    own, send = spread(table, me, projs)
    scale = 1.0 / math.sqrt(nblocks * BLK * parts)
    dlog, slotsum = logits_back(
        src, counts, me, swap(send), own, labels.reshape(nblocks, 1, BLK), tiles, scale, nfeat
    )
    dpre, *small = small_gradients(table, me, swap(slotsum), dlog, hidden, second, nfeat)
    chips = []
    for core in range(2):
        for k in range(nfeat):
            moves = [
                (p * nfeat + f, (p ^ core) * nfeat + (f - k) % nfeat)
                for p in range(parts)
                for f in range(nfeat)
            ]
            here = core == 0 and k == 0
            chips.append(small[k] if here else lax.ppermute(small[k], ("nodes", "feat"), moves))
    rest = tree(chips)
    big = big_gradient(me, dpre, pieces, parts)
    big, rest = lax.optimization_barrier((big, rest))
    moved = lax.all_to_all(
        big.reshape(parts * nfeat, *big.shape[2:]),
        ("nodes", "feat"),
        split_axis=0,
        concat_axis=0,
        tiled=True,
    )
    terms = [rest] + [
        lax.ppermute(rest, "nodes", [(i, i ^ d) for i in range(parts)])
        for d in range(2, parts, 2)
    ]
    grad_first, grad_second, grad_bias = total(moved, terms, grades)
    return grad_first.T, grad_bias.reshape(-1), grad_second.T


def solution(mesh):
    placed = (
        P("nodes", "feat"),
        P("nodes", None),
        P("nodes", None, None),
        P("nodes", None),
        P("nodes", None, None, None),
        P("nodes"),
        P("feat", None),
        P("feat"),
        P("feat", None),
    )
    return jax.shard_map(
        shards,
        mesh=mesh,
        in_specs=placed,
        out_specs=(P("feat", "nodes"), P("feat"), P("feat", None)),
        check_vma=False,
    )
```

```python
import functools
import math

import jax
import jax.numpy as jnp
from jax import lax
from jax.experimental import pallas as pl
from jax.experimental.pallas import tpu as pltpu
from jax.sharding import PartitionSpec as P

F32 = jnp.float32
BF16 = jnp.bfloat16
NT = (((1,), (1,)), ((), ()))
NN = (((1,), (0,)), ((), ()))
BLK = 128
MIB = 1 << 20


def params(mib):
    return pltpu.CompilerParams(vmem_limit_bytes=mib * MIB)


def cost(flops, nbytes):
    return pl.CostEstimate(flops=flops, bytes_accessed=nbytes, transcendentals=0)


def dot(a, b, dims):
    return lax.dot_general(a, b, dims, preferred_element_type=F32)


def tree(terms):
    while len(terms) > 1:
        terms = [a + b for a, b in zip(terms[::2], terms[1::2])]
    return terms[0]


def in_hbm(x):
    return pltpu.with_memory_space_constraint(x, pltpu.HBM)


def pick_kernel(chunk, table, features, out, held, sems):
    slots = out.shape[0]
    load = pltpu.make_async_copy(features.at[:, pl.ds(chunk * BLK, BLK)], held, sems.at[0])
    load.start()
    load.wait()

    @pl.loop(0, slots, unroll=8)
    def _(k):
        rows = pl.ds(pl.multiple_of(table[k] * BLK, BLK), BLK)
        pltpu.make_async_copy(held.at[rows], out.at[k], sems.at[1]).start()

    pltpu.make_async_copy(out, out, sems.at[1]).wait()


def pick(features, table, chunk):
    slots = table.shape[0]
    return pl.pallas_call(
        functools.partial(pick_kernel, chunk),
        grid_spec=pltpu.PrefetchScalarGridSpec(
            num_scalar_prefetch=1,
            grid=(),
            in_specs=[pl.BlockSpec(memory_space=pltpu.HBM)],
            out_specs=pl.BlockSpec(memory_space=pltpu.HBM),
            scratch_shapes=[
                pltpu.VMEM((features.shape[0], BLK), BF16),
                pltpu.SemaphoreType.DMA((2,)),
            ],
        ),
        out_shape=pltpu.HBM((slots, BLK, BLK), BF16),
        compiler_params=params(4),
        cost_estimate=cost(0, 4 * MIB),
        name="pick",
    )(table, in_hbm(features))


def agg_kernel(which, chunk, nfeat, src, counts, me, arrived_hbm, tiles_hbm, features, *refs):
    outs, (arrived, tiles, own, sems) = refs[: len(which)], refs[len(which) :]
    group, per = tiles.shape[1:3]
    moves = [pltpu.make_async_copy(arrived_hbm, arrived, sems.at[0])]
    firsts = [lax.rem(me[0] + k, nfeat) * group for k in which]
    for i, first in enumerate(firsts):
        rows = pl.ds(pl.multiple_of(first * BLK, BLK), group * BLK)
        moves.append(
            pltpu.make_async_copy(tiles_hbm.at[pl.ds(first, group)], tiles.at[i], sems.at[1 + 2 * i])
        )
        moves.append(
            pltpu.make_async_copy(
                features.at[rows, pl.ds(chunk * BLK, BLK)], own.at[i], sems.at[2 + 2 * i]
            )
        )
    for move in moves:
        move.start()
    moves[0].wait()
    for i, (first, out) in enumerate(zip(firsts, outs)):
        moves[1 + 2 * i].wait()
        moves[2 + 2 * i].wait()
        for b in range(group):
            rows, weights = [], []
            for t in range(per):
                slot = src[(first + b) * per + t]
                live = lax.rem(slot, 2) < counts[lax.div(slot, 2)]
                rows.append(arrived[slot])
                weights.append(tiles[i, b, t] * jnp.where(live, 1.0, 0.0).astype(BF16))
            total = dot(jnp.concatenate(weights, 1), jnp.concatenate(rows, 0), NN)
            at = pl.ds(b * BLK, BLK)
            out[at, :] = (own[i, at, :].astype(F32) + total).astype(BF16)


def aggregate(src, counts, me, arrived, tiles, features, chunk, nfeat, which):
    nblocks, per = tiles.shape[:2]
    group = nblocks // nfeat
    piece = jax.ShapeDtypeStruct((group * BLK, BLK), BF16)
    hbm = pl.BlockSpec(memory_space=pltpu.HBM)
    return pl.pallas_call(
        functools.partial(agg_kernel, which, chunk, nfeat),
        grid_spec=pltpu.PrefetchScalarGridSpec(
            num_scalar_prefetch=3,
            grid=(),
            in_specs=[pl.BlockSpec(memory_space=pl.ANY), hbm, hbm],
            out_specs=[pl.BlockSpec(memory_space=pltpu.VMEM)] * len(which),
            scratch_shapes=[
                pltpu.VMEM(arrived.shape, BF16),
                pltpu.VMEM((len(which), group, per, BLK, BLK), BF16),
                pltpu.VMEM((len(which), group * BLK, BLK), BF16),
                pltpu.SemaphoreType.DMA((1 + 2 * len(which),)),
            ],
        ),
        out_shape=[piece] * len(which),
        compiler_params=params(14),
        cost_estimate=cost(len(which) * group * per * 2 * BLK**3, 8 * MIB),
        name="aggregate",
    )(src, counts, me, arrived, in_hbm(tiles), in_hbm(features))


def dense_kernel(nfeat, *refs):
    pieces, (weights, bias, second, hidden, proj) = refs[: 2 * nfeat], refs[2 * nfeat :]
    order = [pieces[i * nfeat + k][...] for k in range(nfeat) for i in range(2)]
    pre = dot(weights[...], jnp.concatenate(order, 1), NT)
    hid = jnp.maximum(pre + bias[...], 0.0).astype(BF16)
    hidden[...] = hid
    out = dot(second[...], hid, NN)
    for b in range(proj.shape[0]):
        proj[b] = out[:, b * BLK : (b + 1) * BLK]


def dense(pieces, weights, bias, second):
    nodes, nfeat = pieces[0].shape[0], len(pieces) // 2
    hid, width = weights.shape
    grades = second.shape[0]
    step = 256
    return pl.pallas_call(
        functools.partial(dense_kernel, nfeat),
        grid=(nodes // step,),
        in_specs=[pl.BlockSpec((step, BLK), lambda g: (g, 0))] * (2 * nfeat)
        + [
            pl.BlockSpec((hid, width), lambda g: (0, 0)),
            pl.BlockSpec((hid, 1), lambda g: (0, 0)),
            pl.BlockSpec((grades, hid), lambda g: (0, 0)),
        ],
        out_specs=[
            pl.BlockSpec((hid, step), lambda g: (0, g)),
            pl.BlockSpec((step // BLK, grades, BLK), lambda g: (g, 0, 0)),
        ],
        out_shape=[
            jax.ShapeDtypeStruct((hid, nodes), BF16),
            jax.ShapeDtypeStruct((nodes // BLK, grades, BLK), F32),
        ],
        compiler_params=params(20),
        cost_estimate=cost(2 * nodes * hid * width, 7 * MIB),
        name="dense",
    )(*pieces, weights, bias, second)


def spread_kernel(table, me, p0, p1, p2, p3, whole, out):
    nfeat, group = 4, p0.shape[0]
    for k, piece in enumerate((p0, p1, p2, p3)):
        owner = lax.rem(me[0] + nfeat - k, nfeat)
        whole[pl.ds(owner * group, group)] = piece[...]

    @pl.loop(0, out.shape[0], unroll=8)
    def _(k):
        out[k] = whole[table[k]]


def spread(table, me, pieces):
    group, grades, _ = pieces[0].shape
    slots = table.shape[0]
    vmem = pl.BlockSpec(memory_space=pltpu.VMEM)
    return pl.pallas_call(
        spread_kernel,
        grid_spec=pltpu.PrefetchScalarGridSpec(
            num_scalar_prefetch=2,
            grid=(),
            in_specs=[vmem] * 4,
            out_specs=[vmem] * 2,
        ),
        out_shape=[
            jax.ShapeDtypeStruct((group * 4, grades, BLK), F32),
            jax.ShapeDtypeStruct((slots, grades, BLK), F32),
        ],
        compiler_params=params(4),
        cost_estimate=cost(0, MIB),
        name="spread",
    )(table, me, *pieces)


def logits_kernel(
    scale, src, counts, me, arrived, own, labels, tiles, dlog_out, slots_out, parts, field, grad_b, sums
):
    nblocks, per = tiles.shape[:2]
    nslots, grades, _ = arrived.shape
    mine = dlog_out.shape[0]

    def live_of(slot):
        return jnp.where(lax.rem(slot, 2) < counts[lax.div(slot, 2)], 1.0, 0.0)

    x = arrived[...]
    for i in range(3):
        y = x.astype(BF16)
        parts[:, i * grades : (i + 1) * grades, :] = y
        x = x - y.astype(F32)

    @pl.loop(0, nblocks, unroll=8)
    def _(b):
        rows, weights = [], []
        for t in range(per):
            slot = src[b * per + t]
            rows.append(parts[slot] * live_of(slot).astype(BF16))
            weights.append(tiles[b, t])
        triple = dot(jnp.concatenate(rows, 1), jnp.concatenate(weights, 1), NT)
        field[b] = own[b] + (
            triple[:grades] + (triple[grades : 2 * grades] + triple[2 * grades :])
        )

    expo = jnp.exp(field[...])
    probs = expo / jnp.sum(expo, axis=1, keepdims=True)
    grade = lax.broadcasted_iota(jnp.int32, field.shape, 1)
    onehot = jnp.where(labels[...] == grade, 1.0, 0.0)
    dlog = (probs - onehot) * scale
    field[...] = dlog
    grad_b[...] = dlog.astype(BF16)
    dlog_out[...] = field[pl.ds(me[0] * mine, mine)]
    sums[...] = jnp.zeros_like(sums)

    @pl.loop(0, nblocks, unroll=8)
    def _(b):
        back = dot(grad_b[b], jnp.concatenate([tiles[b, t] for t in range(per)], 1), NN)
        for t in range(per):
            slot = src[b * per + t]
            sums[slot] += back[:, t * BLK : (t + 1) * BLK] * live_of(slot)

    slots_out[...] = sums[...].astype(BF16)


def logits_back(src, counts, me, arrived, own, labels, tiles, scale, nfeat):
    nblocks, per = tiles.shape[:2]
    nslots, grades, _ = arrived.shape
    vmem = pl.BlockSpec(memory_space=pltpu.VMEM)
    return pl.pallas_call(
        functools.partial(logits_kernel, scale),
        grid_spec=pltpu.PrefetchScalarGridSpec(
            num_scalar_prefetch=3,
            grid=(),
            in_specs=[vmem] * 4,
            out_specs=[vmem] * 2,
            scratch_shapes=[
                pltpu.VMEM((nslots, 3 * grades, BLK), BF16),
                pltpu.VMEM((nblocks, grades, BLK), F32),
                pltpu.VMEM((nblocks, grades, BLK), BF16),
                pltpu.VMEM(arrived.shape, F32),
            ],
        ),
        out_shape=[
            jax.ShapeDtypeStruct((nblocks // nfeat, grades, BLK), F32),
            jax.ShapeDtypeStruct(arrived.shape, BF16),
        ],
        compiler_params=params(8),
        cost_estimate=cost(nblocks * per * 2 * 64 * BLK**2, 6 * MIB),
        name="logits",
    )(src, counts, me, arrived, own, labels, tiles)


def small_kernel(table, me, returned, dlog, hidden, second, dpre_out, *refs):
    small, (total, dproj, buf) = refs[:-3], refs[-3:]
    group, grades, _ = dlog.shape
    g = pl.program_id(0)
    width = hidden.shape[0]

    @pl.when(g == 0)
    def _():
        total[pl.ds(0, group)] = dlog[...]

        @pl.loop(0, returned.shape[0], unroll=8)
        def _(k):
            at = table[k] - me[0] * group
            at = jnp.where((at >= 0) & (at < group), at, group)
            total[at] += returned[k].astype(F32)

        for b in range(group):
            dproj[:, b * BLK : (b + 1) * BLK] = total[b].astype(BF16)

    active = hidden[...]
    dproj_b = dproj[...]
    dpre = jnp.where(active > 0, dot(second[...], dproj_b, NN), 0.0)
    dpre_out[...] = dpre.astype(BF16)
    buf[pl.ds(0, grades), :] = dot(dproj_b, active, NT)
    part = dpre[:, :BLK]
    for i in range(1, dpre.shape[1] // BLK):
        part += dpre[:, i * BLK : (i + 1) * BLK]
    buf[pl.ds(grades, 8), :] = jnp.broadcast_to(
        jnp.sum(part.T, axis=0, keepdims=True), (8, width)
    )
    for k, out in enumerate(small):

        @pl.when(g == k)
        def _():
            out[...] = buf[...]


def small_gradients(table, me, returned, dlog, hidden, second, nfeat):
    hid, nodes = hidden.shape
    group, grades, _ = dlog.shape
    width = hid // nfeat
    turn = lambda g, m: lax.rem(m[0] + nfeat - g, nfeat)
    whole3 = lambda g, t, m: (0, 0, 0)
    small = jax.ShapeDtypeStruct((grades + 8, width), F32)
    return pl.pallas_call(
        small_kernel,
        grid_spec=pltpu.PrefetchScalarGridSpec(
            num_scalar_prefetch=2,
            grid=(nfeat,),
            in_specs=[
                pl.BlockSpec(returned.shape, whole3),
                pl.BlockSpec(dlog.shape, whole3),
                pl.BlockSpec((width, nodes), lambda g, t, m: (turn(g, m), 0)),
                pl.BlockSpec((width, grades), lambda g, t, m: (turn(g, m), 0)),
            ],
            out_specs=[pl.BlockSpec((width, nodes), lambda g, t, m: (turn(g, m), 0))]
            + [pl.BlockSpec(small.shape, lambda g, t, m: (0, 0))] * nfeat,
            scratch_shapes=[
                pltpu.VMEM((group + 1, grades, BLK), F32),
                pltpu.VMEM((grades, nodes), BF16),
                pltpu.VMEM(small.shape, F32),
            ],
        ),
        out_shape=[pltpu.HBM((hid, nodes), BF16)] + [small] * nfeat,
        compiler_params=params(16),
        cost_estimate=cost(2 * nodes * hid * 256, 4 * MIB),
        name="small_gradients",
    )(table, me, returned, dlog, hidden, second)


def big_kernel(me, dpre, *refs):
    pieces, out = refs[:-1], refs[-1]
    nfeat = len(pieces) // 2
    for k in range(nfeat):
        owner = lax.rem(me[0] + nfeat - k, nfeat)
        both = jnp.concatenate([pieces[k][...], pieces[nfeat + k][...]], 1)
        grad = dot(dpre[...], both, NN).astype(BF16)
        out[:, owner] = grad.reshape(out.shape[0], out.shape[2], out.shape[3])


def big_gradient(me, dpre, pieces, parts):
    nfeat = len(pieces) // 2
    hid, nodes = dpre.shape
    steps = 2
    return pl.pallas_call(
        big_kernel,
        grid_spec=pltpu.PrefetchScalarGridSpec(
            num_scalar_prefetch=1,
            grid=(steps,),
            in_specs=[pl.BlockSpec((hid // steps, nodes), lambda g, m: (g, 0))]
            + [pl.BlockSpec((nodes, BLK), lambda g, m: (0, 0))] * (2 * nfeat),
            out_specs=pl.BlockSpec(
                (parts // steps, nfeat, hid // parts, 2 * BLK), lambda g, m: (g, 0, 0, 0)
            ),
        ),
        out_shape=pltpu.HBM((parts, nfeat, hid // parts, 2 * BLK), BF16),
        compiler_params=params(24),
        cost_estimate=cost(2 * nodes * hid * hid, 6 * MIB),
        name="big_gradient",
    )(me, in_hbm(dpre), *pieces)


def total_kernel(nsmall, arrived, *refs):
    small, (out, second, bias, acc) = refs[:nsmall], refs[nsmall:]
    g = pl.program_id(0)

    @pl.when(g == 0)
    def _():
        acc[...] = jnp.zeros_like(acc)
        whole = tree([ref[...] for ref in small])
        grades = second.shape[0]
        second[...] = whole[:grades]
        bias[...] = whole[grades : grades + 1]

    total = arrived[0].astype(F32)
    for i in range(1, arrived.shape[0]):
        total += arrived[i].astype(F32)
    acc[...] += total

    @pl.when(g == pl.num_programs(0) - 1)
    def _():
        out[...] = acc[...]


def total(arrived, small, grades):
    n, cols, rows = arrived.shape
    step = n // 8
    whole = lambda g: (0, 0)
    return pl.pallas_call(
        functools.partial(total_kernel, len(small)),
        grid=(n // step,),
        in_specs=[pl.BlockSpec((step, cols, rows), lambda g: (g, 0, 0))]
        + [pl.BlockSpec(small[0].shape, whole)] * len(small),
        out_specs=[
            pl.BlockSpec((cols, rows), whole),
            pl.BlockSpec((grades, rows), whole),
            pl.BlockSpec((1, rows), whole),
        ],
        out_shape=[
            jax.ShapeDtypeStruct((cols, rows), F32),
            jax.ShapeDtypeStruct((grades, rows), F32),
            jax.ShapeDtypeStruct((1, rows), F32),
        ],
        scratch_shapes=[pltpu.VMEM((cols, rows), F32)],
        compiler_params=params(8),
        cost_estimate=cost(0, 2 * MIB),
        name="total",
    )(arrived, *small)


def shards(features, pair_count, send_blocks, tile_src, tiles, labels, w_first, b_first, w_second):
    nblocks = tile_src.shape[0]
    parts = lax.axis_size("nodes")
    nfeat = lax.axis_size("feat")
    slots = send_blocks.shape[2]
    grades = w_second.shape[1]
    hid = w_first.shape[1]
    axis = lax.axis_index("feat").astype(jnp.int32)
    me = axis.reshape(1)
    table = send_blocks.reshape(parts * slots)
    src = tile_src.reshape(-1)
    counts = pair_count.reshape(-1)

    def ahead(x, k):
        return lax.ppermute(x, "feat", [(i, (i + k) % nfeat) for i in range(nfeat)])

    def nearby(x, masks):
        return [x] + [
            lax.ppermute(x, "nodes", [(i, i ^ mask) for i in range(parts)]) for mask in masks
        ]

    def swap(x):
        shaped = x.reshape(parts, slots, *x.shape[1:])
        moved = lax.all_to_all(shaped, "nodes", split_axis=0, concat_axis=0, tiled=True)
        return moved.reshape(x.shape)

    arrived = [swap(pick(features, table, 0))]
    send = pick(features, table, 1)

    flat = w_first.T
    weights = [ahead(flat, k) for k in (2, 1, 3)]
    consts = jnp.concatenate(
        [w_second.T.astype(F32), jnp.broadcast_to(b_first[None], (8, b_first.shape[0]))], 0
    )
    send, weights = lax.optimization_barrier((send, weights))
    consts, first_weight = lax.optimization_barrier((consts, weights[1]))
    weights = jnp.concatenate([flat, first_weight, weights[0], weights[2]], 1)
    turned = [consts] + [ahead(consts, k) for k in range(1, nfeat)]
    ring = jnp.stack([turned[k] for k in (3, 2, 1, 0, 3, 2, 1)])
    ordered = lax.dynamic_slice_in_dim(ring, nfeat - 1 - axis, nfeat, 0)
    second_t = ordered[:, :grades].transpose(1, 0, 2).reshape(grades, hid).astype(BF16)
    bias = ordered[:, grades].reshape(hid, 1)
    second = second_t.T

    arrived.append(swap(send))
    others = (2, 1, 3)
    make = functools.partial(aggregate, src, counts, me)
    first = [None] * nfeat
    *sent, first[0] = make(arrived[0], tiles, features, 0, nfeat, others + (0,))
    for k, piece in zip(others, sent):
        first[k] = ahead(piece, k)
    last = [None] * nfeat
    for k, piece in zip(others, make(arrived[1], tiles, features, 1, nfeat, others)):
        last[k] = ahead(piece, k)
    (last[0],) = make(arrived[1], tiles, features, 1, nfeat, (0,))
    hidden, proj = dense(first + last, weights, bias, second_t)

    projs = [proj] + [ahead(proj, k) for k in range(1, nfeat)]
    own, send = spread(table, me, projs)
    scale = 1.0 / math.sqrt(nblocks * BLK * parts)
    dlog, slotsum = logits_back(
        src, counts, me, swap(send), own, labels.reshape(nblocks, 1, BLK), tiles, scale, nfeat
    )
    dpre, *small = small_gradients(table, me, swap(slotsum), dlog, hidden, second, nfeat)
    rest = small[0]
    for k in range(1, nfeat):
        rest = rest + ahead(small[k], nfeat - k)
    big = big_gradient(me, dpre, first + last, parts)
    rest = nearby(rest, (1, 2, 3))
    big, rest = lax.optimization_barrier((big, tree(rest)))
    moved = lax.all_to_all(
        big.reshape(parts * nfeat, *big.shape[2:]),
        ("nodes", "feat"),
        split_axis=0,
        concat_axis=0,
        tiled=True,
    )
    terms = nearby(rest, range(4, parts, 4))
    grad_first, grad_second, grad_bias = total(moved, terms, grades)
    return grad_first.T, grad_bias.reshape(-1), grad_second.T


def solution(mesh):
    placed = (
        P("nodes", "feat"),
        P("nodes", None),
        P("nodes", None, None),
        P("nodes", None),
        P("nodes", None, None, None),
        P("nodes"),
        P("feat", None),
        P("feat"),
        P("feat", None),
    )
    return jax.shard_map(
        shards,
        mesh=mesh,
        in_specs=placed,
        out_specs=(P("feat", "nodes"), P("feat"), P("feat", None)),
        check_vma=False,
    )
```

```python
import functools
import math

import jax
import jax.numpy as jnp
from jax import lax
from jax.experimental import pallas as pl
from jax.experimental.pallas import tpu as pltpu
from jax.sharding import PartitionSpec as P

F32 = jnp.float32
BF16 = jnp.bfloat16
NT = (((1,), (1,)), ((), ()))
NN = (((1,), (0,)), ((), ()))
BLK = 128
MIB = 1 << 20


def params(mib):
    return pltpu.CompilerParams(vmem_limit_bytes=mib * MIB)


def cost(flops, nbytes):
    return pl.CostEstimate(flops=flops, bytes_accessed=nbytes, transcendentals=0)


def dot(a, b, dims):
    return lax.dot_general(a, b, dims, preferred_element_type=F32)


def tree(terms):
    while len(terms) > 1:
        terms = [a + b for a, b in zip(terms[::2], terms[1::2])]
    return terms[0]


def in_hbm(x):
    return pltpu.with_memory_space_constraint(x, pltpu.HBM)


def pick_kernel(chunk, table, features, out, held, sems):
    slots = out.shape[0]
    load = pltpu.make_async_copy(features.at[:, pl.ds(chunk * BLK, BLK)], held, sems.at[0])
    load.start()
    load.wait()

    @pl.loop(0, slots, unroll=8)
    def _(k):
        rows = pl.ds(pl.multiple_of(table[k] * BLK, BLK), BLK)
        pltpu.make_async_copy(held.at[rows], out.at[k], sems.at[1]).start()

    pltpu.make_async_copy(out, out, sems.at[1]).wait()


def pick(features, table, chunk):
    slots = table.shape[0]
    return pl.pallas_call(
        functools.partial(pick_kernel, chunk),
        grid_spec=pltpu.PrefetchScalarGridSpec(
            num_scalar_prefetch=1,
            grid=(),
            in_specs=[pl.BlockSpec(memory_space=pltpu.HBM)],
            out_specs=pl.BlockSpec(memory_space=pltpu.HBM),
            scratch_shapes=[
                pltpu.VMEM((features.shape[0], BLK), BF16),
                pltpu.SemaphoreType.DMA((2,)),
            ],
        ),
        out_shape=pltpu.HBM((slots, BLK, BLK), BF16),
        compiler_params=params(63),
        cost_estimate=cost(0, 4 * MIB),
        name="pick",
    )(table, in_hbm(features))


def agg_kernel(which, chunk, nfeat, src, counts, me, arrived_hbm, tiles_hbm, features, *refs):
    outs, (arrived, tiles, own, sems) = refs[: len(which)], refs[len(which) :]
    group, per = tiles.shape[1:3]
    moves = [pltpu.make_async_copy(arrived_hbm, arrived, sems.at[0])]
    firsts = [lax.rem(me[0] + k, nfeat) * group for k in which]
    for i, first in enumerate(firsts):
        rows = pl.ds(pl.multiple_of(first * BLK, BLK), group * BLK)
        moves.append(
            pltpu.make_async_copy(tiles_hbm.at[pl.ds(first, group)], tiles.at[i], sems.at[1 + 2 * i])
        )
        moves.append(
            pltpu.make_async_copy(
                features.at[rows, pl.ds(chunk * BLK, BLK)], own.at[i], sems.at[2 + 2 * i]
            )
        )
    for move in moves:
        move.start()
    moves[0].wait()
    for i, (first, out) in enumerate(zip(firsts, outs)):
        moves[1 + 2 * i].wait()
        moves[2 + 2 * i].wait()
        for b in range(group):
            rows, weights = [], []
            for t in range(per):
                slot = src[(first + b) * per + t]
                live = lax.rem(slot, 2) < counts[lax.div(slot, 2)]
                rows.append(arrived[slot])
                weights.append(tiles[i, b, t] * jnp.where(live, 1.0, 0.0).astype(BF16))
            total = dot(jnp.concatenate(weights, 1), jnp.concatenate(rows, 0), NN)
            at = pl.ds(b * BLK, BLK)
            out[at, :] = (own[i, at, :].astype(F32) + total).astype(BF16)


def aggregate(src, counts, me, arrived, tiles, features, chunk, nfeat, which):
    nblocks, per = tiles.shape[:2]
    group = nblocks // nfeat
    piece = jax.ShapeDtypeStruct((group * BLK, BLK), BF16)
    hbm = pl.BlockSpec(memory_space=pltpu.HBM)
    return pl.pallas_call(
        functools.partial(agg_kernel, which, chunk, nfeat),
        grid_spec=pltpu.PrefetchScalarGridSpec(
            num_scalar_prefetch=3,
            grid=(),
            in_specs=[pl.BlockSpec(memory_space=pl.ANY), hbm, hbm],
            out_specs=[pl.BlockSpec(memory_space=pltpu.VMEM)] * len(which),
            scratch_shapes=[
                pltpu.VMEM(arrived.shape, BF16),
                pltpu.VMEM((len(which), group, per, BLK, BLK), BF16),
                pltpu.VMEM((len(which), group * BLK, BLK), BF16),
                pltpu.SemaphoreType.DMA((1 + 2 * len(which),)),
            ],
        ),
        out_shape=[piece] * len(which),
        compiler_params=params(14),
        cost_estimate=cost(len(which) * group * per * 2 * BLK**3, 8 * MIB),
        name="aggregate",
    )(src, counts, me, arrived, in_hbm(tiles), in_hbm(features))


def dense_kernel(nfeat, *refs):
    pieces, (weights, bias, second, hidden, proj) = refs[: 2 * nfeat], refs[2 * nfeat :]
    order = [pieces[i * nfeat + k][...] for k in range(nfeat) for i in range(2)]
    pre = dot(weights[...], jnp.concatenate(order, 1), NT)
    hid = jnp.maximum(pre + bias[...], 0.0).astype(BF16)
    hidden[...] = hid
    out = dot(second[...], hid, NN)
    for b in range(proj.shape[0]):
        proj[b] = out[:, b * BLK : (b + 1) * BLK]


def dense(pieces, weights, bias, second):
    nodes, nfeat = pieces[0].shape[0], len(pieces) // 2
    hid, width = weights.shape
    grades = second.shape[0]
    step = 512
    return pl.pallas_call(
        functools.partial(dense_kernel, nfeat),
        grid=(nodes // step,),
        in_specs=[pl.BlockSpec((step, BLK), lambda g: (g, 0))] * (2 * nfeat)
        + [
            pl.BlockSpec((hid, width), lambda g: (0, 0)),
            pl.BlockSpec((hid, 1), lambda g: (0, 0)),
            pl.BlockSpec((grades, hid), lambda g: (0, 0)),
        ],
        out_specs=[
            pl.BlockSpec((hid, step), lambda g: (0, g)),
            pl.BlockSpec((step // BLK, grades, BLK), lambda g: (g, 0, 0)),
        ],
        out_shape=[
            jax.ShapeDtypeStruct((hid, nodes), BF16),
            jax.ShapeDtypeStruct((nodes // BLK, grades, BLK), F32),
        ],
        compiler_params=params(20),
        cost_estimate=cost(2 * nodes * hid * width, 7 * MIB),
        name="dense",
    )(*pieces, weights, bias, second)


def spread_kernel(table, me, p0, p1, p2, p3, whole, out):
    nfeat, group = 4, p0.shape[0]
    for k, piece in enumerate((p0, p1, p2, p3)):
        owner = lax.rem(me[0] + nfeat - k, nfeat)
        whole[pl.ds(owner * group, group)] = piece[...]

    @pl.loop(0, out.shape[0], unroll=8)
    def _(k):
        out[k] = whole[table[k]]


def spread(table, me, pieces):
    group, grades, _ = pieces[0].shape
    slots = table.shape[0]
    vmem = pl.BlockSpec(memory_space=pltpu.VMEM)
    return pl.pallas_call(
        spread_kernel,
        grid_spec=pltpu.PrefetchScalarGridSpec(
            num_scalar_prefetch=2,
            grid=(),
            in_specs=[vmem] * 4,
            out_specs=[vmem] * 2,
        ),
        out_shape=[
            jax.ShapeDtypeStruct((group * 4, grades, BLK), F32),
            jax.ShapeDtypeStruct((slots, grades, BLK), F32),
        ],
        compiler_params=params(4),
        cost_estimate=cost(0, MIB),
        name="spread",
    )(table, me, *pieces)


def logits_kernel(
    scale, src, counts, me, arrived, own, labels, tiles, dlog_out, slots_out, parts, field, grad_b, sums
):
    nblocks, per = tiles.shape[:2]
    nslots, grades, _ = arrived.shape
    mine = dlog_out.shape[0]

    def live_of(slot):
        return jnp.where(lax.rem(slot, 2) < counts[lax.div(slot, 2)], 1.0, 0.0)

    x = arrived[...]
    for i in range(3):
        y = x.astype(BF16)
        parts[:, i * grades : (i + 1) * grades, :] = y
        x = x - y.astype(F32)

    @pl.loop(0, nblocks, unroll=8)
    def _(b):
        rows, weights = [], []
        for t in range(per):
            slot = src[b * per + t]
            rows.append(parts[slot] * live_of(slot).astype(BF16))
            weights.append(tiles[b, t])
        triple = dot(jnp.concatenate(rows, 1), jnp.concatenate(weights, 1), NT)
        field[b] = own[b] + (
            triple[:grades] + (triple[grades : 2 * grades] + triple[2 * grades :])
        )

    expo = jnp.exp(field[...])
    probs = expo / jnp.sum(expo, axis=1, keepdims=True)
    grade = lax.broadcasted_iota(jnp.int32, field.shape, 1)
    onehot = jnp.where(labels[...] == grade, 1.0, 0.0)
    dlog = (probs - onehot) * scale
    field[...] = dlog
    grad_b[...] = dlog.astype(BF16)
    dlog_out[...] = field[pl.ds(me[0] * mine, mine)]
    sums[...] = jnp.zeros_like(sums)

    @pl.loop(0, nblocks, unroll=8)
    def _(b):
        back = dot(grad_b[b], jnp.concatenate([tiles[b, t] for t in range(per)], 1), NN)
        for t in range(per):
            slot = src[b * per + t]
            sums[slot] += back[:, t * BLK : (t + 1) * BLK] * live_of(slot)

    slots_out[...] = sums[...].astype(BF16)


def logits_back(src, counts, me, arrived, own, labels, tiles, scale, nfeat):
    nblocks, per = tiles.shape[:2]
    nslots, grades, _ = arrived.shape
    vmem = pl.BlockSpec(memory_space=pltpu.VMEM)
    return pl.pallas_call(
        functools.partial(logits_kernel, scale),
        grid_spec=pltpu.PrefetchScalarGridSpec(
            num_scalar_prefetch=3,
            grid=(),
            in_specs=[vmem] * 4,
            out_specs=[vmem] * 2,
            scratch_shapes=[
                pltpu.VMEM((nslots, 3 * grades, BLK), BF16),
                pltpu.VMEM((nblocks, grades, BLK), F32),
                pltpu.VMEM((nblocks, grades, BLK), BF16),
                pltpu.VMEM(arrived.shape, F32),
            ],
        ),
        out_shape=[
            jax.ShapeDtypeStruct((nblocks // nfeat, grades, BLK), F32),
            jax.ShapeDtypeStruct(arrived.shape, BF16),
        ],
        compiler_params=params(8),
        cost_estimate=cost(nblocks * per * 2 * 64 * BLK**2, 6 * MIB),
        name="logits",
    )(src, counts, me, arrived, own, labels, tiles)


def small_kernel(table, me, returned, dlog, hidden, second, dpre_out, *refs):
    small, (total, dproj, buf) = refs[:-3], refs[-3:]
    group, grades, _ = dlog.shape
    g = pl.program_id(0)
    width = hidden.shape[0]

    @pl.when(g == 0)
    def _():
        total[pl.ds(0, group)] = dlog[...]

        @pl.loop(0, returned.shape[0], unroll=8)
        def _(k):
            at = table[k] - me[0] * group
            at = jnp.where((at >= 0) & (at < group), at, group)
            total[at] += returned[k].astype(F32)

        for b in range(group):
            dproj[:, b * BLK : (b + 1) * BLK] = total[b].astype(BF16)

    active = hidden[...]
    dproj_b = dproj[...]
    dpre = jnp.where(active > 0, dot(second[...], dproj_b, NN), 0.0)
    dpre_out[...] = dpre.astype(BF16)
    buf[pl.ds(0, grades), :] = dot(dproj_b, active, NT)
    part = dpre[:, :BLK]
    for i in range(1, dpre.shape[1] // BLK):
        part += dpre[:, i * BLK : (i + 1) * BLK]
    buf[pl.ds(grades, 8), :] = jnp.broadcast_to(
        jnp.sum(part.T, axis=0, keepdims=True), (8, width)
    )
    for k, out in enumerate(small):

        @pl.when(g == k)
        def _():
            out[...] = buf[...]


def small_gradients(table, me, returned, dlog, hidden, second, nfeat):
    hid, nodes = hidden.shape
    group, grades, _ = dlog.shape
    width = hid // nfeat
    turn = lambda g, m: lax.rem(m[0] + nfeat - g, nfeat)
    whole3 = lambda g, t, m: (0, 0, 0)
    small = jax.ShapeDtypeStruct((grades + 8, width), F32)
    return pl.pallas_call(
        small_kernel,
        grid_spec=pltpu.PrefetchScalarGridSpec(
            num_scalar_prefetch=2,
            grid=(nfeat,),
            in_specs=[
                pl.BlockSpec(returned.shape, whole3),
                pl.BlockSpec(dlog.shape, whole3),
                pl.BlockSpec((width, nodes), lambda g, t, m: (turn(g, m), 0)),
                pl.BlockSpec((width, grades), lambda g, t, m: (turn(g, m), 0)),
            ],
            out_specs=[pl.BlockSpec((width, nodes), lambda g, t, m: (turn(g, m), 0))]
            + [pl.BlockSpec(small.shape, lambda g, t, m: (0, 0))] * nfeat,
            scratch_shapes=[
                pltpu.VMEM((group + 1, grades, BLK), F32),
                pltpu.VMEM((grades, nodes), BF16),
                pltpu.VMEM(small.shape, F32),
            ],
        ),
        out_shape=[pltpu.HBM((hid, nodes), BF16)] + [small] * nfeat,
        compiler_params=params(16),
        cost_estimate=cost(2 * nodes * hid * 256, 4 * MIB),
        name="small_gradients",
    )(table, me, returned, dlog, hidden, second)


def big_kernel(me, side, dpre, *refs):
    pieces, out = refs[:-1], refs[-1]
    nfeat = len(pieces) // 2
    rows = dpre[...].reshape(-1, dpre.shape[-1])
    for k in range(nfeat):
        owner = lax.rem(me[0] + nfeat - k, nfeat)
        both = jnp.concatenate([pieces[k][...], pieces[nfeat + k][...]], 1)
        grad = dot(rows, both, NN).astype(BF16)
        out[:, owner] = grad.reshape(out.shape[0], out.shape[2], out.shape[3])


def big_gradient(me, side, dpre, pieces, parts):
    nfeat = len(pieces) // 2
    hid, nodes = dpre.shape
    cols = hid // parts
    vmem = pl.BlockSpec(memory_space=pltpu.VMEM)
    return pl.pallas_call(
        big_kernel,
        grid_spec=pltpu.PrefetchScalarGridSpec(
            num_scalar_prefetch=2,
            grid=(1,),
            in_specs=[
                pl.BlockSpec((parts // 2, 1, cols, nodes), lambda g, m, s: (0, s[0], 0, 0))
            ]
            + [vmem] * (2 * nfeat),
            out_specs=pl.BlockSpec(
                (parts // 2, nfeat, cols, 2 * BLK), lambda g, m, s: (0, 0, 0, 0)
            ),
        ),
        out_shape=jax.ShapeDtypeStruct((parts // 2, nfeat, cols, 2 * BLK), BF16),
        compiler_params=params(16),
        cost_estimate=cost(nodes * hid * hid, 4 * MIB),
        name="big_gradient",
    )(me, side, in_hbm(dpre.reshape(parts // 2, 2, cols, nodes)), *pieces)


def join_kernel(a, b, out):
    out[...] = (a[...].astype(F32) + b[...].astype(F32)).astype(BF16)


def join(a, b):
    lead = a.shape[0] // 4
    spec = pl.BlockSpec((lead, *a.shape[1:]), lambda g: (g, 0, 0, 0))
    return pl.pallas_call(
        join_kernel,
        grid=(4,),
        in_specs=[spec, spec],
        out_specs=spec,
        out_shape=pltpu.HBM(a.shape, BF16),
        compiler_params=params(8),
        cost_estimate=cost(a.size, 3 * MIB),
        name="join",
    )(a, b)


def total_kernel(nsmall, arrived, *refs):
    small, (out, second, bias, acc) = refs[:nsmall], refs[nsmall:]
    g = pl.program_id(0)

    @pl.when(g == 0)
    def _():
        acc[...] = jnp.zeros_like(acc)
        whole = tree([ref[...] for ref in small])
        grades = second.shape[0]
        second[...] = whole[:grades]
        bias[...] = whole[grades : grades + 1]

    total = arrived[0].astype(F32)
    for i in range(1, arrived.shape[0]):
        total += arrived[i].astype(F32)
    acc[...] += total

    @pl.when(g == pl.num_programs(0) - 1)
    def _():
        out[...] = acc[...]


def total(arrived, small, grades):
    n, cols, rows = arrived.shape
    step = n // 8
    whole = lambda g: (0, 0)
    return pl.pallas_call(
        functools.partial(total_kernel, len(small)),
        grid=(n // step,),
        in_specs=[pl.BlockSpec((step, cols, rows), lambda g: (g, 0, 0))]
        + [pl.BlockSpec(small[0].shape, whole)] * len(small),
        out_specs=[
            pl.BlockSpec((cols, rows), whole),
            pl.BlockSpec((grades, rows), whole),
            pl.BlockSpec((1, rows), whole),
        ],
        out_shape=[
            jax.ShapeDtypeStruct((cols, rows), F32),
            jax.ShapeDtypeStruct((grades, rows), F32),
            jax.ShapeDtypeStruct((1, rows), F32),
        ],
        scratch_shapes=[pltpu.VMEM((cols, rows), F32)],
        compiler_params=params(8),
        cost_estimate=cost(0, 2 * MIB),
        name="total",
    )(arrived, *small)


def shards(features, pair_count, send_blocks, tile_src, tiles, labels, w_first, b_first, w_second):
    nblocks = tile_src.shape[0]
    parts = lax.axis_size("nodes")
    nfeat = lax.axis_size("feat")
    slots = send_blocks.shape[2]
    grades = w_second.shape[1]
    hid = w_first.shape[1]
    axis = lax.axis_index("feat").astype(jnp.int32)
    me = axis.reshape(1)
    table = send_blocks.reshape(parts * slots)
    src = tile_src.reshape(-1)
    counts = pair_count.reshape(-1)

    def ahead(x, k):
        return lax.ppermute(x, "feat", [(i, (i + k) % nfeat) for i in range(nfeat)])

    def nearby(x, masks):
        return [x] + [
            lax.ppermute(x, "nodes", [(i, i ^ mask) for i in range(parts)]) for mask in masks
        ]

    def swap(x):
        shaped = x.reshape(parts, slots, *x.shape[1:])
        moved = lax.all_to_all(shaped, "nodes", split_axis=0, concat_axis=0, tiled=True)
        return moved.reshape(x.shape)

    arrived = [swap(pick(features, table, 0))]
    send = pick(features, table, 1)

    flat = w_first.T
    weights = [ahead(flat, k) for k in (2, 1, 3)]
    consts = jnp.concatenate(
        [w_second.T.astype(F32), jnp.broadcast_to(b_first[None], (8, b_first.shape[0]))], 0
    )
    send, weights, arrived = lax.optimization_barrier((send, weights, arrived))
    arrived.append(swap(send))
    others = (2, 1, 3)
    make = functools.partial(aggregate, src, counts, me)
    first = [None] * nfeat
    *sent, first[0] = make(arrived[0], tiles, features, 0, nfeat, others + (0,))
    consts, weights, first[0] = lax.optimization_barrier((consts, weights, first[0]))
    weights = jnp.concatenate([flat, weights[1], weights[0], weights[2]], 1)
    turned = [consts] + [ahead(consts, k) for k in range(1, nfeat)]
    ring = jnp.stack([turned[k] for k in (3, 2, 1, 0, 3, 2, 1)])
    ordered = lax.dynamic_slice_in_dim(ring, nfeat - 1 - axis, nfeat, 0)
    second_t = ordered[:, :grades].transpose(1, 0, 2).reshape(grades, hid).astype(BF16)
    bias = ordered[:, grades].reshape(hid, 1)
    second = second_t.T
    for k, piece in zip(others, sent):
        first[k] = ahead(piece, k)
    last = [None] * nfeat
    for k, piece in zip(others, make(arrived[1], tiles, features, 1, nfeat, others)):
        last[k] = ahead(piece, k)
    (last[0],) = make(arrived[1], tiles, features, 1, nfeat, (0,))
    hidden, proj = dense(first + last, weights, bias, second_t)

    projs = [proj] + [ahead(proj, k) for k in range(1, nfeat)]
    own, send = spread(table, me, projs)
    scale = 1.0 / math.sqrt(nblocks * BLK * parts)
    dlog, slotsum = logits_back(
        src, counts, me, swap(send), own, labels.reshape(nblocks, 1, BLK), tiles, scale, nfeat
    )
    dpre, *small = small_gradients(table, me, swap(slotsum), dlog, hidden, second, nfeat)
    rest = small[0]
    for k in range(1, nfeat):
        rest = rest + ahead(small[k], nfeat - k)
    rest = nearby(rest, (1, 2, 3))
    core = (lax.axis_index("nodes").astype(jnp.int32) % 2).reshape(1)
    (away,) = nearby(big_gradient(me, 1 - core, dpre, first + last, parts), (1,))[1:]
    big = join(big_gradient(me, core, dpre, first + last, parts), away)
    big, rest = lax.optimization_barrier((big, tree(rest)))
    moved = lax.all_to_all(
        big.reshape(parts // 2 * nfeat, *big.shape[2:]),
        ("nodes", "feat"),
        split_axis=0,
        concat_axis=0,
        axis_index_groups=[
            [p * nfeat + f for p in range(c, parts, 2) for f in range(nfeat)] for c in range(2)
        ],
        tiled=True,
    )
    terms = nearby(rest, range(4, parts, 4))
    grad_first, grad_second, grad_bias = total(moved, terms, grades)
    return grad_first.T, grad_bias.reshape(-1), grad_second.T


def solution(mesh):
    placed = (
        P("nodes", "feat"),
        P("nodes", None),
        P("nodes", None, None),
        P("nodes", None),
        P("nodes", None, None, None),
        P("nodes"),
        P("feat", None),
        P("feat"),
        P("feat", None),
    )
    return jax.shard_map(
        shards,
        mesh=mesh,
        in_specs=placed,
        out_specs=(P("feat", "nodes"), P("feat"), P("feat", None)),
        check_vma=False,
    )
```

```python
import functools
import math

import jax
import jax.numpy as jnp
from jax import lax
from jax.experimental import pallas as pl
from jax.experimental.pallas import tpu as pltpu
from jax.sharding import PartitionSpec as P

F32 = jnp.float32
BF16 = jnp.bfloat16
NT = (((1,), (1,)), ((), ()))
NN = (((1,), (0,)), ((), ()))
BLK = 128
ORDER = (0, 2, 1, 3)
MIB = 1 << 20


def params(mib):
    return pltpu.CompilerParams(vmem_limit_bytes=mib * MIB)


def cost(flops, nbytes):
    return pl.CostEstimate(flops=flops, bytes_accessed=nbytes, transcendentals=0)


def dot(a, b, dims):
    return lax.dot_general(a, b, dims, preferred_element_type=F32)


def in_hbm(x):
    return pltpu.with_memory_space_constraint(x, pltpu.HBM)


def pick_kernel(chunk, table, features, out, held, sems):
    slots = out.shape[0]
    load = pltpu.make_async_copy(features.at[:, pl.ds(chunk * BLK, BLK)], held, sems.at[0])
    load.start()
    load.wait()

    @pl.loop(0, slots, unroll=8)
    def _(k):
        rows = pl.ds(pl.multiple_of(table[k] * BLK, BLK), BLK)
        pltpu.make_async_copy(held.at[rows], out.at[k], sems.at[1]).start()

    pltpu.make_async_copy(out, out, sems.at[1]).wait()


def pick(features, table, chunk):
    slots = table.shape[0]
    return pl.pallas_call(
        functools.partial(pick_kernel, chunk),
        grid_spec=pltpu.PrefetchScalarGridSpec(
            num_scalar_prefetch=1,
            grid=(),
            in_specs=[pl.BlockSpec(memory_space=pltpu.HBM)],
            out_specs=pl.BlockSpec(memory_space=pltpu.HBM),
            scratch_shapes=[
                pltpu.VMEM((features.shape[0], BLK), BF16),
                pltpu.SemaphoreType.DMA((2,)),
            ],
        ),
        out_shape=pltpu.HBM((slots, BLK, BLK), BF16),
        compiler_params=params(63),
        cost_estimate=cost(0, 4 * MIB),
        name="pick",
    )(table, in_hbm(features))


def agg_kernel(which, chunk, nfeat, src, counts, me, arrived_hbm, tiles_hbm, features, *refs):
    outs, (arrived, tiles, own, sems) = refs[: len(which)], refs[len(which) :]
    group, per = tiles.shape[1:3]
    moves = [pltpu.make_async_copy(arrived_hbm, arrived, sems.at[0])]
    firsts = [lax.rem(me[0] + k, nfeat) * group for k in which]
    for i, first in enumerate(firsts):
        rows = pl.ds(pl.multiple_of(first * BLK, BLK), group * BLK)
        moves.append(
            pltpu.make_async_copy(tiles_hbm.at[pl.ds(first, group)], tiles.at[i], sems.at[1 + 2 * i])
        )
        moves.append(
            pltpu.make_async_copy(
                features.at[rows, pl.ds(chunk * BLK, BLK)], own.at[i], sems.at[2 + 2 * i]
            )
        )
    for move in moves:
        move.start()
    moves[0].wait()
    for i, (first, out) in enumerate(zip(firsts, outs)):
        moves[1 + 2 * i].wait()
        moves[2 + 2 * i].wait()
        for b in range(group):
            rows, weights = [], []
            for t in range(per):
                slot = src[(first + b) * per + t]
                live = lax.rem(slot, 2) < counts[lax.div(slot, 2)]
                rows.append(arrived[slot])
                weights.append(tiles[i, b, t] * jnp.where(live, 1.0, 0.0).astype(BF16))
            total = dot(jnp.concatenate(weights, 1), jnp.concatenate(rows, 0), NN)
            at = pl.ds(b * BLK, BLK)
            out[at, :] = (own[i, at, :].astype(F32) + total).astype(BF16)


def aggregate(src, counts, me, arrived, tiles, features, chunk, nfeat, which):
    nblocks, per = tiles.shape[:2]
    group = nblocks // nfeat
    piece = jax.ShapeDtypeStruct((group * BLK, BLK), BF16)
    hbm = pl.BlockSpec(memory_space=pltpu.HBM)
    return pl.pallas_call(
        functools.partial(agg_kernel, which, chunk, nfeat),
        grid_spec=pltpu.PrefetchScalarGridSpec(
            num_scalar_prefetch=3,
            grid=(),
            in_specs=[pl.BlockSpec(memory_space=pl.ANY), hbm, hbm],
            out_specs=[pl.BlockSpec(memory_space=pltpu.VMEM)] * len(which),
            scratch_shapes=[
                pltpu.VMEM(arrived.shape, BF16),
                pltpu.VMEM((len(which), group, per, BLK, BLK), BF16),
                pltpu.VMEM((len(which), group * BLK, BLK), BF16),
                pltpu.SemaphoreType.DMA((1 + 2 * len(which),)),
            ],
        ),
        out_shape=[piece] * len(which),
        compiler_params=params(14),
        cost_estimate=cost(len(which) * group * per * 2 * BLK**3, 8 * MIB),
        name="aggregate",
    )(src, counts, me, arrived, in_hbm(tiles), in_hbm(features))


def dense_kernel(nfeat, *refs):
    pieces, (weights, bias, second, hidden, proj) = refs[: 2 * nfeat], refs[2 * nfeat :]
    order = [pieces[i * nfeat + k][...] for k in range(nfeat) for i in range(2)]
    pre = dot(weights[...], jnp.concatenate(order, 1), NT)
    hid = jnp.maximum(pre + bias[...], 0.0).astype(BF16)
    hidden[...] = hid
    out = dot(second[...], hid, NN)
    for b in range(proj.shape[0]):
        proj[b] = out[:, b * BLK : (b + 1) * BLK]


def dense(pieces, weights, bias, second):
    nodes, nfeat = pieces[0].shape[0], len(pieces) // 2
    hid, width = weights.shape
    grades = second.shape[0]
    step = 512
    return pl.pallas_call(
        functools.partial(dense_kernel, nfeat),
        grid=(nodes // step,),
        in_specs=[pl.BlockSpec((step, BLK), lambda g: (g, 0))] * (2 * nfeat)
        + [
            pl.BlockSpec((hid, width), lambda g: (0, 0)),
            pl.BlockSpec((hid, 1), lambda g: (0, 0)),
            pl.BlockSpec((grades, hid), lambda g: (0, 0)),
        ],
        out_specs=[
            pl.BlockSpec((hid, step), lambda g: (0, g)),
            pl.BlockSpec((step // BLK, grades, BLK), lambda g: (g, 0, 0)),
        ],
        out_shape=[
            jax.ShapeDtypeStruct((hid, nodes), BF16),
            jax.ShapeDtypeStruct((nodes // BLK, grades, BLK), F32),
        ],
        compiler_params=params(20),
        cost_estimate=cost(2 * nodes * hid * width, 7 * MIB),
        name="dense",
    )(*pieces, weights, bias, second)


def spread_kernel(table, me, p0, p1, p2, p3, whole, out):
    nfeat, group = 4, p0.shape[0]
    for k, piece in enumerate((p0, p1, p2, p3)):
        owner = lax.rem(me[0] + nfeat - k, nfeat)
        whole[pl.ds(owner * group, group)] = piece[...]

    @pl.loop(0, out.shape[0], unroll=8)
    def _(k):
        out[k] = whole[table[k]]


def spread(table, me, pieces):
    group, grades, _ = pieces[0].shape
    slots = table.shape[0]
    vmem = pl.BlockSpec(memory_space=pltpu.VMEM)
    return pl.pallas_call(
        spread_kernel,
        grid_spec=pltpu.PrefetchScalarGridSpec(
            num_scalar_prefetch=2,
            grid=(),
            in_specs=[vmem] * 4,
            out_specs=[vmem] * 2,
        ),
        out_shape=[
            jax.ShapeDtypeStruct((group * 4, grades, BLK), F32),
            jax.ShapeDtypeStruct((slots, grades, BLK), F32),
        ],
        compiler_params=params(4),
        cost_estimate=cost(0, MIB),
        name="spread",
    )(table, me, *pieces)


def logits_kernel(
    scale, src, counts, me, arrived, own, labels, tiles, dlog_out, slots_out, parts, field, grad_b, sums
):
    nblocks, per = tiles.shape[:2]
    nslots, grades, _ = arrived.shape
    mine = dlog_out.shape[0]

    def live_of(slot):
        return jnp.where(lax.rem(slot, 2) < counts[lax.div(slot, 2)], 1.0, 0.0)

    x = arrived[...]
    for i in range(3):
        y = x.astype(BF16)
        parts[:, i * grades : (i + 1) * grades, :] = y
        x = x - y.astype(F32)

    @pl.loop(0, nblocks, unroll=8)
    def _(b):
        rows, weights = [], []
        for t in range(per):
            slot = src[b * per + t]
            rows.append(parts[slot] * live_of(slot).astype(BF16))
            weights.append(tiles[b, t])
        triple = dot(jnp.concatenate(rows, 1), jnp.concatenate(weights, 1), NT)
        field[b] = own[b] + (
            triple[:grades] + (triple[grades : 2 * grades] + triple[2 * grades :])
        )

    expo = jnp.exp(field[...])
    probs = expo / jnp.sum(expo, axis=1, keepdims=True)
    grade = lax.broadcasted_iota(jnp.int32, field.shape, 1)
    onehot = jnp.where(labels[...] == grade, 1.0, 0.0)
    dlog = (probs - onehot) * scale
    field[...] = dlog
    grad_b[...] = dlog.astype(BF16)
    dlog_out[...] = field[pl.ds(me[0] * mine, mine)]
    sums[...] = jnp.zeros_like(sums)

    @pl.loop(0, nblocks, unroll=8)
    def _(b):
        back = dot(grad_b[b], jnp.concatenate([tiles[b, t] for t in range(per)], 1), NN)
        for t in range(per):
            slot = src[b * per + t]
            sums[slot] += back[:, t * BLK : (t + 1) * BLK] * live_of(slot)

    slots_out[...] = sums[...].astype(BF16)


def logits_back(src, counts, me, arrived, own, labels, tiles, scale, nfeat):
    nblocks, per = tiles.shape[:2]
    nslots, grades, _ = arrived.shape
    vmem = pl.BlockSpec(memory_space=pltpu.VMEM)
    return pl.pallas_call(
        functools.partial(logits_kernel, scale),
        grid_spec=pltpu.PrefetchScalarGridSpec(
            num_scalar_prefetch=3,
            grid=(),
            in_specs=[vmem] * 4,
            out_specs=[vmem] * 2,
            scratch_shapes=[
                pltpu.VMEM((nslots, 3 * grades, BLK), BF16),
                pltpu.VMEM((nblocks, grades, BLK), F32),
                pltpu.VMEM((nblocks, grades, BLK), BF16),
                pltpu.VMEM(arrived.shape, F32),
            ],
        ),
        out_shape=[
            jax.ShapeDtypeStruct((nblocks // nfeat, grades, BLK), F32),
            jax.ShapeDtypeStruct(arrived.shape, BF16),
        ],
        compiler_params=params(8),
        cost_estimate=cost(nblocks * per * 2 * 64 * BLK**2, 6 * MIB),
        name="logits",
    )(src, counts, me, arrived, own, labels, tiles)


def small_kernel(table, me, returned, dlog, hidden, second, dpre_out, small, total, dproj):
    group, grades, _ = dlog.shape
    width = hidden.shape[0]

    @pl.when(pl.program_id(0) == 0)
    def _():
        total[pl.ds(0, group)] = dlog[...]

        @pl.loop(0, returned.shape[0], unroll=8)
        def _(k):
            at = table[k] - me[0] * group
            at = jnp.where((at >= 0) & (at < group), at, group)
            total[at] += returned[k].astype(F32)

        for b in range(group):
            dproj[:, b * BLK : (b + 1) * BLK] = total[b].astype(BF16)

    active = hidden[...]
    dproj_b = dproj[...]
    dpre = jnp.where(active > 0, dot(second[...], dproj_b, NN), 0.0)
    dpre_out[...] = dpre.astype(BF16)
    small[pl.ds(0, grades), :] = dot(dproj_b, active, NT)
    part = dpre[:, :BLK]
    for i in range(1, dpre.shape[1] // BLK):
        part += dpre[:, i * BLK : (i + 1) * BLK]
    small[pl.ds(grades, 8), :] = jnp.broadcast_to(
        jnp.sum(part.T, axis=0, keepdims=True), (8, width)
    )


def small_gradients(table, me, returned, dlog, hidden, second, nfeat):
    hid, nodes = hidden.shape
    group, grades, _ = dlog.shape
    width = hid // nfeat
    whole3 = lambda g, t, m: (0, 0, 0)
    return pl.pallas_call(
        small_kernel,
        grid_spec=pltpu.PrefetchScalarGridSpec(
            num_scalar_prefetch=2,
            grid=(nfeat,),
            in_specs=[
                pl.BlockSpec(returned.shape, whole3),
                pl.BlockSpec(dlog.shape, whole3),
                pl.BlockSpec((width, nodes), lambda g, t, m: (g, 0)),
                pl.BlockSpec((width, grades), lambda g, t, m: (g, 0)),
            ],
            out_specs=[
                pl.BlockSpec((width, nodes), lambda g, t, m: (g, 0)),
                pl.BlockSpec((grades + 8, width), lambda g, t, m: (0, g)),
            ],
            scratch_shapes=[
                pltpu.VMEM((group + 1, grades, BLK), F32),
                pltpu.VMEM((grades, nodes), BF16),
            ],
        ),
        out_shape=[
            pltpu.HBM((hid, nodes), BF16),
            jax.ShapeDtypeStruct((grades + 8, hid), F32),
        ],
        compiler_params=params(16),
        cost_estimate=cost(2 * nodes * hid * 256, 4 * MIB),
        name="small_gradients",
    )(table, me, returned, dlog, hidden, second)


def big_kernel(me, side, dpre, *refs):
    pieces, out = refs[:-1], refs[-1]
    nfeat = len(pieces) // 2
    rows = dpre[...].reshape(-1, dpre.shape[-1])
    for i, k in enumerate(ORDER):
        owner = lax.rem(me[0] + nfeat - k, nfeat)
        both = jnp.concatenate([pieces[i][...], pieces[nfeat + i][...]], 1)
        grad = dot(rows, both, NN).astype(BF16)
        out[:, owner] = grad.reshape(out.shape[0], out.shape[2], out.shape[3])


def big_gradient(me, side, dpre, pieces, parts):
    nfeat = len(pieces) // 2
    hid, nodes = dpre.shape
    cols = hid // parts
    vmem = pl.BlockSpec(memory_space=pltpu.VMEM)
    return pl.pallas_call(
        big_kernel,
        grid_spec=pltpu.PrefetchScalarGridSpec(
            num_scalar_prefetch=2,
            grid=(1,),
            in_specs=[
                pl.BlockSpec((parts // 2, 1, cols, nodes), lambda g, m, s: (0, s[0], 0, 0))
            ]
            + [vmem] * (2 * nfeat),
            out_specs=pl.BlockSpec(
                (parts // 2, nfeat, cols, 2 * BLK), lambda g, m, s: (0, 0, 0, 0)
            ),
        ),
        out_shape=jax.ShapeDtypeStruct((parts // 2, nfeat, cols, 2 * BLK), BF16),
        compiler_params=params(16),
        cost_estimate=cost(nodes * hid * hid, 4 * MIB),
        name="big_gradient",
    )(me, side, in_hbm(dpre.reshape(parts // 2, 2, cols, nodes)), *pieces)


def join_kernel(side, a, b, small, other, out):
    rows, width = a.shape[2:]
    both = small[...] + other[...]
    near = both.astype(BF16)
    rest = both - near.astype(F32)
    kept = jnp.where(side[0] == 0, near.astype(F32), rest)
    for f in range(a.shape[1]):
        share = kept[:, f * width : (f + 1) * width]
        for p in range(a.shape[0]):
            grad = a[p, f].astype(F32) + b[p, f].astype(F32)
            out[p, f] = jnp.concatenate([grad, share], 0).astype(BF16)


def join(side, a, b, small, other):
    steps = 4
    lead, nfeat, rows, width = a.shape
    more = small.shape[0]
    spec = lambda n: pl.BlockSpec((lead // steps, nfeat, n, width), lambda g, s: (g, 0, 0, 0))
    whole = pl.BlockSpec(small.shape, lambda g, s: (0, 0))
    return pl.pallas_call(
        join_kernel,
        grid_spec=pltpu.PrefetchScalarGridSpec(
            num_scalar_prefetch=1,
            grid=(steps,),
            in_specs=[spec(rows), spec(rows), whole, whole],
            out_specs=spec(rows + more),
        ),
        out_shape=pltpu.HBM((lead, nfeat, rows + more, width), BF16),
        compiler_params=params(8),
        cost_estimate=cost(a.size, 4 * MIB),
        name="join",
    )(side, a, b, small, other)


def total_kernel(arrived, out, small, acc):
    g = pl.program_id(0)
    rows = out.shape[0]

    @pl.when(g == 0)
    def _():
        acc[...] = jnp.zeros_like(acc)

    total = arrived[0].astype(F32)
    for i in range(1, arrived.shape[0]):
        total += arrived[i].astype(F32)
    acc[...] += total

    @pl.when(g == pl.num_programs(0) - 1)
    def _():
        out[...] = acc[pl.ds(0, rows), :]
        small[...] = acc[pl.ds(rows, small.shape[0]), :]


def total(arrived, rows):
    n, full, width = arrived.shape
    step = n // 8
    shapes = [(rows, width), (full - rows, width)]
    return pl.pallas_call(
        total_kernel,
        grid=(n // step,),
        in_specs=[pl.BlockSpec((step, full, width), lambda g: (g, 0, 0))],
        out_specs=[pl.BlockSpec(shape, lambda g: (0, 0)) for shape in shapes],
        out_shape=[jax.ShapeDtypeStruct(shape, F32) for shape in shapes],
        scratch_shapes=[pltpu.VMEM((full, width), F32)],
        compiler_params=params(8),
        cost_estimate=cost(0, 2 * MIB),
        name="total",
    )(arrived)


def finish_kernel(a, b, second, bias):
    grades = second.shape[0]
    second[...] = a[pl.ds(0, grades), :] + b[pl.ds(0, grades), :]
    bias[...] = a[pl.ds(grades, 1), :] + b[pl.ds(grades, 1), :]


def finish(a, b, grades):
    vmem = pl.BlockSpec(memory_space=pltpu.VMEM)
    return pl.pallas_call(
        finish_kernel,
        in_specs=[vmem] * 2,
        out_specs=[vmem] * 2,
        out_shape=[
            jax.ShapeDtypeStruct((grades, a.shape[1]), F32),
            jax.ShapeDtypeStruct((1, a.shape[1]), F32),
        ],
        compiler_params=params(2),
        cost_estimate=cost(0, MIB // 8),
        name="finish",
    )(a, b)


def shards(features, pair_count, send_blocks, tile_src, tiles, labels, w_first, b_first, w_second):
    nblocks = tile_src.shape[0]
    parts = lax.axis_size("nodes")
    nfeat = lax.axis_size("feat")
    slots = send_blocks.shape[2]
    grades = w_second.shape[1]
    hid = w_first.shape[1]
    axis = lax.axis_index("feat").astype(jnp.int32)
    me = axis.reshape(1)
    table = send_blocks.reshape(parts * slots)
    src = tile_src.reshape(-1)
    counts = pair_count.reshape(-1)

    def ahead(x, k):
        return lax.ppermute(x, "feat", [(i, (i + k) % nfeat) for i in range(nfeat)])

    def nearby(x):
        return lax.ppermute(x, "nodes", [(i, i ^ 1) for i in range(parts)])

    def swap(x):
        shaped = x.reshape(parts, slots, *x.shape[1:])
        moved = lax.all_to_all(shaped, "nodes", split_axis=0, concat_axis=0, tiled=True)
        return moved.reshape(x.shape)

    arrived = [swap(pick(features, table, 0))]
    send = pick(features, table, 1)

    flat = w_first.T
    weights = [ahead(flat, k) for k in (2, 1, 3)]
    consts = jnp.concatenate(
        [w_second.T.astype(F32), jnp.broadcast_to(b_first[None], (8, b_first.shape[0]))], 0
    )
    send, weights, arrived = lax.optimization_barrier((send, weights, arrived))
    arrived.append(swap(send))
    others = (2, 1, 3)
    make = functools.partial(aggregate, src, counts, me)
    *sent, own = make(arrived[0], tiles, features, 0, nfeat, others + (0,))
    first = [own] + [ahead(piece, k) for k, piece in zip(others, sent)]
    core = (lax.axis_index("nodes").astype(jnp.int32) % 2).reshape(1)
    consts, weights, here, there, first[0] = lax.optimization_barrier(
        (consts, weights, core, 1 - core, first[0])
    )
    weights = jnp.concatenate([flat] + weights, 1)
    turned = [consts] + [ahead(consts, k) for k in range(1, nfeat)]
    ring = jnp.stack([turned[k] for k in (3, 2, 1, 0, 3, 2, 1)])
    ordered = lax.dynamic_slice_in_dim(ring, nfeat - 1 - axis, nfeat, 0)
    second_t = ordered[:, :grades].transpose(1, 0, 2).reshape(grades, hid).astype(BF16)
    bias = ordered[:, grades].reshape(hid, 1)
    second = second_t.T
    sent = make(arrived[1], tiles, features, 1, nfeat, others)
    last = list(make(arrived[1], tiles, features, 1, nfeat, (0,)))
    last += [ahead(piece, k) for k, piece in zip(others, sent)]
    hidden, proj = dense(first + last, weights, bias, second_t)

    projs = [proj] + [ahead(proj, k) for k in range(1, nfeat)]
    own, send = spread(table, me, projs)
    scale = 1.0 / math.sqrt(nblocks * BLK * parts)
    dlog, slotsum = logits_back(
        src, counts, me, swap(send), own, labels.reshape(nblocks, 1, BLK), tiles, scale, nfeat
    )
    dpre, small = small_gradients(table, me, swap(slotsum), dlog, hidden, second, nfeat)
    away = nearby(big_gradient(me, there, dpre, first + last, parts))
    big = big_gradient(me, here, dpre, first + last, parts)
    big = join(here, big, away, small, nearby(small))
    moved = lax.all_to_all(
        big.reshape(parts // 2 * nfeat, *big.shape[2:]),
        ("nodes", "feat"),
        split_axis=0,
        concat_axis=0,
        axis_index_groups=[
            [p * nfeat + f for p in range(c, parts, 2) for f in range(nfeat)] for c in range(2)
        ],
        tiled=True,
    )
    grad_first, rest = total(moved, hid // parts)
    grad_second, grad_bias = finish(rest, nearby(rest), grades)
    return grad_first.T, grad_bias.reshape(-1), grad_second.T


def solution(mesh):
    placed = (
        P("nodes", "feat"),
        P("nodes", None),
        P("nodes", None, None),
        P("nodes", None),
        P("nodes", None, None, None),
        P("nodes"),
        P("feat", None),
        P("feat"),
        P("feat", None),
    )
    return jax.shard_map(
        shards,
        mesh=mesh,
        in_specs=placed,
        out_specs=(P("feat", "nodes"), P("feat"), P("feat", None)),
        check_vma=False,
    )
```

```python
import functools
import math

import jax
import jax.numpy as jnp
from jax import lax
from jax.experimental import pallas as pl
from jax.experimental.pallas import tpu as pltpu
from jax.sharding import PartitionSpec as P

F32 = jnp.float32
BF16 = jnp.bfloat16
NT = (((1,), (1,)), ((), ()))
NN = (((1,), (0,)), ((), ()))
BLK = 128
ORDER = (0, 2, 1, 3)
MIB = 1 << 20


def params(mib):
    return pltpu.CompilerParams(vmem_limit_bytes=mib * MIB)


def cost(flops, nbytes):
    return pl.CostEstimate(flops=flops, bytes_accessed=nbytes, transcendentals=0)


def dot(a, b, dims):
    return lax.dot_general(a, b, dims, preferred_element_type=F32)


def in_hbm(x):
    return pltpu.with_memory_space_constraint(x, pltpu.HBM)


def pick_kernel(chunk, table, features, out, held, sems):
    slots = out.shape[0]
    load = pltpu.make_async_copy(features.at[:, pl.ds(chunk * BLK, BLK)], held, sems.at[0])
    load.start()
    load.wait()

    @pl.loop(0, slots, unroll=8)
    def _(k):
        block = table[0, lax.div(k, 2), lax.rem(k, 2)]
        rows = pl.ds(pl.multiple_of(block * BLK, BLK), BLK)
        pltpu.make_async_copy(held.at[rows], out.at[k], sems.at[1]).start()

    pltpu.make_async_copy(out, out, sems.at[1]).wait()


def pick(features, table, chunk):
    slots = table.size
    return pl.pallas_call(
        functools.partial(pick_kernel, chunk),
        grid_spec=pltpu.PrefetchScalarGridSpec(
            num_scalar_prefetch=1,
            grid=(),
            in_specs=[pl.BlockSpec(memory_space=pltpu.HBM)],
            out_specs=pl.BlockSpec(memory_space=pltpu.HBM),
            scratch_shapes=[
                pltpu.VMEM((features.shape[0], BLK), BF16),
                pltpu.SemaphoreType.DMA((2,)),
            ],
        ),
        out_shape=pltpu.HBM((slots, BLK, BLK), BF16),
        compiler_params=params(63),
        cost_estimate=cost(0, 4 * MIB),
        name="pick",
    )(table, in_hbm(features))


def agg_kernel(which, chunk, nfeat, src, counts, me, arrived, tiles_hbm, features, *refs):
    outs, (tiles, own, sems, *held) = refs[: len(which)], refs[len(which) :]
    group, per = tiles.shape[1:3]
    moves = []
    if held:
        moves.append(pltpu.make_async_copy(arrived, held[0], sems.at[2 * len(which)]))
        arrived = held[0]
    firsts = [lax.rem(me[0] + k, nfeat) * group for k in which]
    pairs = []
    for i, first in enumerate(firsts):
        rows = pl.ds(pl.multiple_of(first * BLK, BLK), group * BLK)
        tiles_move = pltpu.make_async_copy(
            tiles_hbm.at[pl.ds(first, group)], tiles.at[i], sems.at[2 * i]
        )
        own_move = pltpu.make_async_copy(
            features.at[rows, pl.ds(chunk * BLK, BLK)], own.at[i], sems.at[2 * i + 1]
        )
        pairs.append((tiles_move, own_move))
    for move in moves + [move for pair in pairs for move in pair]:
        move.start()
    for move in moves:
        move.wait()
    for i, (first, out) in enumerate(zip(firsts, outs)):
        for move in pairs[i]:
            move.wait()
        for b in range(group):
            rows, weights = [], []
            for t in range(per):
                slot = src[(first + b) * per + t]
                live = lax.rem(slot, 2) < counts[lax.div(slot, 2)]
                rows.append(arrived[slot])
                weights.append(tiles[i, b, t] * jnp.where(live, 1.0, 0.0).astype(BF16))
            total = dot(jnp.concatenate(weights, 1), jnp.concatenate(rows, 0), NN)
            at = pl.ds(b * BLK, BLK)
            out[at, :] = (own[i, at, :].astype(F32) + total).astype(BF16)


def aggregate(src, counts, me, arrived, tiles, features, chunk, nfeat, which):
    nblocks, per = tiles.shape[:2]
    group = nblocks // nfeat
    piece = jax.ShapeDtypeStruct((group * BLK, BLK), BF16)
    hbm = pl.BlockSpec(memory_space=pltpu.HBM)
    vmem = pl.BlockSpec(memory_space=pltpu.VMEM)
    load = chunk == 0
    return pl.pallas_call(
        functools.partial(agg_kernel, which, chunk, nfeat),
        grid_spec=pltpu.PrefetchScalarGridSpec(
            num_scalar_prefetch=3,
            grid=(),
            in_specs=[pl.BlockSpec(memory_space=pl.ANY) if load else vmem, hbm, hbm],
            out_specs=[vmem] * len(which),
            scratch_shapes=[
                pltpu.VMEM((len(which), group, per, BLK, BLK), BF16),
                pltpu.VMEM((len(which), group * BLK, BLK), BF16),
                pltpu.SemaphoreType.DMA((1 + 2 * len(which),)),
            ]
            + [pltpu.VMEM(arrived.shape, BF16)] * load,
        ),
        out_shape=[piece] * len(which),
        compiler_params=params(14),
        cost_estimate=cost(len(which) * group * per * 2 * BLK**3, 8 * MIB),
        name="aggregate",
    )(src, counts, me, arrived, in_hbm(tiles), in_hbm(features))


def dense_kernel(nfeat, *refs):
    pieces, (weights, bias, second, hidden, proj) = refs[: 2 * nfeat], refs[2 * nfeat :]
    order = [pieces[i * nfeat + k][...] for k in range(nfeat) for i in range(2)]
    pre = dot(weights[...], jnp.concatenate(order, 1), NT)
    hid = jnp.maximum(pre + bias[...], 0.0).astype(BF16)
    hidden[...] = hid
    out = dot(second[...], hid, NN)
    for b in range(proj.shape[0]):
        proj[b] = out[:, b * BLK : (b + 1) * BLK]


def dense(pieces, weights, bias, second):
    nodes, nfeat = pieces[0].shape[0], len(pieces) // 2
    hid, width = weights.shape
    grades = second.shape[0]
    step = 512
    return pl.pallas_call(
        functools.partial(dense_kernel, nfeat),
        grid=(nodes // step,),
        in_specs=[pl.BlockSpec((step, BLK), lambda g: (g, 0))] * (2 * nfeat)
        + [
            pl.BlockSpec((hid, width), lambda g: (0, 0)),
            pl.BlockSpec((hid, 1), lambda g: (0, 0)),
            pl.BlockSpec((grades, hid), lambda g: (0, 0)),
        ],
        out_specs=[
            pl.BlockSpec((hid, step), lambda g: (0, g)),
            pl.BlockSpec((step // BLK, grades, BLK), lambda g: (g, 0, 0)),
        ],
        out_shape=[
            jax.ShapeDtypeStruct((hid, nodes), BF16),
            jax.ShapeDtypeStruct((nodes // BLK, grades, BLK), F32),
        ],
        compiler_params=params(20),
        cost_estimate=cost(2 * nodes * hid * width, 7 * MIB),
        name="dense",
    )(*pieces, weights, bias, second)


def spread_kernel(table, me, p0, p1, p2, p3, whole, out):
    nfeat, group = 4, p0.shape[0]
    for k, piece in enumerate((p0, p1, p2, p3)):
        owner = lax.rem(me[0] + nfeat - k, nfeat)
        whole[pl.ds(owner * group, group)] = piece[...]

    @pl.loop(0, out.shape[0], unroll=8)
    def _(k):
        out[k] = whole[table[k]]


def spread(table, me, pieces):
    group, grades, _ = pieces[0].shape
    slots = table.shape[0]
    vmem = pl.BlockSpec(memory_space=pltpu.VMEM)
    return pl.pallas_call(
        spread_kernel,
        grid_spec=pltpu.PrefetchScalarGridSpec(
            num_scalar_prefetch=2,
            grid=(),
            in_specs=[vmem] * 4,
            out_specs=[vmem] * 2,
        ),
        out_shape=[
            jax.ShapeDtypeStruct((group * 4, grades, BLK), F32),
            jax.ShapeDtypeStruct((slots, grades, BLK), F32),
        ],
        compiler_params=params(4),
        cost_estimate=cost(0, MIB),
        name="spread",
    )(table, me, *pieces)


def logits_kernel(
    scale, src, counts, me, arrived, own, labels, tiles, dlog_out, slots_out, parts, field, grad_b, sums
):
    nblocks, per = tiles.shape[:2]
    nslots, grades, _ = arrived.shape
    mine = dlog_out.shape[0]

    def live_of(slot):
        return jnp.where(lax.rem(slot, 2) < counts[lax.div(slot, 2)], 1.0, 0.0)

    x = arrived[...]
    for i in range(3):
        y = x.astype(BF16)
        parts[:, i * grades : (i + 1) * grades, :] = y
        x = x - y.astype(F32)

    @pl.loop(0, nblocks, unroll=8)
    def _(b):
        rows, weights = [], []
        for t in range(per):
            slot = src[b * per + t]
            rows.append(parts[slot] * live_of(slot).astype(BF16))
            weights.append(tiles[b, t])
        triple = dot(jnp.concatenate(rows, 1), jnp.concatenate(weights, 1), NT)
        field[b] = own[b] + (
            triple[:grades] + (triple[grades : 2 * grades] + triple[2 * grades :])
        )

    expo = jnp.exp(field[...])
    probs = expo / jnp.sum(expo, axis=1, keepdims=True)
    grade = lax.broadcasted_iota(jnp.int32, field.shape, 1)
    onehot = jnp.where(labels[...] == grade, 1.0, 0.0)
    dlog = (probs - onehot) * scale
    field[...] = dlog
    grad_b[...] = dlog.astype(BF16)
    dlog_out[...] = field[pl.ds(me[0] * mine, mine)]
    sums[...] = jnp.zeros_like(sums)

    @pl.loop(0, nblocks, unroll=8)
    def _(b):
        back = dot(grad_b[b], jnp.concatenate([tiles[b, t] for t in range(per)], 1), NN)
        for t in range(per):
            slot = src[b * per + t]
            sums[slot] += back[:, t * BLK : (t + 1) * BLK] * live_of(slot)

    slots_out[...] = sums[...].astype(BF16)


def logits_back(src, counts, me, arrived, own, labels, tiles, scale, nfeat):
    nblocks, per = tiles.shape[:2]
    nslots, grades, _ = arrived.shape
    vmem = pl.BlockSpec(memory_space=pltpu.VMEM)
    return pl.pallas_call(
        functools.partial(logits_kernel, scale),
        grid_spec=pltpu.PrefetchScalarGridSpec(
            num_scalar_prefetch=3,
            grid=(),
            in_specs=[vmem] * 4,
            out_specs=[vmem] * 2,
            scratch_shapes=[
                pltpu.VMEM((nslots, 3 * grades, BLK), BF16),
                pltpu.VMEM((nblocks, grades, BLK), F32),
                pltpu.VMEM((nblocks, grades, BLK), BF16),
                pltpu.VMEM(arrived.shape, F32),
            ],
        ),
        out_shape=[
            jax.ShapeDtypeStruct((nblocks // nfeat, grades, BLK), F32),
            jax.ShapeDtypeStruct(arrived.shape, BF16),
        ],
        compiler_params=params(8),
        cost_estimate=cost(nblocks * per * 2 * 64 * BLK**2, 6 * MIB),
        name="logits",
    )(src, counts, me, arrived, own, labels, tiles)


def small_kernel(table, me, returned, dlog, hidden, second, dpre_out, small, total, dproj):
    group, grades, _ = dlog.shape
    width = hidden.shape[0]

    @pl.when(pl.program_id(0) == 0)
    def _():
        total[pl.ds(0, group)] = dlog[...]

        @pl.loop(0, returned.shape[0], unroll=8)
        def _(k):
            at = table[k] - me[0] * group
            at = jnp.where((at >= 0) & (at < group), at, group)
            total[at] += returned[k].astype(F32)

        for b in range(group):
            dproj[:, b * BLK : (b + 1) * BLK] = total[b].astype(BF16)

    active = hidden[...]
    dproj_b = dproj[...]
    dpre = jnp.where(active > 0, dot(second[...], dproj_b, NN), 0.0)
    dpre_out[...] = dpre.astype(BF16)
    small[pl.ds(0, grades), :] = dot(dproj_b, active, NT)
    part = dpre[:, :BLK]
    for i in range(1, dpre.shape[1] // BLK):
        part += dpre[:, i * BLK : (i + 1) * BLK]
    small[pl.ds(grades, 8), :] = jnp.broadcast_to(
        jnp.sum(part.T, axis=0, keepdims=True), (8, width)
    )


def small_gradients(table, me, returned, dlog, hidden, second, nfeat):
    hid, nodes = hidden.shape
    group, grades, _ = dlog.shape
    width = hid // nfeat
    whole3 = lambda g, t, m: (0, 0, 0)
    return pl.pallas_call(
        small_kernel,
        grid_spec=pltpu.PrefetchScalarGridSpec(
            num_scalar_prefetch=2,
            grid=(nfeat,),
            in_specs=[
                pl.BlockSpec(returned.shape, whole3),
                pl.BlockSpec(dlog.shape, whole3),
                pl.BlockSpec((width, nodes), lambda g, t, m: (g, 0)),
                pl.BlockSpec((width, grades), lambda g, t, m: (g, 0)),
            ],
            out_specs=[
                pl.BlockSpec((width, nodes), lambda g, t, m: (g, 0)),
                pl.BlockSpec((grades + 8, width), lambda g, t, m: (0, g)),
            ],
            scratch_shapes=[
                pltpu.VMEM((group + 1, grades, BLK), F32),
                pltpu.VMEM((grades, nodes), BF16),
            ],
        ),
        out_shape=[
            pltpu.HBM((hid, nodes), BF16),
            jax.ShapeDtypeStruct((grades + 8, hid), F32),
        ],
        compiler_params=params(16),
        cost_estimate=cost(2 * nodes * hid * 256, 4 * MIB),
        name="small_gradients",
    )(table, me, returned, dlog, hidden, second)


def big_kernel(me, side, dpre, *refs):
    pieces, out = refs[:-1], refs[-1]
    nfeat = len(pieces) // 2
    rows = dpre[...].reshape(-1, dpre.shape[-1])
    for i, k in enumerate(ORDER):
        owner = lax.rem(me[0] + nfeat - k, nfeat)
        both = jnp.concatenate([pieces[i][...], pieces[nfeat + i][...]], 1)
        grad = dot(rows, both, NN).astype(BF16)
        out[:, owner] = grad.reshape(out.shape[0], out.shape[2], out.shape[3])


def big_gradient(me, side, dpre, pieces, parts):
    nfeat = len(pieces) // 2
    hid, nodes = dpre.shape
    cols = hid // parts
    vmem = pl.BlockSpec(memory_space=pltpu.VMEM)
    return pl.pallas_call(
        big_kernel,
        grid_spec=pltpu.PrefetchScalarGridSpec(
            num_scalar_prefetch=2,
            grid=(1,),
            in_specs=[
                pl.BlockSpec((parts // 2, 1, cols, nodes), lambda g, m, s: (0, s[0], 0, 0))
            ]
            + [vmem] * (2 * nfeat),
            out_specs=pl.BlockSpec(
                (parts // 2, nfeat, cols, 2 * BLK), lambda g, m, s: (0, 0, 0, 0)
            ),
        ),
        out_shape=jax.ShapeDtypeStruct((parts // 2, nfeat, cols, 2 * BLK), BF16),
        compiler_params=params(16),
        cost_estimate=cost(nodes * hid * hid, 4 * MIB),
        name="big_gradient",
    )(me, side, in_hbm(dpre.reshape(parts // 2, 2, cols, nodes)), *pieces)


def join_kernel(side, a, b, small, other, out):
    width = a.shape[3]
    more = out.shape[2] - a.shape[2]
    both = small[...] + other[...]
    near = both.astype(BF16).astype(F32)
    rest = both - near
    second = jnp.concatenate(
        [near[more : more + 1], rest[more : more + 1], rest[: more - 2]], 0
    )
    kept = jnp.where(side[0] == 0, near[:more], second)
    for f in range(a.shape[1]):
        share = kept[:, f * width : (f + 1) * width]
        for p in range(a.shape[0]):
            grad = a[p, f].astype(F32) + b[p, f].astype(F32)
            out[p, f] = jnp.concatenate([grad, share], 0).astype(BF16)


def join(side, a, b, small, other):
    steps = 4
    lead, nfeat, rows, width = a.shape
    more = small.shape[0] - 8
    spec = lambda n: pl.BlockSpec((lead // steps, nfeat, n, width), lambda g, s: (g, 0, 0, 0))
    whole = pl.BlockSpec(small.shape, lambda g, s: (0, 0))
    return pl.pallas_call(
        join_kernel,
        grid_spec=pltpu.PrefetchScalarGridSpec(
            num_scalar_prefetch=1,
            grid=(steps,),
            in_specs=[spec(rows), spec(rows), whole, whole],
            out_specs=spec(rows + more),
        ),
        out_shape=pltpu.HBM((lead, nfeat, rows + more, width), BF16),
        compiler_params=params(8),
        cost_estimate=cost(a.size, 4 * MIB),
        name="join",
    )(side, a, b, small, other)


def total_kernel(arrived, out, small, acc):
    g = pl.program_id(0)
    rows = out.shape[0]

    @pl.when(g == 0)
    def _():
        acc[...] = jnp.zeros_like(acc)

    total = arrived[0].astype(F32)
    for i in range(1, arrived.shape[0]):
        total += arrived[i].astype(F32)
    acc[...] += total

    @pl.when(g == pl.num_programs(0) - 1)
    def _():
        out[...] = acc[pl.ds(0, rows), :]
        small[...] = acc[pl.ds(rows, small.shape[0]), :]


def total(arrived, rows):
    n, full, width = arrived.shape
    step = n // 8
    shapes = [(rows, width), (full - rows, width)]
    return pl.pallas_call(
        total_kernel,
        grid=(n // step,),
        in_specs=[pl.BlockSpec((step, full, width), lambda g: (g, 0, 0))],
        out_specs=[pl.BlockSpec(shape, lambda g: (0, 0)) for shape in shapes],
        out_shape=[jax.ShapeDtypeStruct(shape, F32) for shape in shapes],
        scratch_shapes=[pltpu.VMEM((full, width), F32)],
        compiler_params=params(8),
        cost_estimate=cost(0, 2 * MIB),
        name="total",
    )(arrived)


def finish_kernel(side, a, b, second, bias):
    first = side[0] == 0
    near = jnp.where(first, a[...], b[...])
    rest = jnp.where(first, b[...], a[...])
    second[...] = near + jnp.concatenate([rest[2:], jnp.zeros_like(rest[:2])], 0)
    bias[...] = rest[:1] + rest[1:2]


def finish(side, a, b):
    vmem = pl.BlockSpec(memory_space=pltpu.VMEM)
    return pl.pallas_call(
        finish_kernel,
        grid_spec=pltpu.PrefetchScalarGridSpec(
            num_scalar_prefetch=1,
            grid=(),
            in_specs=[vmem] * 2,
            out_specs=[vmem] * 2,
        ),
        out_shape=[
            jax.ShapeDtypeStruct(a.shape, F32),
            jax.ShapeDtypeStruct((1, a.shape[1]), F32),
        ],
        compiler_params=params(2),
        cost_estimate=cost(0, MIB // 8),
        name="finish",
    )(side, a, b)


def shards(features, pair_count, send_blocks, tile_src, tiles, labels, w_first, b_first, w_second):
    nblocks = tile_src.shape[0]
    parts = lax.axis_size("nodes")
    nfeat = lax.axis_size("feat")
    slots = send_blocks.shape[2]
    grades = w_second.shape[1]
    hid = w_first.shape[1]
    axis = lax.axis_index("feat").astype(jnp.int32)
    me = axis.reshape(1)
    table = send_blocks.reshape(parts * slots)
    src = tile_src.reshape(-1)
    counts = pair_count.reshape(-1)

    def ahead(x, k):
        return lax.ppermute(x, "feat", [(i, (i + k) % nfeat) for i in range(nfeat)])

    def nearby(x):
        return lax.ppermute(x, "nodes", [(i, i ^ 1) for i in range(parts)])

    def swap(x):
        shaped = x.reshape(parts, slots, *x.shape[1:])
        moved = lax.all_to_all(shaped, "nodes", split_axis=0, concat_axis=0, tiled=True)
        return moved.reshape(x.shape)

    arrived = [swap(pick(features, send_blocks, 0))]
    send = pick(features, send_blocks, 1)

    flat = w_first.T
    weights = [ahead(flat, k) for k in (2, 1, 3)]
    consts = jnp.concatenate(
        [w_second.T.astype(F32), jnp.broadcast_to(b_first[None], (8, b_first.shape[0]))], 0
    )
    send, weights, arrived = lax.optimization_barrier((send, weights, arrived))
    arrived.append(swap(send))
    others = (2, 1, 3)
    make = functools.partial(aggregate, src, counts, me)
    *sent, own = make(arrived[0], tiles, features, 0, nfeat, others + (0,))
    first = [own] + [ahead(piece, k) for k, piece in zip(others, sent)]
    core = (lax.axis_index("nodes").astype(jnp.int32) % 2).reshape(1)
    consts, weights, here, there, first[0] = lax.optimization_barrier(
        (consts, weights, core, 1 - core, first[0])
    )
    weights = jnp.concatenate([flat] + weights, 1)
    turned = [consts] + [ahead(consts, k) for k in range(1, nfeat)]
    ring = jnp.stack([turned[k] for k in (3, 2, 1, 0, 3, 2, 1)])
    ordered = lax.dynamic_slice_in_dim(ring, nfeat - 1 - axis, nfeat, 0)
    second_t = ordered[:, :grades].transpose(1, 0, 2).reshape(grades, hid).astype(BF16)
    bias = ordered[:, grades].reshape(hid, 1)
    second = second_t.T
    sent = make(arrived[1], tiles, features, 1, nfeat, others)
    last = list(make(arrived[1], tiles, features, 1, nfeat, (0,)))
    last += [ahead(piece, k) for k, piece in zip(others, sent)]
    hidden, proj = dense(first + last, weights, bias, second_t)

    projs = [proj] + [ahead(proj, k) for k in range(1, nfeat)]
    own, send = spread(table, me, projs)
    scale = 1.0 / math.sqrt(nblocks * BLK * parts)
    dlog, slotsum = logits_back(
        src, counts, me, swap(send), own, labels.reshape(nblocks, 1, BLK), tiles, scale, nfeat
    )
    dpre, small = small_gradients(table, me, swap(slotsum), dlog, hidden, second, nfeat)
    away = nearby(big_gradient(me, there, dpre, first + last, parts))
    big = big_gradient(me, here, dpre, first + last, parts)
    big = join(here, big, away, small, nearby(small))
    moved = lax.all_to_all(
        big.reshape(parts // 2 * nfeat, *big.shape[2:]),
        ("nodes", "feat"),
        split_axis=0,
        concat_axis=0,
        axis_index_groups=[
            [p * nfeat + f for p in range(c, parts, 2) for f in range(nfeat)] for c in range(2)
        ],
        tiled=True,
    )
    grad_first, rest = total(moved, hid // parts)
    grad_second, grad_bias = finish(here, rest, nearby(rest))
    return grad_first.T, grad_bias.reshape(-1), grad_second.T


def solution(mesh):
    placed = (
        P("nodes", "feat"),
        P("nodes", None),
        P("nodes", None, None),
        P("nodes", None),
        P("nodes", None, None, None),
        P("nodes"),
        P("feat", None),
        P("feat"),
        P("feat", None),
    )
    return jax.shard_map(
        shards,
        mesh=mesh,
        in_specs=placed,
        out_specs=(P("feat", "nodes"), P("feat"), P("feat", None)),
        check_vma=False,
    )
```

```python
import functools
import math

import jax
import jax.numpy as jnp
from jax import lax
from jax.experimental import pallas as pl
from jax.experimental.pallas import tpu as pltpu
from jax.sharding import PartitionSpec as P

F32 = jnp.float32
BF16 = jnp.bfloat16
NT = (((1,), (1,)), ((), ()))
NN = (((1,), (0,)), ((), ()))
BLK = 128
ORDER = (0, 2, 1, 3)
MIB = 1 << 20


def params(mib):
    return pltpu.CompilerParams(vmem_limit_bytes=mib * MIB)


def cost(flops, nbytes):
    return pl.CostEstimate(flops=flops, bytes_accessed=nbytes, transcendentals=0)


def dot(a, b, dims):
    return lax.dot_general(a, b, dims, preferred_element_type=F32)


def in_hbm(x):
    return pltpu.with_memory_space_constraint(x, pltpu.HBM)


def pick_kernel(chunk, table, features, out, held, sems):
    slots = out.shape[0]
    load = pltpu.make_async_copy(features.at[:, pl.ds(chunk * BLK, BLK)], held, sems.at[0])
    load.start()
    load.wait()

    @pl.loop(0, slots, unroll=8)
    def _(k):
        rows = pl.ds(pl.multiple_of(table[k] * BLK, BLK), BLK)
        pltpu.make_async_copy(held.at[rows], out.at[k], sems.at[1]).start()

    pltpu.make_async_copy(out, out, sems.at[1]).wait()


def pick(features, table, chunk):
    slots = table.shape[0]
    return pl.pallas_call(
        functools.partial(pick_kernel, chunk),
        grid_spec=pltpu.PrefetchScalarGridSpec(
            num_scalar_prefetch=1,
            grid=(),
            in_specs=[pl.BlockSpec(memory_space=pltpu.HBM)],
            out_specs=pl.BlockSpec(memory_space=pltpu.HBM),
            scratch_shapes=[
                pltpu.VMEM((features.shape[0], BLK), BF16),
                pltpu.SemaphoreType.DMA((2,)),
            ],
        ),
        out_shape=pltpu.HBM((slots, BLK, BLK), BF16),
        compiler_params=params(63),
        cost_estimate=cost(0, 4 * MIB),
        name="pick",
    )(table, in_hbm(features))


def agg_kernel(which, chunk, nfeat, src, counts, me, arrived, tiles_hbm, features, *refs):
    outs, (tiles, own, sems, *held) = refs[: len(which)], refs[len(which) :]
    group, per = tiles.shape[1:3]
    moves = []
    if held:
        moves.append(pltpu.make_async_copy(arrived, held[0], sems.at[2 * len(which)]))
        arrived = held[0]
    firsts = [lax.rem(me[0] + k, nfeat) * group for k in which]
    pairs = []
    for i, first in enumerate(firsts):
        rows = pl.ds(pl.multiple_of(first * BLK, BLK), group * BLK)
        tiles_move = pltpu.make_async_copy(
            tiles_hbm.at[pl.ds(first, group)], tiles.at[i], sems.at[2 * i]
        )
        own_move = pltpu.make_async_copy(
            features.at[rows, pl.ds(chunk * BLK, BLK)], own.at[i], sems.at[2 * i + 1]
        )
        pairs.append((tiles_move, own_move))
    for move in moves + [move for pair in pairs for move in pair]:
        move.start()
    for move in moves:
        move.wait()
    for i, (first, out) in enumerate(zip(firsts, outs)):
        for move in pairs[i]:
            move.wait()
        for b in range(group):
            rows, weights = [], []
            for t in range(per):
                slot = src[(first + b) * per + t]
                live = lax.rem(slot, 2) < counts[lax.div(slot, 2)]
                rows.append(arrived[slot])
                weights.append(tiles[i, b, t] * jnp.where(live, 1.0, 0.0).astype(BF16))
            total = dot(jnp.concatenate(weights, 1), jnp.concatenate(rows, 0), NN)
            at = pl.ds(b * BLK, BLK)
            out[at, :] = (own[i, at, :].astype(F32) + total).astype(BF16)


def aggregate(src, counts, me, arrived, tiles, features, chunk, nfeat, which):
    nblocks, per = tiles.shape[:2]
    group = nblocks // nfeat
    piece = jax.ShapeDtypeStruct((group * BLK, BLK), BF16)
    hbm = pl.BlockSpec(memory_space=pltpu.HBM)
    vmem = pl.BlockSpec(memory_space=pltpu.VMEM)
    load = chunk == 0
    return pl.pallas_call(
        functools.partial(agg_kernel, which, chunk, nfeat),
        grid_spec=pltpu.PrefetchScalarGridSpec(
            num_scalar_prefetch=3,
            grid=(),
            in_specs=[pl.BlockSpec(memory_space=pl.ANY) if load else vmem, hbm, hbm],
            out_specs=[vmem] * len(which),
            scratch_shapes=[
                pltpu.VMEM((len(which), group, per, BLK, BLK), BF16),
                pltpu.VMEM((len(which), group * BLK, BLK), BF16),
                pltpu.SemaphoreType.DMA((1 + 2 * len(which),)),
            ]
            + [pltpu.VMEM(arrived.shape, BF16)] * load,
        ),
        out_shape=[piece] * len(which),
        compiler_params=params(14),
        cost_estimate=cost(len(which) * group * per * 2 * BLK**3, 8 * MIB),
        name="aggregate",
    )(src, counts, me, arrived, in_hbm(tiles), in_hbm(features))


def dense_kernel(nfeat, *refs):
    pieces, (weights, bias, second, hidden, proj) = refs[: 2 * nfeat], refs[2 * nfeat :]
    order = [pieces[i * nfeat + k][...] for k in range(nfeat) for i in range(2)]
    pre = dot(weights[...], jnp.concatenate(order, 1), NT)
    hid = jnp.maximum(pre + bias[...], 0.0).astype(BF16)
    hidden[...] = hid
    out = dot(second[...], hid, NN)
    for b in range(proj.shape[0]):
        proj[b] = out[:, b * BLK : (b + 1) * BLK]


def dense(pieces, weights, bias, second):
    nodes, nfeat = pieces[0].shape[0], len(pieces) // 2
    hid, width = weights.shape
    grades = second.shape[0]
    step = 512
    return pl.pallas_call(
        functools.partial(dense_kernel, nfeat),
        grid=(nodes // step,),
        in_specs=[pl.BlockSpec((step, BLK), lambda g: (g, 0))] * (2 * nfeat)
        + [
            pl.BlockSpec((hid, width), lambda g: (0, 0)),
            pl.BlockSpec((hid, 1), lambda g: (0, 0)),
            pl.BlockSpec((grades, hid), lambda g: (0, 0)),
        ],
        out_specs=[
            pl.BlockSpec((hid, step), lambda g: (0, g)),
            pl.BlockSpec((step // BLK, grades, BLK), lambda g: (g, 0, 0)),
        ],
        out_shape=[
            jax.ShapeDtypeStruct((hid, nodes), BF16),
            jax.ShapeDtypeStruct((nodes // BLK, grades, BLK), F32),
        ],
        compiler_params=params(20),
        cost_estimate=cost(2 * nodes * hid * width, 7 * MIB),
        name="dense",
    )(*pieces, weights, bias, second)


def spread_kernel(table, me, p0, p1, p2, p3, whole, out):
    nfeat, group = 4, p0.shape[0]
    for k, piece in enumerate((p0, p1, p2, p3)):
        owner = lax.rem(me[0] + nfeat - k, nfeat)
        whole[pl.ds(owner * group, group)] = piece[...]

    @pl.loop(0, out.shape[0], unroll=8)
    def _(k):
        out[k] = whole[table[k]]


def spread(table, me, pieces):
    group, grades, _ = pieces[0].shape
    slots = table.shape[0]
    vmem = pl.BlockSpec(memory_space=pltpu.VMEM)
    return pl.pallas_call(
        spread_kernel,
        grid_spec=pltpu.PrefetchScalarGridSpec(
            num_scalar_prefetch=2,
            grid=(),
            in_specs=[vmem] * 4,
            out_specs=[vmem] * 2,
        ),
        out_shape=[
            jax.ShapeDtypeStruct((group * 4, grades, BLK), F32),
            jax.ShapeDtypeStruct((slots, grades, BLK), F32),
        ],
        compiler_params=params(4),
        cost_estimate=cost(0, MIB),
        name="spread",
    )(table, me, *pieces)


def logits_kernel(
    scale, src, counts, me, arrived, own, labels, tiles, dlog_out, slots_out, parts, field, grad_b, sums
):
    nblocks, per = tiles.shape[:2]
    nslots, grades, _ = arrived.shape
    mine = dlog_out.shape[0]

    def live_of(slot):
        return jnp.where(lax.rem(slot, 2) < counts[lax.div(slot, 2)], 1.0, 0.0)

    x = arrived[...]
    for i in range(3):
        y = x.astype(BF16)
        parts[:, i * grades : (i + 1) * grades, :] = y
        x = x - y.astype(F32)

    @pl.loop(0, nblocks, unroll=8)
    def _(b):
        rows, weights = [], []
        for t in range(per):
            slot = src[b * per + t]
            rows.append(parts[slot] * live_of(slot).astype(BF16))
            weights.append(tiles[b, t])
        triple = dot(jnp.concatenate(rows, 1), jnp.concatenate(weights, 1), NT)
        field[b] = own[b] + (
            triple[:grades] + (triple[grades : 2 * grades] + triple[2 * grades :])
        )

    expo = jnp.exp(field[...])
    probs = expo / jnp.sum(expo, axis=1, keepdims=True)
    grade = lax.broadcasted_iota(jnp.int32, field.shape, 1)
    onehot = jnp.where(labels[...] == grade, 1.0, 0.0)
    dlog = (probs - onehot) * scale
    field[...] = dlog
    grad_b[...] = dlog.astype(BF16)
    dlog_out[...] = field[pl.ds(me[0] * mine, mine)]
    sums[...] = jnp.zeros_like(sums)

    @pl.loop(0, nblocks, unroll=8)
    def _(b):
        back = dot(grad_b[b], jnp.concatenate([tiles[b, t] for t in range(per)], 1), NN)
        for t in range(per):
            slot = src[b * per + t]
            sums[slot] += back[:, t * BLK : (t + 1) * BLK] * live_of(slot)

    slots_out[...] = sums[...].astype(BF16)


def logits_back(src, counts, me, arrived, own, labels, tiles, scale, nfeat):
    nblocks, per = tiles.shape[:2]
    nslots, grades, _ = arrived.shape
    vmem = pl.BlockSpec(memory_space=pltpu.VMEM)
    return pl.pallas_call(
        functools.partial(logits_kernel, scale),
        grid_spec=pltpu.PrefetchScalarGridSpec(
            num_scalar_prefetch=3,
            grid=(),
            in_specs=[vmem] * 4,
            out_specs=[vmem] * 2,
            scratch_shapes=[
                pltpu.VMEM((nslots, 3 * grades, BLK), BF16),
                pltpu.VMEM((nblocks, grades, BLK), F32),
                pltpu.VMEM((nblocks, grades, BLK), BF16),
                pltpu.VMEM(arrived.shape, F32),
            ],
        ),
        out_shape=[
            jax.ShapeDtypeStruct((nblocks // nfeat, grades, BLK), F32),
            jax.ShapeDtypeStruct(arrived.shape, BF16),
        ],
        compiler_params=params(8),
        cost_estimate=cost(nblocks * per * 2 * 64 * BLK**2, 6 * MIB),
        name="logits",
    )(src, counts, me, arrived, own, labels, tiles)


def small_kernel(table, me, returned, dlog, hidden, second, dpre_out, small, total, dproj):
    group, grades, _ = dlog.shape
    width = hidden.shape[0]

    @pl.when(pl.program_id(0) == 0)
    def _():
        total[pl.ds(0, group)] = dlog[...]

        @pl.loop(0, returned.shape[0], unroll=8)
        def _(k):
            at = table[k] - me[0] * group
            at = jnp.where((at >= 0) & (at < group), at, group)
            total[at] += returned[k].astype(F32)

        for b in range(group):
            dproj[:, b * BLK : (b + 1) * BLK] = total[b].astype(BF16)

    active = hidden[...]
    dproj_b = dproj[...]
    dpre = jnp.where(active > 0, dot(second[...], dproj_b, NN), 0.0)
    dpre_out[...] = dpre.astype(BF16)
    small[pl.ds(0, grades), :] = dot(dproj_b, active, NT)
    part = dpre[:, :BLK]
    for i in range(1, dpre.shape[1] // BLK):
        part += dpre[:, i * BLK : (i + 1) * BLK]
    small[pl.ds(grades, 8), :] = jnp.broadcast_to(
        jnp.sum(part.T, axis=0, keepdims=True), (8, width)
    )


def small_gradients(table, me, returned, dlog, hidden, second, nfeat):
    hid, nodes = hidden.shape
    group, grades, _ = dlog.shape
    width = hid // nfeat
    whole3 = lambda g, t, m: (0, 0, 0)
    return pl.pallas_call(
        small_kernel,
        grid_spec=pltpu.PrefetchScalarGridSpec(
            num_scalar_prefetch=2,
            grid=(nfeat,),
            in_specs=[
                pl.BlockSpec(returned.shape, whole3),
                pl.BlockSpec(dlog.shape, whole3),
                pl.BlockSpec((width, nodes), lambda g, t, m: (g, 0)),
                pl.BlockSpec((width, grades), lambda g, t, m: (g, 0)),
            ],
            out_specs=[
                pl.BlockSpec((width, nodes), lambda g, t, m: (g, 0)),
                pl.BlockSpec((grades + 8, width), lambda g, t, m: (0, g)),
            ],
            scratch_shapes=[
                pltpu.VMEM((group + 1, grades, BLK), F32),
                pltpu.VMEM((grades, nodes), BF16),
            ],
        ),
        out_shape=[
            pltpu.HBM((hid, nodes), BF16),
            jax.ShapeDtypeStruct((grades + 8, hid), F32),
        ],
        compiler_params=params(16),
        cost_estimate=cost(2 * nodes * hid * 256, 4 * MIB),
        name="small_gradients",
    )(table, me, returned, dlog, hidden, second)


def big_kernel(me, side, dpre, *refs):
    pieces, out = refs[:-1], refs[-1]
    nfeat = len(pieces) // 2
    rows = dpre[...].reshape(-1, dpre.shape[-1])
    for i, k in enumerate(ORDER):
        owner = lax.rem(me[0] + nfeat - k, nfeat)
        both = jnp.concatenate([pieces[i][...], pieces[nfeat + i][...]], 1)
        grad = dot(rows, both, NN).astype(BF16)
        out[:, owner] = grad.reshape(out.shape[0], out.shape[2], out.shape[3])


def big_gradient(me, side, dpre, pieces, parts):
    nfeat = len(pieces) // 2
    hid, nodes = dpre.shape
    cols = hid // parts
    vmem = pl.BlockSpec(memory_space=pltpu.VMEM)
    return pl.pallas_call(
        big_kernel,
        grid_spec=pltpu.PrefetchScalarGridSpec(
            num_scalar_prefetch=2,
            grid=(1,),
            in_specs=[
                pl.BlockSpec((parts // 2, 1, cols, nodes), lambda g, m, s: (0, s[0], 0, 0))
            ]
            + [vmem] * (2 * nfeat),
            out_specs=pl.BlockSpec(
                (parts // 2, nfeat, cols, 2 * BLK), lambda g, m, s: (0, 0, 0, 0)
            ),
        ),
        out_shape=jax.ShapeDtypeStruct((parts // 2, nfeat, cols, 2 * BLK), BF16),
        compiler_params=params(16),
        cost_estimate=cost(nodes * hid * hid, 4 * MIB),
        name="big_gradient",
    )(me, side, in_hbm(dpre.reshape(parts // 2, 2, cols, nodes)), *pieces)


def join_kernel(side, a, b, small, other, out):
    width = a.shape[3]
    more = out.shape[2] - a.shape[2]
    both = small[...] + other[...]
    near = both.astype(BF16).astype(F32)
    rest = both - near
    second = jnp.concatenate(
        [near[more : more + 1], rest[more : more + 1], rest[: more - 2]], 0
    )
    kept = jnp.where(side[0] == 0, near[:more], second)
    for f in range(a.shape[1]):
        share = kept[:, f * width : (f + 1) * width]
        for p in range(a.shape[0]):
            grad = a[p, f].astype(F32) + b[p, f].astype(F32)
            out[p, f] = jnp.concatenate([grad, share], 0).astype(BF16)


def join(side, a, b, small, other):
    steps = 4
    lead, nfeat, rows, width = a.shape
    more = small.shape[0] - 8
    spec = lambda n: pl.BlockSpec((lead // steps, nfeat, n, width), lambda g, s: (g, 0, 0, 0))
    whole = pl.BlockSpec(small.shape, lambda g, s: (0, 0))
    return pl.pallas_call(
        join_kernel,
        grid_spec=pltpu.PrefetchScalarGridSpec(
            num_scalar_prefetch=1,
            grid=(steps,),
            in_specs=[spec(rows), spec(rows), whole, whole],
            out_specs=spec(rows + more),
        ),
        out_shape=pltpu.HBM((lead, nfeat, rows + more, width), BF16),
        compiler_params=params(8),
        cost_estimate=cost(a.size, 4 * MIB),
        name="join",
    )(side, a, b, small, other)


def total_kernel(arrived, out, small, acc):
    g = pl.program_id(0)
    rows = out.shape[0]

    @pl.when(g == 0)
    def _():
        acc[...] = jnp.zeros_like(acc)

    total = arrived[0].astype(F32)
    for i in range(1, arrived.shape[0]):
        total += arrived[i].astype(F32)
    acc[...] += total

    @pl.when(g == pl.num_programs(0) - 1)
    def _():
        out[...] = acc[pl.ds(0, rows), :]
        small[...] = acc[pl.ds(rows, small.shape[0]), :]


def total(arrived, rows):
    n, full, width = arrived.shape
    step = n // 8
    shapes = [(rows, width), (full - rows, width)]
    return pl.pallas_call(
        total_kernel,
        grid=(n // step,),
        in_specs=[pl.BlockSpec((step, full, width), lambda g: (g, 0, 0))],
        out_specs=[pl.BlockSpec(shape, lambda g: (0, 0)) for shape in shapes],
        out_shape=[jax.ShapeDtypeStruct(shape, F32) for shape in shapes],
        scratch_shapes=[pltpu.VMEM((full, width), F32)],
        compiler_params=params(8),
        cost_estimate=cost(0, 2 * MIB),
        name="total",
    )(arrived)


def finish_kernel(side, a, b, second, bias):
    first = side[0] == 0
    near = jnp.where(first, a[...], b[...])
    rest = jnp.where(first, b[...], a[...])
    second[...] = near + jnp.concatenate([rest[2:], jnp.zeros_like(rest[:2])], 0)
    bias[...] = rest[:1] + rest[1:2]


def finish(side, a, b):
    vmem = pl.BlockSpec(memory_space=pltpu.VMEM)
    return pl.pallas_call(
        finish_kernel,
        grid_spec=pltpu.PrefetchScalarGridSpec(
            num_scalar_prefetch=1,
            grid=(),
            in_specs=[vmem] * 2,
            out_specs=[vmem] * 2,
        ),
        out_shape=[
            jax.ShapeDtypeStruct(a.shape, F32),
            jax.ShapeDtypeStruct((1, a.shape[1]), F32),
        ],
        compiler_params=params(2),
        cost_estimate=cost(0, MIB // 8),
        name="finish",
    )(side, a, b)


def shards(features, pair_count, send_blocks, tile_src, tiles, labels, w_first, b_first, w_second):
    nblocks = tile_src.shape[0]
    parts = lax.axis_size("nodes")
    nfeat = lax.axis_size("feat")
    slots = send_blocks.shape[2]
    grades = w_second.shape[1]
    hid = w_first.shape[1]
    axis = lax.axis_index("feat").astype(jnp.int32)
    me = axis.reshape(1)
    table = send_blocks.reshape(parts * slots)
    src = tile_src.reshape(-1)
    counts = pair_count.reshape(-1)

    def ahead(x, k):
        return lax.ppermute(x, "feat", [(i, (i + k) % nfeat) for i in range(nfeat)])

    def nearby(x):
        return lax.ppermute(x, "nodes", [(i, i ^ 1) for i in range(parts)])

    def swap(x):
        shaped = x.reshape(parts, slots, *x.shape[1:])
        moved = lax.all_to_all(shaped, "nodes", split_axis=0, concat_axis=0, tiled=True)
        return moved.reshape(x.shape)

    arrived = [swap(pick(features, table, 0))]
    send = pick(features, table, 1)

    flat = w_first.T
    weights = [ahead(flat, k) for k in (2, 1, 3)]
    consts = jnp.concatenate(
        [w_second.T.astype(F32), jnp.broadcast_to(b_first[None], (8, b_first.shape[0]))], 0
    )
    send, weights, arrived = lax.optimization_barrier((send, weights, arrived))
    arrived.append(swap(send))
    others = (2, 1, 3)
    make = functools.partial(aggregate, src, counts, me)
    *sent, own = make(arrived[0], tiles, features, 0, nfeat, others + (0,))
    first = [own] + [ahead(piece, k) for k, piece in zip(others, sent)]
    core = (lax.axis_index("nodes").astype(jnp.int32) % 2).reshape(1)
    consts, weights, here, there, first[0] = lax.optimization_barrier(
        (consts, weights, core, 1 - core, first[0])
    )
    weights = jnp.concatenate([flat] + weights, 1)
    turned = [consts] + [ahead(consts, k) for k in range(1, nfeat)]
    ring = jnp.stack([turned[k] for k in (3, 2, 1, 0, 3, 2, 1)])
    ordered = lax.dynamic_slice_in_dim(ring, nfeat - 1 - axis, nfeat, 0)
    second_t = ordered[:, :grades].transpose(1, 0, 2).reshape(grades, hid).astype(BF16)
    bias = ordered[:, grades].reshape(hid, 1)
    second = second_t.T
    sent = make(arrived[1], tiles, features, 1, nfeat, others)
    last = list(make(arrived[1], tiles, features, 1, nfeat, (0,)))
    last += [ahead(piece, k) for k, piece in zip(others, sent)]
    hidden, proj = dense(first + last, weights, bias, second_t)

    projs = [proj] + [ahead(proj, k) for k in range(1, nfeat)]
    own, send = spread(table, me, projs)
    scale = 1.0 / math.sqrt(nblocks * BLK * parts)
    dlog, slotsum = logits_back(
        src, counts, me, swap(send), own, labels.reshape(nblocks, 1, BLK), tiles, scale, nfeat
    )
    dpre, small = small_gradients(table, me, swap(slotsum), dlog, hidden, second, nfeat)
    away = nearby(big_gradient(me, there, dpre, first + last, parts))
    big = big_gradient(me, here, dpre, first + last, parts)
    big = join(here, big, away, small, nearby(small))
    moved = lax.all_to_all(
        big.reshape(parts // 2 * nfeat, *big.shape[2:]),
        ("nodes", "feat"),
        split_axis=0,
        concat_axis=0,
        axis_index_groups=[
            [p * nfeat + f for p in range(c, parts, 2) for f in range(nfeat)] for c in range(2)
        ],
        tiled=True,
    )
    grad_first, rest = total(moved, hid // parts)
    grad_second, grad_bias = finish(here, rest, nearby(rest))
    return grad_first.T, grad_bias.reshape(-1), grad_second.T


def solution(mesh):
    placed = (
        P("nodes", "feat"),
        P("nodes", None),
        P("nodes", None, None),
        P("nodes", None),
        P("nodes", None, None, None),
        P("nodes"),
        P("feat", None),
        P("feat"),
        P("feat", None),
    )
    return jax.shard_map(
        shards,
        mesh=mesh,
        in_specs=placed,
        out_specs=(P("feat", "nodes"), P("feat"), P("feat", None)),
        check_vma=False,
    )
```

```python
import functools
import math

import jax
import jax.numpy as jnp
from jax import lax
from jax.experimental import pallas as pl
from jax.experimental.pallas import tpu as pltpu
from jax.sharding import PartitionSpec as P

F32 = jnp.float32
BF16 = jnp.bfloat16
NT = (((1,), (1,)), ((), ()))
NN = (((1,), (0,)), ((), ()))
BLK = 128
ORDER = (0, 2, 1, 3)
MIB = 1 << 20


def params(mib):
    return pltpu.CompilerParams(vmem_limit_bytes=mib * MIB)


def cost(flops, nbytes):
    return pl.CostEstimate(flops=flops, bytes_accessed=nbytes, transcendentals=0)


def dot(a, b, dims):
    return lax.dot_general(a, b, dims, preferred_element_type=F32)


def in_hbm(x):
    return pltpu.with_memory_space_constraint(x, pltpu.HBM)


def pick_kernel(chunk, table, features, out, held, sems):
    slots = out.shape[0]
    load = pltpu.make_async_copy(features.at[:, pl.ds(chunk * BLK, BLK)], held, sems.at[0])
    load.start()
    load.wait()

    @pl.loop(0, slots, unroll=8)
    def _(k):
        rows = pl.ds(pl.multiple_of(table[k] * BLK, BLK), BLK)
        pltpu.make_async_copy(held.at[rows], out.at[k], sems.at[1]).start()

    pltpu.make_async_copy(out, out, sems.at[1]).wait()


def pick(features, table, chunk):
    slots = table.shape[0]
    return pl.pallas_call(
        functools.partial(pick_kernel, chunk),
        grid_spec=pltpu.PrefetchScalarGridSpec(
            num_scalar_prefetch=1,
            grid=(),
            in_specs=[pl.BlockSpec(memory_space=pltpu.HBM)],
            out_specs=pl.BlockSpec(memory_space=pltpu.HBM),
            scratch_shapes=[
                pltpu.VMEM((features.shape[0], BLK), BF16),
                pltpu.SemaphoreType.DMA((2,)),
            ],
        ),
        out_shape=pltpu.HBM((slots, BLK, BLK), BF16),
        compiler_params=params(63),
        cost_estimate=cost(0, 4 * MIB),
        name="pick",
    )(table, in_hbm(features))


def agg_kernel(which, chunk, nfeat, src, counts, me, arrived, tiles_hbm, features, *refs):
    outs, (tiles, own, sems, *held) = refs[: len(which)], refs[len(which) :]
    group, per = tiles.shape[1:3]
    moves = []
    if held:
        moves.append(pltpu.make_async_copy(arrived, held[0], sems.at[2 * len(which)]))
        arrived = held[0]
    firsts = [lax.rem(me[0] + k, nfeat) * group for k in which]
    pairs = []
    for i, first in enumerate(firsts):
        rows = pl.ds(pl.multiple_of(first * BLK, BLK), group * BLK)
        tiles_move = pltpu.make_async_copy(
            tiles_hbm.at[pl.ds(first, group)], tiles.at[i], sems.at[2 * i]
        )
        own_move = pltpu.make_async_copy(
            features.at[rows, pl.ds(chunk * BLK, BLK)], own.at[i], sems.at[2 * i + 1]
        )
        pairs.append((tiles_move, own_move))
    for move in moves + [move for pair in pairs for move in pair]:
        move.start()
    for move in moves:
        move.wait()
    for i, (first, out) in enumerate(zip(firsts, outs)):
        for move in pairs[i]:
            move.wait()
        for b in range(group):
            rows, weights = [], []
            for t in range(per):
                slot = src[(first + b) * per + t]
                live = lax.rem(slot, 2) < counts[lax.div(slot, 2)]
                rows.append(arrived[slot])
                weights.append(tiles[i, b, t] * jnp.where(live, 1.0, 0.0).astype(BF16))
            total = dot(jnp.concatenate(weights, 1), jnp.concatenate(rows, 0), NN)
            at = pl.ds(b * BLK, BLK)
            out[at, :] = (own[i, at, :].astype(F32) + total).astype(BF16)


def aggregate(src, counts, me, arrived, tiles, features, chunk, nfeat, which):
    nblocks, per = tiles.shape[:2]
    group = nblocks // nfeat
    piece = jax.ShapeDtypeStruct((group * BLK, BLK), BF16)
    hbm = pl.BlockSpec(memory_space=pltpu.HBM)
    vmem = pl.BlockSpec(memory_space=pltpu.VMEM)
    load = chunk == 0
    return pl.pallas_call(
        functools.partial(agg_kernel, which, chunk, nfeat),
        grid_spec=pltpu.PrefetchScalarGridSpec(
            num_scalar_prefetch=3,
            grid=(),
            in_specs=[pl.BlockSpec(memory_space=pl.ANY) if load else vmem, hbm, hbm],
            out_specs=[vmem] * len(which),
            scratch_shapes=[
                pltpu.VMEM((len(which), group, per, BLK, BLK), BF16),
                pltpu.VMEM((len(which), group * BLK, BLK), BF16),
                pltpu.SemaphoreType.DMA((1 + 2 * len(which),)),
            ]
            + [pltpu.VMEM(arrived.shape, BF16)] * load,
        ),
        out_shape=[piece] * len(which),
        compiler_params=params(14),
        cost_estimate=cost(len(which) * group * per * 2 * BLK**3, 8 * MIB),
        name="aggregate",
    )(src, counts, me, arrived, in_hbm(tiles), in_hbm(features))


def assemble_kernel(me, *refs):
    flats, (weights, second_t, second, bias, consts) = refs[:4], refs[4:]
    hid, grades = second.shape
    width = flats[0].shape[1]
    consts[...] = jnp.zeros_like(consts)
    for i, k in enumerate(ORDER):
        weights[:, i * width : (i + 1) * width] = flats[i][pl.ds(0, hid), :]
        owner = lax.rem(me[0] + len(ORDER) - k, len(ORDER))
        lanes = pl.ds(pl.multiple_of(owner * width, width), width)
        tail = flats[i][pl.ds(hid, 2 * grades), :].astype(F32)
        consts[pl.ds(0, grades), lanes] = tail[:grades]
        b = (tail[grades : grades + 1] + tail[grades + 1 : grades + 2]) + tail[
            grades + 2 : grades + 3
        ]
        consts[pl.ds(grades, 8), lanes] = jnp.broadcast_to(b, (8, width))
    second_t[...] = consts[pl.ds(0, grades), :].astype(BF16)
    turned = consts[...].T
    second[...] = turned[:, :grades].astype(BF16)
    bias[...] = turned[:, grades : grades + 1]


def assemble(me, flats, hid, grades):
    vmem = pl.BlockSpec(memory_space=pltpu.VMEM)
    return pl.pallas_call(
        assemble_kernel,
        grid_spec=pltpu.PrefetchScalarGridSpec(
            num_scalar_prefetch=1,
            grid=(),
            in_specs=[vmem] * 4,
            out_specs=[vmem] * 4,
            scratch_shapes=[pltpu.VMEM((BLK, hid), F32)],
        ),
        out_shape=[
            jax.ShapeDtypeStruct((hid, hid), BF16),
            jax.ShapeDtypeStruct((grades, hid), BF16),
            jax.ShapeDtypeStruct((hid, grades), BF16),
            jax.ShapeDtypeStruct((hid, 1), F32),
        ],
        compiler_params=params(16),
        cost_estimate=cost(0, 5 * MIB),
        name="assemble",
    )(me, *flats)


def dense_kernel(nfeat, *refs):
    pieces, (weights, bias, second, hidden, proj) = refs[: 2 * nfeat], refs[2 * nfeat :]
    order = [pieces[i * nfeat + k][...] for k in range(nfeat) for i in range(2)]
    pre = dot(weights[...], jnp.concatenate(order, 1), NT)
    hid = jnp.maximum(pre + bias[...], 0.0).astype(BF16)
    hidden[...] = hid
    out = dot(second[...], hid, NN)
    for b in range(proj.shape[0]):
        proj[b] = out[:, b * BLK : (b + 1) * BLK]


def dense(pieces, weights, bias, second):
    nodes, nfeat = pieces[0].shape[0], len(pieces) // 2
    hid, width = weights.shape
    grades = second.shape[0]
    step = 512
    return pl.pallas_call(
        functools.partial(dense_kernel, nfeat),
        grid=(nodes // step,),
        in_specs=[pl.BlockSpec((step, BLK), lambda g: (g, 0))] * (2 * nfeat)
        + [
            pl.BlockSpec((hid, width), lambda g: (0, 0)),
            pl.BlockSpec((hid, 1), lambda g: (0, 0)),
            pl.BlockSpec((grades, hid), lambda g: (0, 0)),
        ],
        out_specs=[
            pl.BlockSpec((hid, step), lambda g: (0, g)),
            pl.BlockSpec((step // BLK, grades, BLK), lambda g: (g, 0, 0)),
        ],
        out_shape=[
            jax.ShapeDtypeStruct((hid, nodes), BF16),
            jax.ShapeDtypeStruct((nodes // BLK, grades, BLK), F32),
        ],
        compiler_params=params(20),
        cost_estimate=cost(2 * nodes * hid * width, 7 * MIB),
        name="dense",
    )(*pieces, weights, bias, second)


def spread_kernel(table, me, p0, p1, p2, p3, whole, out):
    nfeat, group = 4, p0.shape[0]
    for k, piece in enumerate((p0, p1, p2, p3)):
        owner = lax.rem(me[0] + nfeat - k, nfeat)
        whole[pl.ds(owner * group, group)] = piece[...]

    @pl.loop(0, out.shape[0], unroll=8)
    def _(k):
        out[k] = whole[table[k]]


def spread(table, me, pieces):
    group, grades, _ = pieces[0].shape
    slots = table.shape[0]
    vmem = pl.BlockSpec(memory_space=pltpu.VMEM)
    return pl.pallas_call(
        spread_kernel,
        grid_spec=pltpu.PrefetchScalarGridSpec(
            num_scalar_prefetch=2,
            grid=(),
            in_specs=[vmem] * 4,
            out_specs=[vmem] * 2,
        ),
        out_shape=[
            jax.ShapeDtypeStruct((group * 4, grades, BLK), F32),
            jax.ShapeDtypeStruct((slots, grades, BLK), F32),
        ],
        compiler_params=params(4),
        cost_estimate=cost(0, MIB),
        name="spread",
    )(table, me, *pieces)


def logits_kernel(
    scale, src, counts, me, arrived, own, labels, tiles, dlog_out, slots_out, parts, field, grad_b, sums
):
    nblocks, per = tiles.shape[:2]
    nslots, grades, _ = arrived.shape
    mine = dlog_out.shape[0]

    def live_of(slot):
        return jnp.where(lax.rem(slot, 2) < counts[lax.div(slot, 2)], 1.0, 0.0)

    x = arrived[...]
    for i in range(3):
        y = x.astype(BF16)
        parts[:, i * grades : (i + 1) * grades, :] = y
        x = x - y.astype(F32)

    @pl.loop(0, nblocks, unroll=8)
    def _(b):
        rows, weights = [], []
        for t in range(per):
            slot = src[b * per + t]
            rows.append(parts[slot] * live_of(slot).astype(BF16))
            weights.append(tiles[b, t])
        triple = dot(jnp.concatenate(rows, 1), jnp.concatenate(weights, 1), NT)
        field[b] = own[b] + (
            triple[:grades] + (triple[grades : 2 * grades] + triple[2 * grades :])
        )

    expo = jnp.exp(field[...])
    probs = expo / jnp.sum(expo, axis=1, keepdims=True)
    grade = lax.broadcasted_iota(jnp.int32, field.shape, 1)
    onehot = jnp.where(labels[...] == grade, 1.0, 0.0)
    dlog = (probs - onehot) * scale
    field[...] = dlog
    grad_b[...] = dlog.astype(BF16)
    dlog_out[...] = field[pl.ds(me[0] * mine, mine)]
    sums[...] = jnp.zeros_like(sums)

    @pl.loop(0, nblocks, unroll=8)
    def _(b):
        back = dot(grad_b[b], jnp.concatenate([tiles[b, t] for t in range(per)], 1), NN)
        for t in range(per):
            slot = src[b * per + t]
            sums[slot] += back[:, t * BLK : (t + 1) * BLK] * live_of(slot)

    slots_out[...] = sums[...].astype(BF16)


def logits_back(src, counts, me, arrived, own, labels, tiles, scale, nfeat):
    nblocks, per = tiles.shape[:2]
    nslots, grades, _ = arrived.shape
    vmem = pl.BlockSpec(memory_space=pltpu.VMEM)
    return pl.pallas_call(
        functools.partial(logits_kernel, scale),
        grid_spec=pltpu.PrefetchScalarGridSpec(
            num_scalar_prefetch=3,
            grid=(),
            in_specs=[vmem] * 4,
            out_specs=[vmem] * 2,
            scratch_shapes=[
                pltpu.VMEM((nslots, 3 * grades, BLK), BF16),
                pltpu.VMEM((nblocks, grades, BLK), F32),
                pltpu.VMEM((nblocks, grades, BLK), BF16),
                pltpu.VMEM(arrived.shape, F32),
            ],
        ),
        out_shape=[
            jax.ShapeDtypeStruct((nblocks // nfeat, grades, BLK), F32),
            jax.ShapeDtypeStruct(arrived.shape, BF16),
        ],
        compiler_params=params(8),
        cost_estimate=cost(nblocks * per * 2 * 64 * BLK**2, 6 * MIB),
        name="logits",
    )(src, counts, me, arrived, own, labels, tiles)


def small_kernel(table, me, returned, dlog, hidden, second, dpre_out, small, total, dproj):
    group, grades, _ = dlog.shape
    width = hidden.shape[0]

    @pl.when(pl.program_id(0) == 0)
    def _():
        total[pl.ds(0, group)] = dlog[...]

        @pl.loop(0, returned.shape[0], unroll=8)
        def _(k):
            at = table[k] - me[0] * group
            at = jnp.where((at >= 0) & (at < group), at, group)
            total[at] += returned[k].astype(F32)

        for b in range(group):
            dproj[:, b * BLK : (b + 1) * BLK] = total[b].astype(BF16)

    active = hidden[...]
    dproj_b = dproj[...]
    dpre = jnp.where(active > 0, dot(second[...], dproj_b, NN), 0.0)
    dpre_out[...] = dpre.astype(BF16)
    small[pl.ds(0, grades), :] = dot(dproj_b, active, NT)
    part = dpre[:, :BLK]
    for i in range(1, dpre.shape[1] // BLK):
        part += dpre[:, i * BLK : (i + 1) * BLK]
    small[pl.ds(grades, 8), :] = jnp.broadcast_to(
        jnp.sum(part.T, axis=0, keepdims=True), (8, width)
    )


def small_gradients(table, me, returned, dlog, hidden, second, nfeat):
    hid, nodes = hidden.shape
    group, grades, _ = dlog.shape
    width = hid // nfeat
    whole3 = lambda g, t, m: (0, 0, 0)
    return pl.pallas_call(
        small_kernel,
        grid_spec=pltpu.PrefetchScalarGridSpec(
            num_scalar_prefetch=2,
            grid=(nfeat,),
            in_specs=[
                pl.BlockSpec(returned.shape, whole3),
                pl.BlockSpec(dlog.shape, whole3),
                pl.BlockSpec((width, nodes), lambda g, t, m: (g, 0)),
                pl.BlockSpec((width, grades), lambda g, t, m: (g, 0)),
            ],
            out_specs=[
                pl.BlockSpec((width, nodes), lambda g, t, m: (g, 0)),
                pl.BlockSpec((grades + 8, width), lambda g, t, m: (0, g)),
            ],
            scratch_shapes=[
                pltpu.VMEM((group + 1, grades, BLK), F32),
                pltpu.VMEM((grades, nodes), BF16),
            ],
        ),
        out_shape=[
            pltpu.HBM((hid, nodes), BF16),
            jax.ShapeDtypeStruct((grades + 8, hid), F32),
        ],
        compiler_params=params(16),
        cost_estimate=cost(2 * nodes * hid * 256, 4 * MIB),
        name="small_gradients",
    )(table, me, returned, dlog, hidden, second)


def big_kernel(me, side, dpre, *refs):
    pieces, out = refs[:-1], refs[-1]
    nfeat = len(pieces) // 2
    rows = dpre[...].reshape(-1, dpre.shape[-1])
    for i, k in enumerate(ORDER):
        owner = lax.rem(me[0] + nfeat - k, nfeat)
        both = jnp.concatenate([pieces[i][...], pieces[nfeat + i][...]], 1)
        grad = dot(rows, both, NN).astype(BF16)
        out[:, owner] = grad.reshape(out.shape[0], out.shape[2], out.shape[3])


def big_gradient(me, side, dpre, pieces, parts):
    nfeat = len(pieces) // 2
    hid, nodes = dpre.shape
    cols = hid // parts
    vmem = pl.BlockSpec(memory_space=pltpu.VMEM)
    return pl.pallas_call(
        big_kernel,
        grid_spec=pltpu.PrefetchScalarGridSpec(
            num_scalar_prefetch=2,
            grid=(1,),
            in_specs=[
                pl.BlockSpec((parts // 2, 1, cols, nodes), lambda g, m, s: (0, s[0], 0, 0))
            ]
            + [vmem] * (2 * nfeat),
            out_specs=pl.BlockSpec(
                (parts // 2, nfeat, cols, 2 * BLK), lambda g, m, s: (0, 0, 0, 0)
            ),
        ),
        out_shape=jax.ShapeDtypeStruct((parts // 2, nfeat, cols, 2 * BLK), BF16),
        compiler_params=params(16),
        cost_estimate=cost(nodes * hid * hid, 4 * MIB),
        name="big_gradient",
    )(me, side, in_hbm(dpre.reshape(parts // 2, 2, cols, nodes)), *pieces)


def join_kernel(side, a, b, small, other, out):
    width = a.shape[3]
    more = out.shape[2] - a.shape[2]
    both = small[...] + other[...]
    near = both.astype(BF16).astype(F32)
    rest = both - near
    second = jnp.concatenate(
        [near[more : more + 1], rest[more : more + 1], rest[: more - 2]], 0
    )
    kept = jnp.where(side[0] == 0, near[:more], second)
    for f in range(a.shape[1]):
        share = kept[:, f * width : (f + 1) * width]
        for p in range(a.shape[0]):
            grad = a[p, f].astype(F32) + b[p, f].astype(F32)
            out[p, f] = jnp.concatenate([grad, share], 0).astype(BF16)


def join(side, a, b, small, other):
    steps = 4
    lead, nfeat, rows, width = a.shape
    more = small.shape[0] - 8
    spec = lambda n: pl.BlockSpec((lead // steps, nfeat, n, width), lambda g, s: (g, 0, 0, 0))
    whole = pl.BlockSpec(small.shape, lambda g, s: (0, 0))
    return pl.pallas_call(
        join_kernel,
        grid_spec=pltpu.PrefetchScalarGridSpec(
            num_scalar_prefetch=1,
            grid=(steps,),
            in_specs=[spec(rows), spec(rows), whole, whole],
            out_specs=spec(rows + more),
        ),
        out_shape=pltpu.HBM((lead, nfeat, rows + more, width), BF16),
        compiler_params=params(8),
        cost_estimate=cost(a.size, 4 * MIB),
        name="join",
    )(side, a, b, small, other)


def total_kernel(arrived, out, small, acc):
    g = pl.program_id(0)
    rows = out.shape[0]

    @pl.when(g == 0)
    def _():
        acc[...] = jnp.zeros_like(acc)

    total = arrived[0].astype(F32)
    for i in range(1, arrived.shape[0]):
        total += arrived[i].astype(F32)
    acc[...] += total

    @pl.when(g == pl.num_programs(0) - 1)
    def _():
        out[...] = acc[pl.ds(0, rows), :]
        small[...] = acc[pl.ds(rows, small.shape[0]), :]


def total(arrived, rows):
    n, full, width = arrived.shape
    step = n // 8
    shapes = [(rows, width), (full - rows, width)]
    return pl.pallas_call(
        total_kernel,
        grid=(n // step,),
        in_specs=[pl.BlockSpec((step, full, width), lambda g: (g, 0, 0))],
        out_specs=[pl.BlockSpec(shape, lambda g: (0, 0)) for shape in shapes],
        out_shape=[jax.ShapeDtypeStruct(shape, F32) for shape in shapes],
        scratch_shapes=[pltpu.VMEM((full, width), F32)],
        compiler_params=params(8),
        cost_estimate=cost(0, 2 * MIB),
        name="total",
    )(arrived)


def finish_kernel(side, a, b, second, bias):
    first = side[0] == 0
    near = jnp.where(first, a[...], b[...])
    rest = jnp.where(first, b[...], a[...])
    second[...] = near + jnp.concatenate([rest[2:], jnp.zeros_like(rest[:2])], 0)
    bias[...] = rest[:1] + rest[1:2]


def finish(side, a, b):
    vmem = pl.BlockSpec(memory_space=pltpu.VMEM)
    return pl.pallas_call(
        finish_kernel,
        grid_spec=pltpu.PrefetchScalarGridSpec(
            num_scalar_prefetch=1,
            grid=(),
            in_specs=[vmem] * 2,
            out_specs=[vmem] * 2,
        ),
        out_shape=[
            jax.ShapeDtypeStruct(a.shape, F32),
            jax.ShapeDtypeStruct((1, a.shape[1]), F32),
        ],
        compiler_params=params(2),
        cost_estimate=cost(0, MIB // 8),
        name="finish",
    )(side, a, b)


def shards(features, pair_count, send_blocks, tile_src, tiles, labels, w_first, b_first, w_second):
    nblocks = tile_src.shape[0]
    parts = lax.axis_size("nodes")
    nfeat = lax.axis_size("feat")
    slots = send_blocks.shape[2]
    grades = w_second.shape[1]
    hid = w_first.shape[1]
    axis = lax.axis_index("feat").astype(jnp.int32)
    me = axis.reshape(1)
    table = send_blocks.reshape(parts * slots)
    src = tile_src.reshape(-1)
    counts = pair_count.reshape(-1)

    def ahead(x, k):
        return lax.ppermute(x, "feat", [(i, (i + k) % nfeat) for i in range(nfeat)])

    def nearby(x):
        return lax.ppermute(x, "nodes", [(i, i ^ 1) for i in range(parts)])

    def swap(x):
        shaped = x.reshape(parts, slots, *x.shape[1:])
        moved = lax.all_to_all(shaped, "nodes", split_axis=0, concat_axis=0, tiled=True)
        return moved.reshape(x.shape)

    arrived = [swap(pick(features, table, 0))]
    send = pick(features, table, 1)

    high = lax.reduce_precision(b_first, 8, 7)
    middle = lax.reduce_precision(b_first - high, 8, 7)
    split = jnp.stack([high, middle, (b_first - high) - middle]).astype(BF16)
    flat = jnp.concatenate(
        [w_first.T, w_second.T, jnp.pad(split, ((0, grades - 3), (0, 0)))], 0
    )
    flats = [ahead(flat, k) for k in (2, 1, 3)]
    send, flats, arrived = lax.optimization_barrier((send, flats, arrived))
    arrived.append(swap(send))
    others = (2, 1, 3)
    make = functools.partial(aggregate, src, counts, me)
    *sent, own = make(arrived[0], tiles, features, 0, nfeat, others + (0,))
    first = [own] + [ahead(piece, k) for k, piece in zip(others, sent)]
    core = (lax.axis_index("nodes").astype(jnp.int32) % 2).reshape(1)
    flats, here, there, first[0] = lax.optimization_barrier(
        (flats, core, 1 - core, first[0])
    )
    weights, second_t, second, bias = assemble(me, [flat] + flats, hid, grades)
    arrived[1], weights, second_t, bias, second, first = lax.optimization_barrier(
        (arrived[1], weights, second_t, bias, second, first)
    )
    sent = make(arrived[1], tiles, features, 1, nfeat, others)
    last = list(make(arrived[1], tiles, features, 1, nfeat, (0,)))
    last += [ahead(piece, k) for k, piece in zip(others, sent)]
    hidden, proj = dense(first + last, weights, bias, second_t)

    projs = [proj] + [ahead(proj, k) for k in range(1, nfeat)]
    own, send = spread(table, me, projs)
    scale = 1.0 / math.sqrt(nblocks * BLK * parts)
    dlog, slotsum = logits_back(
        src, counts, me, swap(send), own, labels.reshape(nblocks, 1, BLK), tiles, scale, nfeat
    )
    dpre, small = small_gradients(table, me, swap(slotsum), dlog, hidden, second, nfeat)
    away = nearby(big_gradient(me, there, dpre, first + last, parts))
    big = big_gradient(me, here, dpre, first + last, parts)
    big = join(here, big, away, small, nearby(small))
    moved = lax.all_to_all(
        big.reshape(parts // 2 * nfeat, *big.shape[2:]),
        ("nodes", "feat"),
        split_axis=0,
        concat_axis=0,
        axis_index_groups=[
            [p * nfeat + f for p in range(c, parts, 2) for f in range(nfeat)] for c in range(2)
        ],
        tiled=True,
    )
    grad_first, rest = total(moved, hid // parts)
    grad_second, grad_bias = finish(here, rest, nearby(rest))
    return grad_first.T, grad_bias.reshape(-1), grad_second.T


def solution(mesh):
    placed = (
        P("nodes", "feat"),
        P("nodes", None),
        P("nodes", None, None),
        P("nodes", None),
        P("nodes", None, None, None),
        P("nodes"),
        P("feat", None),
        P("feat"),
        P("feat", None),
    )
    return jax.shard_map(
        shards,
        mesh=mesh,
        in_specs=placed,
        out_specs=(P("feat", "nodes"), P("feat"), P("feat", None)),
        check_vma=False,
    )
```

```python
import functools
import math

import jax
import jax.numpy as jnp
from jax import lax
from jax.experimental import pallas as pl
from jax.experimental.pallas import tpu as pltpu
from jax.sharding import PartitionSpec as P

F32 = jnp.float32
BF16 = jnp.bfloat16
NT = (((1,), (1,)), ((), ()))
NN = (((1,), (0,)), ((), ()))
BLK = 128
ORDER = (0, 2, 1, 3)
MIB = 1 << 20


def params(mib):
    return pltpu.CompilerParams(vmem_limit_bytes=mib * MIB)


def cost(flops, nbytes):
    return pl.CostEstimate(flops=flops, bytes_accessed=nbytes, transcendentals=0)


def dot(a, b, dims):
    return lax.dot_general(a, b, dims, preferred_element_type=F32)


def in_hbm(x):
    return pltpu.with_memory_space_constraint(x, pltpu.HBM)


def pick_kernel(chunk, table, features, out, held, sems):
    slots = out.shape[0]
    load = pltpu.make_async_copy(features.at[:, pl.ds(chunk * BLK, BLK)], held, sems.at[0])
    load.start()
    load.wait()

    @pl.loop(0, slots, unroll=8)
    def _(k):
        rows = pl.ds(pl.multiple_of(table[k] * BLK, BLK), BLK)
        pltpu.make_async_copy(held.at[rows], out.at[k], sems.at[1]).start()

    pltpu.make_async_copy(out, out, sems.at[1]).wait()


def pick(features, table, chunk):
    slots = table.shape[0]
    return pl.pallas_call(
        functools.partial(pick_kernel, chunk),
        grid_spec=pltpu.PrefetchScalarGridSpec(
            num_scalar_prefetch=1,
            grid=(),
            in_specs=[pl.BlockSpec(memory_space=pltpu.HBM)],
            out_specs=pl.BlockSpec(memory_space=pltpu.HBM),
            scratch_shapes=[
                pltpu.VMEM((features.shape[0], BLK), BF16),
                pltpu.SemaphoreType.DMA((2,)),
            ],
        ),
        out_shape=pltpu.HBM((slots, BLK, BLK), BF16),
        compiler_params=params(63),
        cost_estimate=cost(0, 4 * MIB),
        name="pick",
    )(table, in_hbm(features))


def agg_kernel(which, chunk, nfeat, src, counts, me, arrived, tiles_hbm, features, *refs):
    n = len(which)
    outs, tiles, own, (sems, *held) = refs[:n], refs[n : 2 * n], refs[2 * n : 3 * n], refs[3 * n :]
    per = tiles[0].shape[1]
    group = tiles_hbm.shape[0] // nfeat
    moves = []
    if held:
        moves.append(pltpu.make_async_copy(arrived, held[0], sems.at[2 * n]))
        arrived = held[0]
    firsts = [lax.rem(me[0] + k, nfeat) * group + low for k, low, _ in which]
    pairs = []
    for i, (first, (_, low, high)) in enumerate(zip(firsts, which)):
        rows = pl.ds(pl.multiple_of(first * BLK, BLK), (high - low) * BLK)
        tiles_move = pltpu.make_async_copy(
            tiles_hbm.at[pl.ds(first, high - low)], tiles[i], sems.at[2 * i]
        )
        own_move = pltpu.make_async_copy(
            features.at[rows, pl.ds(chunk * BLK, BLK)], own[i], sems.at[2 * i + 1]
        )
        pairs.append((tiles_move, own_move))
    for move in moves + [move for pair in pairs for move in pair]:
        move.start()
    for move in moves:
        move.wait()
    for i, (first, out, (_, low, high)) in enumerate(zip(firsts, outs, which)):
        for move in pairs[i]:
            move.wait()
        for b in range(high - low):
            rows, weights = [], []
            for t in range(per):
                slot = src[(first + b) * per + t]
                live = lax.rem(slot, 2) < counts[lax.div(slot, 2)]
                rows.append(arrived[slot])
                weights.append(tiles[i][b, t] * jnp.where(live, 1.0, 0.0).astype(BF16))
            total = dot(jnp.concatenate(weights, 1), jnp.concatenate(rows, 0), NN)
            at = pl.ds(b * BLK, BLK)
            out[at, :] = (own[i][at, :].astype(F32) + total).astype(BF16)


def aggregate(src, counts, me, arrived, tiles, features, chunk, nfeat, which):
    nblocks, per = tiles.shape[:2]
    group = nblocks // nfeat
    which = [k if isinstance(k, tuple) else (k, 0, group) for k in which]
    sizes = [high - low for _, low, high in which]
    hbm = pl.BlockSpec(memory_space=pltpu.HBM)
    vmem = pl.BlockSpec(memory_space=pltpu.VMEM)
    load = chunk == 0
    return pl.pallas_call(
        functools.partial(agg_kernel, which, chunk, nfeat),
        grid_spec=pltpu.PrefetchScalarGridSpec(
            num_scalar_prefetch=3,
            grid=(),
            in_specs=[pl.BlockSpec(memory_space=pl.ANY) if load else vmem, hbm, hbm],
            out_specs=[vmem] * len(which),
            scratch_shapes=[pltpu.VMEM((n, per, BLK, BLK), BF16) for n in sizes]
            + [pltpu.VMEM((n * BLK, BLK), BF16) for n in sizes]
            + [pltpu.SemaphoreType.DMA((1 + 2 * len(which),))]
            + [pltpu.VMEM(arrived.shape, BF16)] * load,
        ),
        out_shape=[jax.ShapeDtypeStruct((n * BLK, BLK), BF16) for n in sizes],
        compiler_params=params(14),
        cost_estimate=cost(sum(sizes) * per * 2 * BLK**3, 8 * MIB),
        name="aggregate",
    )(src, counts, me, arrived, in_hbm(tiles), in_hbm(features))


def assemble_kernel(me, *refs):
    flats, (weights, second_t, second, bias, consts) = refs[:4], refs[4:]
    hid, grades = second.shape
    width = flats[0].shape[1]
    consts[...] = jnp.zeros_like(consts)
    for i, k in enumerate(ORDER):
        weights[:, i * width : (i + 1) * width] = flats[i][pl.ds(0, hid), :]
        owner = lax.rem(me[0] + len(ORDER) - k, len(ORDER))
        lanes = pl.ds(pl.multiple_of(owner * width, width), width)
        tail = flats[i][pl.ds(hid, 2 * grades), :].astype(F32)
        consts[pl.ds(0, grades), lanes] = tail[:grades]
        b = (tail[grades : grades + 1] + tail[grades + 1 : grades + 2]) + tail[
            grades + 2 : grades + 3
        ]
        consts[pl.ds(grades, 8), lanes] = jnp.broadcast_to(b, (8, width))
    second_t[...] = consts[pl.ds(0, grades), :].astype(BF16)
    turned = consts[...].T
    second[...] = turned[:, :grades].astype(BF16)
    bias[...] = turned[:, grades : grades + 1]


def assemble(me, flats, hid, grades):
    vmem = pl.BlockSpec(memory_space=pltpu.VMEM)
    return pl.pallas_call(
        assemble_kernel,
        grid_spec=pltpu.PrefetchScalarGridSpec(
            num_scalar_prefetch=1,
            grid=(),
            in_specs=[vmem] * 4,
            out_specs=[vmem] * 4,
            scratch_shapes=[pltpu.VMEM((BLK, hid), F32)],
        ),
        out_shape=[
            jax.ShapeDtypeStruct((hid, hid), BF16),
            jax.ShapeDtypeStruct((grades, hid), BF16),
            jax.ShapeDtypeStruct((hid, grades), BF16),
            jax.ShapeDtypeStruct((hid, 1), F32),
        ],
        compiler_params=params(16),
        cost_estimate=cost(0, 5 * MIB),
        name="assemble",
    )(me, *flats)


def dense_kernel(nfeat, *refs):
    pieces, (weights, bias, second, hidden, proj) = refs[: 2 * nfeat + 1], refs[2 * nfeat + 1 :]
    first, (own, low, high, *others) = pieces[:nfeat], pieces[nfeat:]
    half = jnp.where(pl.program_id(0) == 0, low[...], high[...])
    last = [own[...], half] + [piece[...] for piece in others]
    order = [x for k in range(nfeat) for x in (first[k][...], last[k])]
    pre = dot(weights[...], jnp.concatenate(order, 1), NT)
    hid = jnp.maximum(pre + bias[...], 0.0).astype(BF16)
    hidden[...] = hid
    out = dot(second[...], hid, NN)
    for b in range(proj.shape[0]):
        proj[b] = out[:, b * BLK : (b + 1) * BLK]


def dense(pieces, weights, bias, second):
    nodes, nfeat = pieces[0].shape[0], len(pieces) // 2
    hid, width = weights.shape
    grades = second.shape[0]
    step = nodes // 2
    return pl.pallas_call(
        functools.partial(dense_kernel, nfeat),
        grid=(2,),
        in_specs=[
            pl.BlockSpec((step, BLK), lambda g, n=piece.shape[0]: (g * (n // nodes), 0))
            for piece in pieces
        ]
        + [
            pl.BlockSpec((hid, width), lambda g: (0, 0)),
            pl.BlockSpec((hid, 1), lambda g: (0, 0)),
            pl.BlockSpec((grades, hid), lambda g: (0, 0)),
        ],
        out_specs=[
            pl.BlockSpec((hid, step), lambda g: (0, g)),
            pl.BlockSpec((step // BLK, grades, BLK), lambda g: (g, 0, 0)),
        ],
        out_shape=[
            jax.ShapeDtypeStruct((hid, nodes), BF16),
            jax.ShapeDtypeStruct((nodes // BLK, grades, BLK), F32),
        ],
        compiler_params=params(20),
        cost_estimate=cost(2 * nodes * hid * width, 7 * MIB),
        name="dense",
    )(*pieces, weights, bias, second)


def spread_kernel(table, me, p0, p1, p2, p3, whole, out):
    nfeat, group = 4, p0.shape[0]
    for k, piece in enumerate((p0, p1, p2, p3)):
        owner = lax.rem(me[0] + nfeat - k, nfeat)
        whole[pl.ds(owner * group, group)] = piece[...]

    @pl.loop(0, out.shape[0], unroll=8)
    def _(k):
        out[k] = whole[table[k]]


def spread(table, me, pieces):
    group, grades, _ = pieces[0].shape
    slots = table.shape[0]
    vmem = pl.BlockSpec(memory_space=pltpu.VMEM)
    return pl.pallas_call(
        spread_kernel,
        grid_spec=pltpu.PrefetchScalarGridSpec(
            num_scalar_prefetch=2,
            grid=(),
            in_specs=[vmem] * 4,
            out_specs=[vmem] * 2,
        ),
        out_shape=[
            jax.ShapeDtypeStruct((group * 4, grades, BLK), F32),
            jax.ShapeDtypeStruct((slots, grades, BLK), F32),
        ],
        compiler_params=params(4),
        cost_estimate=cost(0, MIB),
        name="spread",
    )(table, me, *pieces)


def logits_kernel(
    scale, src, counts, me, arrived, own, labels, tiles, dlog_out, slots_out, parts, field, grad_b, sums
):
    nblocks, per = tiles.shape[:2]
    nslots, grades, _ = arrived.shape
    mine = dlog_out.shape[0]

    def live_of(slot):
        return jnp.where(lax.rem(slot, 2) < counts[lax.div(slot, 2)], 1.0, 0.0)

    x = arrived[...]
    for i in range(3):
        y = x.astype(BF16)
        parts[:, i * grades : (i + 1) * grades, :] = y
        x = x - y.astype(F32)

    @pl.loop(0, nblocks, unroll=8)
    def _(b):
        rows, weights = [], []
        for t in range(per):
            slot = src[b * per + t]
            rows.append(parts[slot] * live_of(slot).astype(BF16))
            weights.append(tiles[b, t])
        triple = dot(jnp.concatenate(rows, 1), jnp.concatenate(weights, 1), NT)
        field[b] = own[b] + (
            triple[:grades] + (triple[grades : 2 * grades] + triple[2 * grades :])
        )

    expo = jnp.exp(field[...])
    probs = expo / jnp.sum(expo, axis=1, keepdims=True)
    grade = lax.broadcasted_iota(jnp.int32, field.shape, 1)
    onehot = jnp.where(labels[...] == grade, 1.0, 0.0)
    dlog = (probs - onehot) * scale
    field[...] = dlog
    grad_b[...] = dlog.astype(BF16)
    dlog_out[...] = field[pl.ds(me[0] * mine, mine)]
    sums[...] = jnp.zeros_like(sums)

    @pl.loop(0, nblocks, unroll=8)
    def _(b):
        back = dot(grad_b[b], jnp.concatenate([tiles[b, t] for t in range(per)], 1), NN)
        for t in range(per):
            slot = src[b * per + t]
            sums[slot] += back[:, t * BLK : (t + 1) * BLK] * live_of(slot)

    slots_out[...] = sums[...].astype(BF16)


def logits_back(src, counts, me, arrived, own, labels, tiles, scale, nfeat):
    nblocks, per = tiles.shape[:2]
    nslots, grades, _ = arrived.shape
    vmem = pl.BlockSpec(memory_space=pltpu.VMEM)
    return pl.pallas_call(
        functools.partial(logits_kernel, scale),
        grid_spec=pltpu.PrefetchScalarGridSpec(
            num_scalar_prefetch=3,
            grid=(),
            in_specs=[vmem] * 4,
            out_specs=[vmem] * 2,
            scratch_shapes=[
                pltpu.VMEM((nslots, 3 * grades, BLK), BF16),
                pltpu.VMEM((nblocks, grades, BLK), F32),
                pltpu.VMEM((nblocks, grades, BLK), BF16),
                pltpu.VMEM(arrived.shape, F32),
            ],
        ),
        out_shape=[
            jax.ShapeDtypeStruct((nblocks // nfeat, grades, BLK), F32),
            jax.ShapeDtypeStruct(arrived.shape, BF16),
        ],
        compiler_params=params(8),
        cost_estimate=cost(nblocks * per * 2 * 64 * BLK**2, 6 * MIB),
        name="logits",
    )(src, counts, me, arrived, own, labels, tiles)


def small_kernel(table, me, returned, dlog, hidden, second, dpre_out, small, total, dproj):
    group, grades, _ = dlog.shape
    width = hidden.shape[0]

    @pl.when(pl.program_id(0) == 0)
    def _():
        total[pl.ds(0, group)] = dlog[...]

        @pl.loop(0, returned.shape[0], unroll=8)
        def _(k):
            at = table[k] - me[0] * group
            at = jnp.where((at >= 0) & (at < group), at, group)
            total[at] += returned[k].astype(F32)

        for b in range(group):
            dproj[:, b * BLK : (b + 1) * BLK] = total[b].astype(BF16)

    active = hidden[...]
    dproj_b = dproj[...]
    dpre = jnp.where(active > 0, dot(second[...], dproj_b, NN), 0.0)
    dpre_out[...] = dpre.astype(BF16)
    small[pl.ds(0, grades), :] = dot(dproj_b, active, NT)
    part = dpre[:, :BLK]
    for i in range(1, dpre.shape[1] // BLK):
        part += dpre[:, i * BLK : (i + 1) * BLK]
    small[pl.ds(grades, 8), :] = jnp.broadcast_to(
        jnp.sum(part.T, axis=0, keepdims=True), (8, width)
    )


def small_gradients(table, me, returned, dlog, hidden, second, nfeat):
    hid, nodes = hidden.shape
    group, grades, _ = dlog.shape
    width = hid // nfeat
    whole3 = lambda g, t, m: (0, 0, 0)
    return pl.pallas_call(
        small_kernel,
        grid_spec=pltpu.PrefetchScalarGridSpec(
            num_scalar_prefetch=2,
            grid=(nfeat,),
            in_specs=[
                pl.BlockSpec(returned.shape, whole3),
                pl.BlockSpec(dlog.shape, whole3),
                pl.BlockSpec((width, nodes), lambda g, t, m: (g, 0)),
                pl.BlockSpec((width, grades), lambda g, t, m: (g, 0)),
            ],
            out_specs=[
                pl.BlockSpec((width, nodes), lambda g, t, m: (g, 0)),
                pl.BlockSpec((grades + 8, width), lambda g, t, m: (0, g)),
            ],
            scratch_shapes=[
                pltpu.VMEM((group + 1, grades, BLK), F32),
                pltpu.VMEM((grades, nodes), BF16),
            ],
        ),
        out_shape=[
            pltpu.HBM((hid, nodes), BF16),
            jax.ShapeDtypeStruct((grades + 8, hid), F32),
        ],
        compiler_params=params(16),
        cost_estimate=cost(2 * nodes * hid * 256, 4 * MIB),
        name="small_gradients",
    )(table, me, returned, dlog, hidden, second)


def big_kernel(me, side, dpre, *refs):
    pieces, out = refs[:-1], refs[-1]
    nfeat = len(pieces) // 2
    rows = dpre[...].reshape(-1, dpre.shape[-1])
    first, (own, low, high, *others) = pieces[:nfeat], pieces[nfeat:]
    middle = jnp.concatenate([low[...], high[...]], 0)
    last = [own[...], middle] + [piece[...] for piece in others]
    for i, k in enumerate(ORDER):
        owner = lax.rem(me[0] + nfeat - k, nfeat)
        both = jnp.concatenate([first[i][...], last[i]], 1)
        grad = dot(rows, both, NN).astype(BF16)
        out[:, owner] = grad.reshape(out.shape[0], out.shape[2], out.shape[3])


def big_gradient(me, side, dpre, pieces, parts):
    nfeat = len(pieces) // 2
    hid, nodes = dpre.shape
    cols = hid // parts
    vmem = pl.BlockSpec(memory_space=pltpu.VMEM)
    return pl.pallas_call(
        big_kernel,
        grid_spec=pltpu.PrefetchScalarGridSpec(
            num_scalar_prefetch=2,
            grid=(1,),
            in_specs=[
                pl.BlockSpec((parts // 2, 1, cols, nodes), lambda g, m, s: (0, s[0], 0, 0))
            ]
            + [vmem] * len(pieces),
            out_specs=pl.BlockSpec(
                (parts // 2, nfeat, cols, 2 * BLK), lambda g, m, s: (0, 0, 0, 0)
            ),
        ),
        out_shape=jax.ShapeDtypeStruct((parts // 2, nfeat, cols, 2 * BLK), BF16),
        compiler_params=params(16),
        cost_estimate=cost(nodes * hid * hid, 4 * MIB),
        name="big_gradient",
    )(me, side, in_hbm(dpre.reshape(parts // 2, 2, cols, nodes)), *pieces)


def join_kernel(side, a, b, small, other, out):
    width = a.shape[3]
    more = out.shape[2] - a.shape[2]
    both = small[...] + other[...]
    near = both.astype(BF16).astype(F32)
    rest = both - near
    second = jnp.concatenate(
        [near[more : more + 1], rest[more : more + 1], rest[: more - 2]], 0
    )
    kept = jnp.where(side[0] == 0, near[:more], second)
    for f in range(a.shape[1]):
        share = kept[:, f * width : (f + 1) * width]
        for p in range(a.shape[0]):
            grad = a[p, f].astype(F32) + b[p, f].astype(F32)
            out[p, f] = jnp.concatenate([grad, share], 0).astype(BF16)


def join(side, a, b, small, other):
    steps = 4
    lead, nfeat, rows, width = a.shape
    more = small.shape[0] - 8
    spec = lambda n: pl.BlockSpec((lead // steps, nfeat, n, width), lambda g, s: (g, 0, 0, 0))
    whole = pl.BlockSpec(small.shape, lambda g, s: (0, 0))
    return pl.pallas_call(
        join_kernel,
        grid_spec=pltpu.PrefetchScalarGridSpec(
            num_scalar_prefetch=1,
            grid=(steps,),
            in_specs=[spec(rows), spec(rows), whole, whole],
            out_specs=spec(rows + more),
        ),
        out_shape=pltpu.HBM((lead, nfeat, rows + more, width), BF16),
        compiler_params=params(8),
        cost_estimate=cost(a.size, 4 * MIB),
        name="join",
    )(side, a, b, small, other)


def total_kernel(arrived, out, small, acc):
    g = pl.program_id(0)
    rows = out.shape[0]

    @pl.when(g == 0)
    def _():
        acc[...] = jnp.zeros_like(acc)

    total = arrived[0].astype(F32)
    for i in range(1, arrived.shape[0]):
        total += arrived[i].astype(F32)
    acc[...] += total

    @pl.when(g == pl.num_programs(0) - 1)
    def _():
        out[...] = acc[pl.ds(0, rows), :]
        small[...] = acc[pl.ds(rows, small.shape[0]), :]


def total(arrived, rows):
    n, full, width = arrived.shape
    step = n // 8
    shapes = [(rows, width), (full - rows, width)]
    return pl.pallas_call(
        total_kernel,
        grid=(n // step,),
        in_specs=[pl.BlockSpec((step, full, width), lambda g: (g, 0, 0))],
        out_specs=[pl.BlockSpec(shape, lambda g: (0, 0)) for shape in shapes],
        out_shape=[jax.ShapeDtypeStruct(shape, F32) for shape in shapes],
        scratch_shapes=[pltpu.VMEM((full, width), F32)],
        compiler_params=params(8),
        cost_estimate=cost(0, 2 * MIB),
        name="total",
    )(arrived)


def finish_kernel(side, a, b, second, bias):
    first = side[0] == 0
    near = jnp.where(first, a[...], b[...])
    rest = jnp.where(first, b[...], a[...])
    second[...] = near + jnp.concatenate([rest[2:], jnp.zeros_like(rest[:2])], 0)
    bias[...] = rest[:1] + rest[1:2]


def finish(side, a, b):
    vmem = pl.BlockSpec(memory_space=pltpu.VMEM)
    return pl.pallas_call(
        finish_kernel,
        grid_spec=pltpu.PrefetchScalarGridSpec(
            num_scalar_prefetch=1,
            grid=(),
            in_specs=[vmem] * 2,
            out_specs=[vmem] * 2,
        ),
        out_shape=[
            jax.ShapeDtypeStruct(a.shape, F32),
            jax.ShapeDtypeStruct((1, a.shape[1]), F32),
        ],
        compiler_params=params(2),
        cost_estimate=cost(0, MIB // 8),
        name="finish",
    )(side, a, b)


def shards(features, pair_count, send_blocks, tile_src, tiles, labels, w_first, b_first, w_second):
    nblocks = tile_src.shape[0]
    parts = lax.axis_size("nodes")
    nfeat = lax.axis_size("feat")
    slots = send_blocks.shape[2]
    grades = w_second.shape[1]
    hid = w_first.shape[1]
    axis = lax.axis_index("feat").astype(jnp.int32)
    me = axis.reshape(1)
    table = send_blocks.reshape(parts * slots)
    src = tile_src.reshape(-1)
    counts = pair_count.reshape(-1)

    def ahead(x, k):
        return lax.ppermute(x, "feat", [(i, (i + k) % nfeat) for i in range(nfeat)])

    def nearby(x):
        return lax.ppermute(x, "nodes", [(i, i ^ 1) for i in range(parts)])

    def swap(x):
        shaped = x.reshape(parts, slots, *x.shape[1:])
        moved = lax.all_to_all(shaped, "nodes", split_axis=0, concat_axis=0, tiled=True)
        return moved.reshape(x.shape)

    arrived = [swap(pick(features, table, 0))]
    send = pick(features, table, 1)

    high = lax.reduce_precision(b_first, 8, 7)
    middle = lax.reduce_precision(b_first - high, 8, 7)
    split = jnp.stack([high, middle, (b_first - high) - middle]).astype(BF16)
    flat = jnp.concatenate(
        [w_first.T, w_second.T, jnp.pad(split, ((0, grades - 3), (0, 0)))], 0
    )
    flats = [ahead(flat, k) for k in (2, 1, 3)]
    send, flats, arrived = lax.optimization_barrier((send, flats, arrived))
    arrived.append(swap(send))
    others = (2, 1, 3)
    make = functools.partial(aggregate, src, counts, me)
    *sent, own = make(arrived[0], tiles, features, 0, nfeat, others + (0,))
    first = [own] + [ahead(piece, k) for k, piece in zip(others, sent)]
    core = (lax.axis_index("nodes").astype(jnp.int32) % 2).reshape(1)
    flats, here, there, first[0] = lax.optimization_barrier(
        (flats, core, 1 - core, first[0])
    )
    weights, second_t, second, bias = assemble(me, [flat] + flats, hid, grades)
    arrived[1], weights, second_t, bias, second, first = lax.optimization_barrier(
        (arrived[1], weights, second_t, bias, second, first)
    )
    far = nblocks // nfeat // 2
    high, low, one, three = make(
        arrived[1], tiles, features, 1, nfeat, ((2, far, 2 * far), (2, 0, far), 1, 3)
    )
    high = ahead(high, 3)
    last = list(make(arrived[1], tiles, features, 1, nfeat, (0,)))
    last += [ahead(low, 2), ahead(high, 3), ahead(one, 1), ahead(three, 3)]
    hidden, proj = dense(first + last, weights, bias, second_t)

    projs = [proj] + [ahead(proj, k) for k in range(1, nfeat)]
    own, send = spread(table, me, projs)
    scale = 1.0 / math.sqrt(nblocks * BLK * parts)
    dlog, slotsum = logits_back(
        src, counts, me, swap(send), own, labels.reshape(nblocks, 1, BLK), tiles, scale, nfeat
    )
    dpre, small = small_gradients(table, me, swap(slotsum), dlog, hidden, second, nfeat)
    away = nearby(big_gradient(me, there, dpre, first + last, parts))
    big = big_gradient(me, here, dpre, first + last, parts)
    big = join(here, big, away, small, nearby(small))
    moved = lax.all_to_all(
        big.reshape(parts // 2 * nfeat, *big.shape[2:]),
        ("nodes", "feat"),
        split_axis=0,
        concat_axis=0,
        axis_index_groups=[
            [p * nfeat + f for p in range(c, parts, 2) for f in range(nfeat)] for c in range(2)
        ],
        tiled=True,
    )
    grad_first, rest = total(moved, hid // parts)
    grad_second, grad_bias = finish(here, rest, nearby(rest))
    return grad_first.T, grad_bias.reshape(-1), grad_second.T


def solution(mesh):
    placed = (
        P("nodes", "feat"),
        P("nodes", None),
        P("nodes", None, None),
        P("nodes", None),
        P("nodes", None, None, None),
        P("nodes"),
        P("feat", None),
        P("feat"),
        P("feat", None),
    )
    return jax.shard_map(
        shards,
        mesh=mesh,
        in_specs=placed,
        out_specs=(P("feat", "nodes"), P("feat"), P("feat", None)),
        check_vma=False,
    )
```

```python
import functools
import math

import jax
import jax.numpy as jnp
from jax import lax
from jax.experimental import pallas as pl
from jax.experimental.pallas import tpu as pltpu
from jax.sharding import PartitionSpec as P

F32 = jnp.float32
BF16 = jnp.bfloat16
NT = (((1,), (1,)), ((), ()))
NN = (((1,), (0,)), ((), ()))
BLK = 128
ORDER = (0, 2, 1, 3)
MIB = 1 << 20


def params(mib):
    return pltpu.CompilerParams(vmem_limit_bytes=mib * MIB)


def cost(flops, nbytes):
    return pl.CostEstimate(flops=flops, bytes_accessed=nbytes, transcendentals=0)


def dot(a, b, dims):
    return lax.dot_general(a, b, dims, preferred_element_type=F32)


def in_hbm(x):
    return pltpu.with_memory_space_constraint(x, pltpu.HBM)


def pick_kernel(chunk, table, features, out, held, sems):
    slots = out.shape[0]
    load = pltpu.make_async_copy(features.at[:, pl.ds(chunk * BLK, BLK)], held, sems.at[0])
    load.start()
    load.wait()

    @pl.loop(0, slots, unroll=8)
    def _(k):
        rows = pl.ds(pl.multiple_of(table[k] * BLK, BLK), BLK)
        pltpu.make_async_copy(held.at[rows], out.at[k], sems.at[1]).start()

    pltpu.make_async_copy(out, out, sems.at[1]).wait()


def pick(features, table, chunk):
    slots = table.shape[0]
    return pl.pallas_call(
        functools.partial(pick_kernel, chunk),
        grid_spec=pltpu.PrefetchScalarGridSpec(
            num_scalar_prefetch=1,
            grid=(),
            in_specs=[pl.BlockSpec(memory_space=pltpu.HBM)],
            out_specs=pl.BlockSpec(memory_space=pltpu.HBM),
            scratch_shapes=[
                pltpu.VMEM((features.shape[0], BLK), BF16),
                pltpu.SemaphoreType.DMA((2,)),
            ],
        ),
        out_shape=pltpu.HBM((slots, BLK, BLK), BF16),
        compiler_params=params(63),
        cost_estimate=cost(0, 4 * MIB),
        name="pick",
    )(table, in_hbm(features))


def agg_kernel(which, chunk, nfeat, src, counts, me, arrived, tiles_hbm, features, *refs):
    outs, (tiles, own, sems, *held) = refs[: len(which)], refs[len(which) :]
    group, per = tiles.shape[1:3]
    moves = []
    if held:
        moves.append(pltpu.make_async_copy(arrived, held[0], sems.at[2 * len(which)]))
        arrived = held[0]
    firsts = [lax.rem(me[0] + k, nfeat) * group for k in which]
    pairs = []
    for i, first in enumerate(firsts):
        rows = pl.ds(pl.multiple_of(first * BLK, BLK), group * BLK)
        tiles_move = pltpu.make_async_copy(
            tiles_hbm.at[pl.ds(first, group)], tiles.at[i], sems.at[2 * i]
        )
        own_move = pltpu.make_async_copy(
            features.at[rows, pl.ds(chunk * BLK, BLK)], own.at[i], sems.at[2 * i + 1]
        )
        pairs.append((tiles_move, own_move))
    for move in moves + [move for pair in pairs for move in pair]:
        move.start()
    for move in moves:
        move.wait()
    for i, (first, out) in enumerate(zip(firsts, outs)):
        for move in pairs[i]:
            move.wait()
        for b in range(group):
            rows, weights = [], []
            for t in range(per):
                slot = src[(first + b) * per + t]
                live = lax.rem(slot, 2) < counts[lax.div(slot, 2)]
                rows.append(arrived[slot])
                weights.append(tiles[i, b, t] * jnp.where(live, 1.0, 0.0).astype(BF16))
            total = dot(jnp.concatenate(weights, 1), jnp.concatenate(rows, 0), NN)
            at = pl.ds(b * BLK, BLK)
            out[at, :] = (own[i, at, :].astype(F32) + total).astype(BF16)


def aggregate(src, counts, me, arrived, tiles, features, chunk, nfeat, which):
    nblocks, per = tiles.shape[:2]
    group = nblocks // nfeat
    piece = jax.ShapeDtypeStruct((group * BLK, BLK), BF16)
    hbm = pl.BlockSpec(memory_space=pltpu.HBM)
    vmem = pl.BlockSpec(memory_space=pltpu.VMEM)
    load = chunk == 0
    return pl.pallas_call(
        functools.partial(agg_kernel, which, chunk, nfeat),
        grid_spec=pltpu.PrefetchScalarGridSpec(
            num_scalar_prefetch=3,
            grid=(),
            in_specs=[pl.BlockSpec(memory_space=pl.ANY) if load else vmem, hbm, hbm],
            out_specs=[vmem] * len(which),
            scratch_shapes=[
                pltpu.VMEM((len(which), group, per, BLK, BLK), BF16),
                pltpu.VMEM((len(which), group * BLK, BLK), BF16),
                pltpu.SemaphoreType.DMA((1 + 2 * len(which),)),
            ]
            + [pltpu.VMEM(arrived.shape, BF16)] * load,
        ),
        out_shape=[piece] * len(which),
        compiler_params=params(14),
        cost_estimate=cost(len(which) * group * per * 2 * BLK**3, 8 * MIB),
        name="aggregate",
    )(src, counts, me, arrived, in_hbm(tiles), in_hbm(features))


def assemble_kernel(me, *refs):
    flats, (weights, second_t, second, bias, consts) = refs[:4], refs[4:]
    hid, grades = second.shape
    width = flats[0].shape[1]
    consts[...] = jnp.zeros_like(consts)
    for i, k in enumerate(ORDER):
        weights[:, i * width : (i + 1) * width] = flats[i][pl.ds(0, hid), :]
        owner = lax.rem(me[0] + len(ORDER) - k, len(ORDER))
        lanes = pl.ds(pl.multiple_of(owner * width, width), width)
        tail = flats[i][pl.ds(hid, 2 * grades), :].astype(F32)
        consts[pl.ds(0, grades), lanes] = tail[:grades]
        b = (tail[grades : grades + 1] + tail[grades + 1 : grades + 2]) + tail[
            grades + 2 : grades + 3
        ]
        consts[pl.ds(grades, 8), lanes] = jnp.broadcast_to(b, (8, width))
    second_t[...] = consts[pl.ds(0, grades), :].astype(BF16)
    turned = consts[...].T
    second[...] = turned[:, :grades].astype(BF16)
    bias[...] = turned[:, grades : grades + 1]


def assemble(me, flats, hid, grades):
    vmem = pl.BlockSpec(memory_space=pltpu.VMEM)
    return pl.pallas_call(
        assemble_kernel,
        grid_spec=pltpu.PrefetchScalarGridSpec(
            num_scalar_prefetch=1,
            grid=(),
            in_specs=[vmem] * 4,
            out_specs=[vmem] * 4,
            scratch_shapes=[pltpu.VMEM((BLK, hid), F32)],
        ),
        out_shape=[
            jax.ShapeDtypeStruct((hid, hid), BF16),
            jax.ShapeDtypeStruct((grades, hid), BF16),
            jax.ShapeDtypeStruct((hid, grades), BF16),
            jax.ShapeDtypeStruct((hid, 1), F32),
        ],
        compiler_params=params(16),
        cost_estimate=cost(0, 5 * MIB),
        name="assemble",
    )(me, *flats)


def dense_kernel(nfeat, *refs):
    pieces, (weights, bias, second, hidden, proj) = refs[: 2 * nfeat], refs[2 * nfeat :]
    order = [pieces[i * nfeat + k][...] for k in range(nfeat) for i in range(2)]
    pre = dot(weights[...], jnp.concatenate(order, 1), NT)
    hid = jnp.maximum(pre + bias[...], 0.0).astype(BF16)
    hidden[...] = hid
    out = dot(second[...], hid, NN)
    for b in range(proj.shape[0]):
        proj[b] = out[:, b * BLK : (b + 1) * BLK]


def dense(pieces, weights, bias, second):
    nodes, nfeat = pieces[0].shape[0], len(pieces) // 2
    hid, width = weights.shape
    grades = second.shape[0]
    step = 512
    return pl.pallas_call(
        functools.partial(dense_kernel, nfeat),
        grid=(nodes // step,),
        in_specs=[pl.BlockSpec((step, BLK), lambda g: (g, 0))] * (2 * nfeat)
        + [
            pl.BlockSpec((hid, width), lambda g: (0, 0)),
            pl.BlockSpec((hid, 1), lambda g: (0, 0)),
            pl.BlockSpec((grades, hid), lambda g: (0, 0)),
        ],
        out_specs=[
            pl.BlockSpec((hid, step), lambda g: (0, g)),
            pl.BlockSpec((step // BLK, grades, BLK), lambda g: (g, 0, 0)),
        ],
        out_shape=[
            jax.ShapeDtypeStruct((hid, nodes), BF16),
            jax.ShapeDtypeStruct((nodes // BLK, grades, BLK), F32),
        ],
        compiler_params=params(20),
        cost_estimate=cost(2 * nodes * hid * width, 7 * MIB),
        name="dense",
    )(*pieces, weights, bias, second)


def spread_kernel(table, me, p0, p1, p2, p3, whole, out):
    nfeat, group = 4, p0.shape[0]
    for k, piece in enumerate((p0, p1, p2, p3)):
        owner = lax.rem(me[0] + nfeat - k, nfeat)
        whole[pl.ds(owner * group, group)] = piece[...]

    @pl.loop(0, out.shape[0], unroll=8)
    def _(k):
        out[k] = whole[table[k]].astype(BF16)


def spread(table, me, pieces):
    group, grades, _ = pieces[0].shape
    slots = table.shape[0]
    vmem = pl.BlockSpec(memory_space=pltpu.VMEM)
    return pl.pallas_call(
        spread_kernel,
        grid_spec=pltpu.PrefetchScalarGridSpec(
            num_scalar_prefetch=2,
            grid=(),
            in_specs=[vmem] * 4,
            out_specs=[vmem] * 2,
        ),
        out_shape=[
            jax.ShapeDtypeStruct((group * 4, grades, BLK), F32),
            jax.ShapeDtypeStruct((slots, grades, BLK), BF16),
        ],
        compiler_params=params(4),
        cost_estimate=cost(0, MIB),
        name="spread",
    )(table, me, *pieces)


def logits_kernel(
    scale, src, counts, me, arrived, own, labels, tiles, dlog_out, slots_out, field, grad_b, sums
):
    nblocks, per = tiles.shape[:2]
    grades = arrived.shape[1]
    mine = dlog_out.shape[0]

    def live_of(slot):
        return jnp.where(lax.rem(slot, 2) < counts[lax.div(slot, 2)], 1.0, 0.0)

    @pl.loop(0, nblocks, unroll=8)
    def _(b):
        rows, weights = [], []
        for t in range(per):
            slot = src[b * per + t]
            rows.append(arrived[slot] * live_of(slot).astype(BF16))
            weights.append(tiles[b, t])
        field[b] = own[b] + dot(
            jnp.concatenate(rows, 1), jnp.concatenate(weights, 1), NT
        )

    expo = jnp.exp(field[...])
    probs = expo / jnp.sum(expo, axis=1, keepdims=True)
    grade = lax.broadcasted_iota(jnp.int32, field.shape, 1)
    onehot = jnp.where(labels[...] == grade, 1.0, 0.0)
    dlog = (probs - onehot) * scale
    field[...] = dlog
    grad_b[...] = dlog.astype(BF16)
    dlog_out[...] = field[pl.ds(me[0] * mine, mine)]
    sums[...] = jnp.zeros_like(sums)

    @pl.loop(0, nblocks, unroll=8)
    def _(b):
        back = dot(grad_b[b], jnp.concatenate([tiles[b, t] for t in range(per)], 1), NN)
        for t in range(per):
            slot = src[b * per + t]
            sums[slot] += back[:, t * BLK : (t + 1) * BLK] * live_of(slot)

    slots_out[...] = sums[...].astype(BF16)


def logits_back(src, counts, me, arrived, own, labels, tiles, scale, nfeat):
    nblocks, per = tiles.shape[:2]
    grades = arrived.shape[1]
    vmem = pl.BlockSpec(memory_space=pltpu.VMEM)
    return pl.pallas_call(
        functools.partial(logits_kernel, scale),
        grid_spec=pltpu.PrefetchScalarGridSpec(
            num_scalar_prefetch=3,
            grid=(),
            in_specs=[vmem] * 4,
            out_specs=[vmem] * 2,
            scratch_shapes=[
                pltpu.VMEM((nblocks, grades, BLK), F32),
                pltpu.VMEM((nblocks, grades, BLK), BF16),
                pltpu.VMEM(arrived.shape, F32),
            ],
        ),
        out_shape=[
            jax.ShapeDtypeStruct((nblocks // nfeat, grades, BLK), F32),
            jax.ShapeDtypeStruct(arrived.shape, BF16),
        ],
        compiler_params=params(8),
        cost_estimate=cost(nblocks * per * 2 * 64 * BLK**2, 6 * MIB),
        name="logits",
    )(src, counts, me, arrived, own, labels, tiles)


def small_kernel(table, me, returned, dlog, hidden, second, dpre_out, small, total, dproj):
    group, grades, _ = dlog.shape
    width = hidden.shape[0]

    @pl.when(pl.program_id(0) == 0)
    def _():
        total[pl.ds(0, group)] = dlog[...]

        @pl.loop(0, returned.shape[0], unroll=8)
        def _(k):
            at = table[k] - me[0] * group
            at = jnp.where((at >= 0) & (at < group), at, group)
            total[at] += returned[k].astype(F32)

        for b in range(group):
            dproj[:, b * BLK : (b + 1) * BLK] = total[b].astype(BF16)

    active = hidden[...]
    dproj_b = dproj[...]
    dpre = jnp.where(active > 0, dot(second[...], dproj_b, NN), 0.0)
    dpre_out[...] = dpre.astype(BF16)
    small[pl.ds(0, grades), :] = dot(dproj_b, active, NT)
    part = dpre[:, :BLK]
    for i in range(1, dpre.shape[1] // BLK):
        part += dpre[:, i * BLK : (i + 1) * BLK]
    small[pl.ds(grades, 8), :] = jnp.broadcast_to(
        jnp.sum(part.T, axis=0, keepdims=True), (8, width)
    )


def small_gradients(table, me, returned, dlog, hidden, second, steps):
    hid, nodes = hidden.shape
    group, grades, _ = dlog.shape
    width = hid // steps
    whole3 = lambda g, t, m: (0, 0, 0)
    return pl.pallas_call(
        small_kernel,
        grid_spec=pltpu.PrefetchScalarGridSpec(
            num_scalar_prefetch=2,
            grid=(steps,),
            in_specs=[
                pl.BlockSpec(returned.shape, whole3),
                pl.BlockSpec(dlog.shape, whole3),
                pl.BlockSpec((width, nodes), lambda g, t, m: (g, 0)),
                pl.BlockSpec((width, grades), lambda g, t, m: (g, 0)),
            ],
            out_specs=[
                pl.BlockSpec((width, nodes), lambda g, t, m: (g, 0)),
                pl.BlockSpec((grades + 8, width), lambda g, t, m: (0, g)),
            ],
            scratch_shapes=[
                pltpu.VMEM((group + 1, grades, BLK), F32),
                pltpu.VMEM((grades, nodes), BF16),
            ],
        ),
        out_shape=[
            pltpu.HBM((hid, nodes), BF16),
            jax.ShapeDtypeStruct((grades + 8, hid), F32),
        ],
        compiler_params=params(16),
        cost_estimate=cost(2 * nodes * hid * 256, 4 * MIB),
        name="small_gradients",
    )(table, me, returned, dlog, hidden, second)


def big_kernel(me, side, dpre, *refs):
    pieces, out = refs[:-1], refs[-1]
    nfeat = len(pieces) // 2
    rows = dpre[...].reshape(-1, dpre.shape[-1])
    for i, k in enumerate(ORDER):
        owner = lax.rem(me[0] + nfeat - k, nfeat)
        both = jnp.concatenate([pieces[i][...], pieces[nfeat + i][...]], 1)
        grad = dot(rows, both, NN).astype(BF16)
        out[:, owner] = grad.reshape(out.shape[0], out.shape[2], out.shape[3])


def big_gradient(me, side, dpre, pieces, parts):
    nfeat = len(pieces) // 2
    hid, nodes = dpre.shape
    cols = hid // parts
    vmem = pl.BlockSpec(memory_space=pltpu.VMEM)
    return pl.pallas_call(
        big_kernel,
        grid_spec=pltpu.PrefetchScalarGridSpec(
            num_scalar_prefetch=2,
            grid=(1,),
            in_specs=[
                pl.BlockSpec((parts // 2, 1, cols, nodes), lambda g, m, s: (0, s[0], 0, 0))
            ]
            + [vmem] * (2 * nfeat),
            out_specs=pl.BlockSpec(
                (parts // 2, nfeat, cols, 2 * BLK), lambda g, m, s: (0, 0, 0, 0)
            ),
        ),
        out_shape=jax.ShapeDtypeStruct((parts // 2, nfeat, cols, 2 * BLK), BF16),
        compiler_params=params(16),
        cost_estimate=cost(nodes * hid * hid, 4 * MIB),
        name="big_gradient",
    )(me, side, in_hbm(dpre.reshape(parts // 2, 2, cols, nodes)), *pieces)


def join_kernel(side, a, b, small, other, out):
    width = a.shape[3]
    more = out.shape[2] - a.shape[2]
    both = small[...] + other[...]
    near = both.astype(BF16).astype(F32)
    rest = both - near
    second = jnp.concatenate(
        [near[more : more + 1], rest[more : more + 1], rest[: more - 2]], 0
    )
    kept = jnp.where(side[0] == 0, near[:more], second)
    for f in range(a.shape[1]):
        share = kept[:, f * width : (f + 1) * width]
        for p in range(a.shape[0]):
            grad = a[p, f].astype(F32) + b[p, f].astype(F32)
            out[p, f] = jnp.concatenate([grad, share], 0).astype(BF16)


def join(side, a, b, small, other):
    steps = 4
    lead, nfeat, rows, width = a.shape
    more = small.shape[0] - 8
    spec = lambda n: pl.BlockSpec((lead // steps, nfeat, n, width), lambda g, s: (g, 0, 0, 0))
    whole = pl.BlockSpec(small.shape, lambda g, s: (0, 0))
    return pl.pallas_call(
        join_kernel,
        grid_spec=pltpu.PrefetchScalarGridSpec(
            num_scalar_prefetch=1,
            grid=(steps,),
            in_specs=[spec(rows), spec(rows), whole, whole],
            out_specs=spec(rows + more),
        ),
        out_shape=pltpu.HBM((lead, nfeat, rows + more, width), BF16),
        compiler_params=params(8),
        cost_estimate=cost(a.size, 4 * MIB),
        name="join",
    )(side, a, b, small, other)


def total_kernel(arrived, out, small, acc):
    g = pl.program_id(0)
    rows = out.shape[0]

    @pl.when(g == 0)
    def _():
        acc[...] = jnp.zeros_like(acc)

    total = arrived[0].astype(F32)
    for i in range(1, arrived.shape[0]):
        total += arrived[i].astype(F32)
    acc[...] += total

    @pl.when(g == pl.num_programs(0) - 1)
    def _():
        out[...] = acc[pl.ds(0, rows), :]
        small[...] = acc[pl.ds(rows, small.shape[0]), :]


def total(arrived, rows):
    n, full, width = arrived.shape
    step = n // 8
    shapes = [(rows, width), (full - rows, width)]
    return pl.pallas_call(
        total_kernel,
        grid=(n // step,),
        in_specs=[pl.BlockSpec((step, full, width), lambda g: (g, 0, 0))],
        out_specs=[pl.BlockSpec(shape, lambda g: (0, 0)) for shape in shapes],
        out_shape=[jax.ShapeDtypeStruct(shape, F32) for shape in shapes],
        scratch_shapes=[pltpu.VMEM((full, width), F32)],
        compiler_params=params(8),
        cost_estimate=cost(0, 2 * MIB),
        name="total",
    )(arrived)


def finish_kernel(side, a, b, second, bias):
    first = side[0] == 0
    near = jnp.where(first, a[...], b[...])
    rest = jnp.where(first, b[...], a[...])
    second[...] = near + jnp.concatenate([rest[2:], jnp.zeros_like(rest[:2])], 0)
    bias[...] = rest[:1] + rest[1:2]


def finish(side, a, b):
    vmem = pl.BlockSpec(memory_space=pltpu.VMEM)
    return pl.pallas_call(
        finish_kernel,
        grid_spec=pltpu.PrefetchScalarGridSpec(
            num_scalar_prefetch=1,
            grid=(),
            in_specs=[vmem] * 2,
            out_specs=[vmem] * 2,
        ),
        out_shape=[
            jax.ShapeDtypeStruct(a.shape, F32),
            jax.ShapeDtypeStruct((1, a.shape[1]), F32),
        ],
        compiler_params=params(2),
        cost_estimate=cost(0, MIB // 8),
        name="finish",
    )(side, a, b)


def shards(features, pair_count, send_blocks, tile_src, tiles, labels, w_first, b_first, w_second):
    nblocks = tile_src.shape[0]
    parts = lax.axis_size("nodes")
    nfeat = lax.axis_size("feat")
    slots = send_blocks.shape[2]
    grades = w_second.shape[1]
    hid = w_first.shape[1]
    axis = lax.axis_index("feat").astype(jnp.int32)
    me = axis.reshape(1)
    table = send_blocks.reshape(parts * slots)
    src = tile_src.reshape(-1)
    counts = pair_count.reshape(-1)

    def ahead(x, k):
        return lax.ppermute(x, "feat", [(i, (i + k) % nfeat) for i in range(nfeat)])

    def nearby(x):
        return lax.ppermute(x, "nodes", [(i, i ^ 1) for i in range(parts)])

    def swap(x):
        shaped = x.reshape(parts, slots, *x.shape[1:])
        moved = lax.all_to_all(shaped, "nodes", split_axis=0, concat_axis=0, tiled=True)
        return moved.reshape(x.shape)

    arrived = [swap(pick(features, table, 0))]
    send = pick(features, table, 1)

    high = lax.reduce_precision(b_first, 8, 7)
    middle = lax.reduce_precision(b_first - high, 8, 7)
    split = jnp.stack([high, middle, (b_first - high) - middle]).astype(BF16)
    flat = jnp.concatenate(
        [w_first.T, w_second.T, jnp.pad(split, ((0, grades - 3), (0, 0)))], 0
    )
    flats = [ahead(flat, k) for k in (2, 1, 3)]
    send, flats, arrived = lax.optimization_barrier((send, flats, arrived))
    arrived.append(swap(send))
    others = (2, 1, 3)
    make = functools.partial(aggregate, src, counts, me)
    *sent, own = make(arrived[0], tiles, features, 0, nfeat, others + (0,))
    first = [own] + [ahead(piece, k) for k, piece in zip(others, sent)]
    core = (lax.axis_index("nodes").astype(jnp.int32) % 2).reshape(1)
    flats, here, there, first[0] = lax.optimization_barrier(
        (flats, core, 1 - core, first[0])
    )
    weights, second_t, second, bias = assemble(me, [flat] + flats, hid, grades)
    arrived[1], weights, second_t, bias, second, first = lax.optimization_barrier(
        (arrived[1], weights, second_t, bias, second, first)
    )
    sent = make(arrived[1], tiles, features, 1, nfeat, others)
    last = list(make(arrived[1], tiles, features, 1, nfeat, (0,)))
    last += [ahead(piece, k) for k, piece in zip(others, sent)]
    hidden, proj = dense(first + last, weights, bias, second_t)

    projs = [proj] + [ahead(proj, k) for k in range(1, nfeat)]
    own, send = spread(table, me, projs)
    scale = 1.0 / math.sqrt(nblocks * BLK * parts)
    dlog, slotsum = logits_back(
        src, counts, me, swap(send), own, labels.reshape(nblocks, 1, BLK), tiles, scale, nfeat
    )
    dpre, small = small_gradients(table, me, swap(slotsum), dlog, hidden, second, 2)
    away = nearby(big_gradient(me, there, dpre, first + last, parts))
    big = big_gradient(me, here, dpre, first + last, parts)
    big = join(here, big, away, small, nearby(small))
    moved = lax.all_to_all(
        big.reshape(parts // 2 * nfeat, *big.shape[2:]),
        ("nodes", "feat"),
        split_axis=0,
        concat_axis=0,
        axis_index_groups=[
            [p * nfeat + f for p in range(c, parts, 2) for f in range(nfeat)] for c in range(2)
        ],
        tiled=True,
    )
    grad_first, rest = total(moved, hid // parts)
    grad_second, grad_bias = finish(here, rest, nearby(rest))
    return grad_first.T, grad_bias.reshape(-1), grad_second.T


def solution(mesh):
    placed = (
        P("nodes", "feat"),
        P("nodes", None),
        P("nodes", None, None),
        P("nodes", None),
        P("nodes", None, None, None),
        P("nodes"),
        P("feat", None),
        P("feat"),
        P("feat", None),
    )
    return jax.shard_map(
        shards,
        mesh=mesh,
        in_specs=placed,
        out_specs=(P("feat", "nodes"), P("feat"), P("feat", None)),
        check_vma=False,
    )
```

```python
import functools
import math

import jax
import jax.numpy as jnp
from jax import lax
from jax.experimental import pallas as pl
from jax.experimental.pallas import tpu as pltpu
from jax.sharding import PartitionSpec as P

F32 = jnp.float32
BF16 = jnp.bfloat16
NT = (((1,), (1,)), ((), ()))
NN = (((1,), (0,)), ((), ()))
BLK = 128
ORDER = (0, 2, 1, 3)
MIB = 1 << 20


def params(mib):
    return pltpu.CompilerParams(vmem_limit_bytes=mib * MIB)


def cost(flops, nbytes):
    return pl.CostEstimate(flops=flops, bytes_accessed=nbytes, transcendentals=0)


def dot(a, b, dims):
    return lax.dot_general(a, b, dims, preferred_element_type=F32)


def in_hbm(x):
    return pltpu.with_memory_space_constraint(x, pltpu.HBM)


def pick_kernel(chunk, table, features, out, held, sems):
    slots = out.shape[0]
    load = pltpu.make_async_copy(features.at[:, pl.ds(chunk * BLK, BLK)], held, sems.at[0])
    load.start()
    load.wait()

    @pl.loop(0, slots, unroll=8)
    def _(k):
        rows = pl.ds(pl.multiple_of(table[k] * BLK, BLK), BLK)
        pltpu.make_async_copy(held.at[rows], out.at[k], sems.at[1]).start()

    pltpu.make_async_copy(out, out, sems.at[1]).wait()


def pick(features, table, chunk):
    slots = table.shape[0]
    return pl.pallas_call(
        functools.partial(pick_kernel, chunk),
        grid_spec=pltpu.PrefetchScalarGridSpec(
            num_scalar_prefetch=1,
            grid=(),
            in_specs=[pl.BlockSpec(memory_space=pltpu.HBM)],
            out_specs=pl.BlockSpec(memory_space=pltpu.HBM),
            scratch_shapes=[
                pltpu.VMEM((features.shape[0], BLK), BF16),
                pltpu.SemaphoreType.DMA((2,)),
            ],
        ),
        out_shape=pltpu.HBM((slots, BLK, BLK), BF16),
        compiler_params=params(63),
        cost_estimate=cost(0, 4 * MIB),
        name="pick",
    )(table, in_hbm(features))


def agg_kernel(which, chunk, nfeat, src, counts, me, arrived, tiles_hbm, features, *refs):
    outs, (tiles, own, sems, *held) = refs[: len(which)], refs[len(which) :]
    group, per = tiles.shape[1:3]
    moves = []
    if held:
        moves.append(pltpu.make_async_copy(arrived, held[0], sems.at[2 * len(which)]))
        arrived = held[0]
    firsts = [lax.rem(me[0] + k, nfeat) * group for k in which]
    pairs = []
    for i, first in enumerate(firsts):
        rows = pl.ds(pl.multiple_of(first * BLK, BLK), group * BLK)
        tiles_move = pltpu.make_async_copy(
            tiles_hbm.at[pl.ds(first, group)], tiles.at[i], sems.at[2 * i]
        )
        own_move = pltpu.make_async_copy(
            features.at[rows, pl.ds(chunk * BLK, BLK)], own.at[i], sems.at[2 * i + 1]
        )
        pairs.append((tiles_move, own_move))
    for move in moves + [move for pair in pairs for move in pair]:
        move.start()
    for move in moves:
        move.wait()
    for i, (first, out) in enumerate(zip(firsts, outs)):
        for move in pairs[i]:
            move.wait()
        for b in range(group):
            rows, weights = [], []
            for t in range(per):
                slot = src[(first + b) * per + t]
                live = lax.rem(slot, 2) < counts[lax.div(slot, 2)]
                rows.append(arrived[slot])
                weights.append(tiles[i, b, t] * jnp.where(live, 1.0, 0.0).astype(BF16))
            total = dot(jnp.concatenate(weights, 1), jnp.concatenate(rows, 0), NN)
            at = pl.ds(b * BLK, BLK)
            out[at, :] = (own[i, at, :].astype(F32) + total).astype(BF16)


def aggregate(src, counts, me, arrived, tiles, features, chunk, nfeat, which):
    nblocks, per = tiles.shape[:2]
    group = nblocks // nfeat
    piece = jax.ShapeDtypeStruct((group * BLK, BLK), BF16)
    hbm = pl.BlockSpec(memory_space=pltpu.HBM)
    vmem = pl.BlockSpec(memory_space=pltpu.VMEM)
    load = chunk == 0
    return pl.pallas_call(
        functools.partial(agg_kernel, which, chunk, nfeat),
        grid_spec=pltpu.PrefetchScalarGridSpec(
            num_scalar_prefetch=3,
            grid=(),
            in_specs=[pl.BlockSpec(memory_space=pl.ANY) if load else vmem, hbm, hbm],
            out_specs=[vmem] * len(which),
            scratch_shapes=[
                pltpu.VMEM((len(which), group, per, BLK, BLK), BF16),
                pltpu.VMEM((len(which), group * BLK, BLK), BF16),
                pltpu.SemaphoreType.DMA((1 + 2 * len(which),)),
            ]
            + [pltpu.VMEM(arrived.shape, BF16)] * load,
        ),
        out_shape=[piece] * len(which),
        compiler_params=params(14),
        cost_estimate=cost(len(which) * group * per * 2 * BLK**3, 8 * MIB),
        name="aggregate",
    )(src, counts, me, arrived, in_hbm(tiles), in_hbm(features))


def assemble_kernel(me, *refs):
    flats, (weights, second_t, second, bias, consts) = refs[:4], refs[4:]
    hid, grades = second.shape
    width = flats[0].shape[1]
    consts[...] = jnp.zeros_like(consts)
    for i, k in enumerate(ORDER):
        weights[:, i * width : (i + 1) * width] = flats[i][pl.ds(0, hid), :]
        owner = lax.rem(me[0] + len(ORDER) - k, len(ORDER))
        lanes = pl.ds(pl.multiple_of(owner * width, width), width)
        tail = flats[i][pl.ds(hid, 2 * grades), :].astype(F32)
        consts[pl.ds(0, grades), lanes] = tail[:grades]
        b = (tail[grades : grades + 1] + tail[grades + 1 : grades + 2]) + tail[
            grades + 2 : grades + 3
        ]
        consts[pl.ds(grades, 8), lanes] = jnp.broadcast_to(b, (8, width))
    second_t[...] = consts[pl.ds(0, grades), :].astype(BF16)
    turned = consts[...].T
    second[...] = turned[:, :grades].astype(BF16)
    bias[...] = turned[:, grades : grades + 1]


def assemble(me, flats, hid, grades):
    vmem = pl.BlockSpec(memory_space=pltpu.VMEM)
    return pl.pallas_call(
        assemble_kernel,
        grid_spec=pltpu.PrefetchScalarGridSpec(
            num_scalar_prefetch=1,
            grid=(),
            in_specs=[vmem] * 4,
            out_specs=[vmem] * 4,
            scratch_shapes=[pltpu.VMEM((BLK, hid), F32)],
        ),
        out_shape=[
            jax.ShapeDtypeStruct((hid, hid), BF16),
            jax.ShapeDtypeStruct((grades, hid), BF16),
            jax.ShapeDtypeStruct((hid, grades), BF16),
            jax.ShapeDtypeStruct((hid, 1), F32),
        ],
        compiler_params=params(16),
        cost_estimate=cost(0, 5 * MIB),
        name="assemble",
    )(me, *flats)


def dense_kernel(nfeat, *refs):
    pieces, (weights, bias, second, hidden, proj) = refs[: 2 * nfeat], refs[2 * nfeat :]
    step = hidden.shape[1] // 2
    for half in range(2):
        rows = slice(half * step, (half + 1) * step)
        order = [pieces[i * nfeat + k][rows, :] for k in range(nfeat) for i in range(2)]
        pre = dot(weights[...], jnp.concatenate(order, 1), NT)
        hid = jnp.maximum(pre + bias[...], 0.0).astype(BF16)
        hidden[:, rows] = hid
        out = dot(second[...], hid, NN)
        for b in range(step // BLK):
            proj[half * (step // BLK) + b] = out[:, b * BLK : (b + 1) * BLK]


def dense(pieces, weights, bias, second):
    nodes, nfeat = pieces[0].shape[0], len(pieces) // 2
    hid, width = weights.shape
    grades = second.shape[0]
    vmem = pl.BlockSpec(memory_space=pltpu.VMEM)
    return pl.pallas_call(
        functools.partial(dense_kernel, nfeat),
        in_specs=[vmem] * (2 * nfeat + 3),
        out_specs=[vmem] * 2,
        out_shape=[
            jax.ShapeDtypeStruct((hid, nodes), BF16),
            jax.ShapeDtypeStruct((nodes // BLK, grades, BLK), F32),
        ],
        compiler_params=params(20),
        cost_estimate=cost(2 * nodes * hid * width, 7 * MIB),
        name="dense",
    )(*pieces, weights, bias, second)


def spread_kernel(table, me, p0, p1, p2, p3, whole, out):
    nfeat, group = 4, p0.shape[0]
    for k, piece in enumerate((p0, p1, p2, p3)):
        owner = lax.rem(me[0] + nfeat - k, nfeat)
        whole[pl.ds(owner * group, group)] = piece[...]

    @pl.loop(0, out.shape[0], unroll=8)
    def _(k):
        out[k] = whole[table[k]].astype(BF16)


def spread(table, me, pieces):
    group, grades, _ = pieces[0].shape
    slots = table.shape[0]
    vmem = pl.BlockSpec(memory_space=pltpu.VMEM)
    return pl.pallas_call(
        spread_kernel,
        grid_spec=pltpu.PrefetchScalarGridSpec(
            num_scalar_prefetch=2,
            grid=(),
            in_specs=[vmem] * 4,
            out_specs=[vmem] * 2,
        ),
        out_shape=[
            jax.ShapeDtypeStruct((group * 4, grades, BLK), F32),
            jax.ShapeDtypeStruct((slots, grades, BLK), BF16),
        ],
        compiler_params=params(4),
        cost_estimate=cost(0, MIB),
        name="spread",
    )(table, me, *pieces)


def logits_kernel(
    scale, src, counts, me, arrived, own, labels, tiles, dlog_out, slots_out, field, grad_b, sums
):
    nblocks, per = tiles.shape[:2]
    grades = arrived.shape[1]
    mine = dlog_out.shape[0]

    def live_of(slot):
        return jnp.where(lax.rem(slot, 2) < counts[lax.div(slot, 2)], 1.0, 0.0)

    @pl.loop(0, nblocks, unroll=8)
    def _(b):
        rows, weights = [], []
        for t in range(per):
            slot = src[b * per + t]
            rows.append(arrived[slot] * live_of(slot).astype(BF16))
            weights.append(tiles[b, t])
        field[b] = own[b] + dot(
            jnp.concatenate(rows, 1), jnp.concatenate(weights, 1), NT
        )

    expo = jnp.exp(field[...])
    probs = expo / jnp.sum(expo, axis=1, keepdims=True)
    grade = lax.broadcasted_iota(jnp.int32, field.shape, 1)
    onehot = jnp.where(labels[...] == grade, 1.0, 0.0)
    dlog = (probs - onehot) * scale
    field[...] = dlog
    grad_b[...] = dlog.astype(BF16)
    dlog_out[...] = field[pl.ds(me[0] * mine, mine)]
    sums[...] = jnp.zeros_like(sums)

    @pl.loop(0, nblocks, unroll=8)
    def _(b):
        back = dot(grad_b[b], jnp.concatenate([tiles[b, t] for t in range(per)], 1), NN)
        for t in range(per):
            slot = src[b * per + t]
            sums[slot] += back[:, t * BLK : (t + 1) * BLK] * live_of(slot)

    slots_out[...] = sums[...].astype(BF16)


def logits_back(src, counts, me, arrived, own, labels, tiles, scale, nfeat):
    nblocks, per = tiles.shape[:2]
    grades = arrived.shape[1]
    vmem = pl.BlockSpec(memory_space=pltpu.VMEM)
    return pl.pallas_call(
        functools.partial(logits_kernel, scale),
        grid_spec=pltpu.PrefetchScalarGridSpec(
            num_scalar_prefetch=3,
            grid=(),
            in_specs=[vmem] * 4,
            out_specs=[vmem] * 2,
            scratch_shapes=[
                pltpu.VMEM((nblocks, grades, BLK), F32),
                pltpu.VMEM((nblocks, grades, BLK), BF16),
                pltpu.VMEM(arrived.shape, F32),
            ],
        ),
        out_shape=[
            jax.ShapeDtypeStruct((nblocks // nfeat, grades, BLK), F32),
            jax.ShapeDtypeStruct(arrived.shape, BF16),
        ],
        compiler_params=params(8),
        cost_estimate=cost(nblocks * per * 2 * 64 * BLK**2, 6 * MIB),
        name="logits",
    )(src, counts, me, arrived, own, labels, tiles)


def small_kernel(table, me, returned, dlog, hidden, second, dpre_out, small, total, dproj):
    group, grades, _ = dlog.shape
    width = hidden.shape[0]

    @pl.when(pl.program_id(0) == 0)
    def _():
        total[pl.ds(0, group)] = dlog[...]

        @pl.loop(0, returned.shape[0], unroll=8)
        def _(k):
            at = table[k] - me[0] * group
            at = jnp.where((at >= 0) & (at < group), at, group)
            total[at] += returned[k].astype(F32)

        for b in range(group):
            dproj[:, b * BLK : (b + 1) * BLK] = total[b].astype(BF16)

    active = hidden[...]
    dproj_b = dproj[...]
    dpre = jnp.where(active > 0, dot(second[...], dproj_b, NN), 0.0)
    dpre_out[...] = dpre.astype(BF16)
    small[pl.ds(0, grades), :] = dot(dproj_b, active, NT)
    part = dpre[:, :BLK]
    for i in range(1, dpre.shape[1] // BLK):
        part += dpre[:, i * BLK : (i + 1) * BLK]
    small[pl.ds(grades, 8), :] = jnp.broadcast_to(
        jnp.sum(part.T, axis=0, keepdims=True), (8, width)
    )


def small_gradients(table, me, returned, dlog, hidden, second, steps):
    hid, nodes = hidden.shape
    group, grades, _ = dlog.shape
    width = hid // steps
    whole3 = lambda g, t, m: (0, 0, 0)
    return pl.pallas_call(
        small_kernel,
        grid_spec=pltpu.PrefetchScalarGridSpec(
            num_scalar_prefetch=2,
            grid=(steps,),
            in_specs=[
                pl.BlockSpec(returned.shape, whole3),
                pl.BlockSpec(dlog.shape, whole3),
                pl.BlockSpec((width, nodes), lambda g, t, m: (g, 0)),
                pl.BlockSpec((width, grades), lambda g, t, m: (g, 0)),
            ],
            out_specs=[
                pl.BlockSpec((width, nodes), lambda g, t, m: (g, 0)),
                pl.BlockSpec((grades + 8, width), lambda g, t, m: (0, g)),
            ],
            scratch_shapes=[
                pltpu.VMEM((group + 1, grades, BLK), F32),
                pltpu.VMEM((grades, nodes), BF16),
            ],
        ),
        out_shape=[
            pltpu.HBM((hid, nodes), BF16),
            jax.ShapeDtypeStruct((grades + 8, hid), F32),
        ],
        compiler_params=params(16),
        cost_estimate=cost(2 * nodes * hid * 256, 4 * MIB),
        name="small_gradients",
    )(table, me, returned, dlog, hidden, second)


def big_kernel(me, side, dpre, *refs):
    pieces, out = refs[:-1], refs[-1]
    nfeat = len(pieces) // 2
    rows = dpre[...].reshape(-1, dpre.shape[-1])
    for i, k in enumerate(ORDER):
        owner = lax.rem(me[0] + nfeat - k, nfeat)
        both = jnp.concatenate([pieces[i][...], pieces[nfeat + i][...]], 1)
        grad = dot(rows, both, NN).astype(BF16)
        out[:, owner] = grad.reshape(out.shape[0], out.shape[2], out.shape[3])


def big_gradient(me, side, dpre, pieces, parts):
    nfeat = len(pieces) // 2
    hid, nodes = dpre.shape
    cols = hid // parts
    vmem = pl.BlockSpec(memory_space=pltpu.VMEM)
    return pl.pallas_call(
        big_kernel,
        grid_spec=pltpu.PrefetchScalarGridSpec(
            num_scalar_prefetch=2,
            grid=(1,),
            in_specs=[
                pl.BlockSpec((parts // 2, 1, cols, nodes), lambda g, m, s: (0, s[0], 0, 0))
            ]
            + [vmem] * (2 * nfeat),
            out_specs=pl.BlockSpec(
                (parts // 2, nfeat, cols, 2 * BLK), lambda g, m, s: (0, 0, 0, 0)
            ),
        ),
        out_shape=jax.ShapeDtypeStruct((parts // 2, nfeat, cols, 2 * BLK), BF16),
        compiler_params=params(16),
        cost_estimate=cost(nodes * hid * hid, 4 * MIB),
        name="big_gradient",
    )(me, side, in_hbm(dpre.reshape(parts // 2, 2, cols, nodes)), *pieces)


def join_kernel(side, a, b, small, other, out):
    width = a.shape[3]
    more = out.shape[2] - a.shape[2]
    both = small[...] + other[...]
    near = both.astype(BF16).astype(F32)
    rest = both - near
    second = jnp.concatenate(
        [near[more : more + 1], rest[more : more + 1], rest[: more - 2]], 0
    )
    kept = jnp.where(side[0] == 0, near[:more], second)
    for f in range(a.shape[1]):
        share = kept[:, f * width : (f + 1) * width]
        for p in range(a.shape[0]):
            grad = a[p, f].astype(F32) + b[p, f].astype(F32)
            out[p, f] = jnp.concatenate([grad, share], 0).astype(BF16)


def join(side, a, b, small, other):
    steps = 4
    lead, nfeat, rows, width = a.shape
    more = small.shape[0] - 8
    spec = lambda n: pl.BlockSpec((lead // steps, nfeat, n, width), lambda g, s: (g, 0, 0, 0))
    whole = pl.BlockSpec(small.shape, lambda g, s: (0, 0))
    return pl.pallas_call(
        join_kernel,
        grid_spec=pltpu.PrefetchScalarGridSpec(
            num_scalar_prefetch=1,
            grid=(steps,),
            in_specs=[spec(rows), spec(rows), whole, whole],
            out_specs=spec(rows + more),
        ),
        out_shape=pltpu.HBM((lead, nfeat, rows + more, width), BF16),
        compiler_params=params(8),
        cost_estimate=cost(a.size, 4 * MIB),
        name="join",
    )(side, a, b, small, other)


def total_kernel(arrived, out, small, acc):
    g = pl.program_id(0)
    rows = out.shape[0]

    @pl.when(g == 0)
    def _():
        acc[...] = jnp.zeros_like(acc)

    total = arrived[0].astype(F32)
    for i in range(1, arrived.shape[0]):
        total += arrived[i].astype(F32)
    acc[...] += total

    @pl.when(g == pl.num_programs(0) - 1)
    def _():
        out[...] = acc[pl.ds(0, rows), :]
        small[...] = acc[pl.ds(rows, small.shape[0]), :]


def total(arrived, rows):
    n, full, width = arrived.shape
    step = n // 8
    shapes = [(rows, width), (full - rows, width)]
    return pl.pallas_call(
        total_kernel,
        grid=(n // step,),
        in_specs=[pl.BlockSpec((step, full, width), lambda g: (g, 0, 0))],
        out_specs=[pl.BlockSpec(shape, lambda g: (0, 0)) for shape in shapes],
        out_shape=[jax.ShapeDtypeStruct(shape, F32) for shape in shapes],
        scratch_shapes=[pltpu.VMEM((full, width), F32)],
        compiler_params=params(8),
        cost_estimate=cost(0, 2 * MIB),
        name="total",
    )(arrived)


def finish_kernel(side, a, b, second, bias):
    first = side[0] == 0
    near = jnp.where(first, a[...], b[...])
    rest = jnp.where(first, b[...], a[...])
    second[...] = near + jnp.concatenate([rest[2:], jnp.zeros_like(rest[:2])], 0)
    bias[...] = rest[:1] + rest[1:2]


def finish(side, a, b):
    vmem = pl.BlockSpec(memory_space=pltpu.VMEM)
    return pl.pallas_call(
        finish_kernel,
        grid_spec=pltpu.PrefetchScalarGridSpec(
            num_scalar_prefetch=1,
            grid=(),
            in_specs=[vmem] * 2,
            out_specs=[vmem] * 2,
        ),
        out_shape=[
            jax.ShapeDtypeStruct(a.shape, F32),
            jax.ShapeDtypeStruct((1, a.shape[1]), F32),
        ],
        compiler_params=params(2),
        cost_estimate=cost(0, MIB // 8),
        name="finish",
    )(side, a, b)


def shards(features, pair_count, send_blocks, tile_src, tiles, labels, w_first, b_first, w_second):
    nblocks = tile_src.shape[0]
    parts = lax.axis_size("nodes")
    nfeat = lax.axis_size("feat")
    slots = send_blocks.shape[2]
    grades = w_second.shape[1]
    hid = w_first.shape[1]
    axis = lax.axis_index("feat").astype(jnp.int32)
    me = axis.reshape(1)
    table = send_blocks.reshape(parts * slots)
    src = tile_src.reshape(-1)
    counts = pair_count.reshape(-1)

    def ahead(x, k):
        return lax.ppermute(x, "feat", [(i, (i + k) % nfeat) for i in range(nfeat)])

    def nearby(x):
        return lax.ppermute(x, "nodes", [(i, i ^ 1) for i in range(parts)])

    def swap(x):
        shaped = x.reshape(parts, slots, *x.shape[1:])
        moved = lax.all_to_all(shaped, "nodes", split_axis=0, concat_axis=0, tiled=True)
        return moved.reshape(x.shape)

    arrived = [swap(pick(features, table, 0))]
    send = pick(features, table, 1)

    high = lax.reduce_precision(b_first, 8, 7)
    middle = lax.reduce_precision(b_first - high, 8, 7)
    split = jnp.stack([high, middle, (b_first - high) - middle]).astype(BF16)
    flat = jnp.concatenate(
        [w_first.T, w_second.T, jnp.pad(split, ((0, grades - 3), (0, 0)))], 0
    )
    flats = [ahead(flat, k) for k in (2, 1, 3)]
    send, flats, arrived = lax.optimization_barrier((send, flats, arrived))
    arrived.append(swap(send))
    others = (2, 1, 3)
    make = functools.partial(aggregate, src, counts, me)
    *sent, own = make(arrived[0], tiles, features, 0, nfeat, others + (0,))
    first = [own] + [ahead(piece, k) for k, piece in zip(others, sent)]
    core = (lax.axis_index("nodes").astype(jnp.int32) % 2).reshape(1)
    flats, here, there, first[0] = lax.optimization_barrier(
        (flats, core, 1 - core, first[0])
    )
    weights, second_t, second, bias = assemble(me, [flat] + flats, hid, grades)
    arrived[1], weights, second_t, bias, second, first = lax.optimization_barrier(
        (arrived[1], weights, second_t, bias, second, first)
    )
    sent = make(arrived[1], tiles, features, 1, nfeat, others)
    last = list(make(arrived[1], tiles, features, 1, nfeat, (0,)))
    last += [ahead(piece, k) for k, piece in zip(others, sent)]
    hidden, proj = dense(first + last, weights, bias, second_t)

    projs = [proj] + [ahead(proj, k) for k in range(1, nfeat)]
    own, send = spread(table, me, projs)
    scale = 1.0 / math.sqrt(nblocks * BLK * parts)
    dlog, slotsum = logits_back(
        src, counts, me, swap(send), own, labels.reshape(nblocks, 1, BLK), tiles, scale, nfeat
    )
    dpre, small = small_gradients(table, me, swap(slotsum), dlog, hidden, second, 2)
    away = nearby(big_gradient(me, there, dpre, first + last, parts))
    big = big_gradient(me, here, dpre, first + last, parts)
    big = join(here, big, away, small, nearby(small))
    moved = lax.all_to_all(
        big.reshape(parts // 2 * nfeat, *big.shape[2:]),
        ("nodes", "feat"),
        split_axis=0,
        concat_axis=0,
        axis_index_groups=[
            [p * nfeat + f for p in range(c, parts, 2) for f in range(nfeat)] for c in range(2)
        ],
        tiled=True,
    )
    grad_first, rest = total(moved, hid // parts)
    grad_second, grad_bias = finish(here, rest, nearby(rest))
    return grad_first.T, grad_bias.reshape(-1), grad_second.T


def solution(mesh):
    placed = (
        P("nodes", "feat"),
        P("nodes", None),
        P("nodes", None, None),
        P("nodes", None),
        P("nodes", None, None, None),
        P("nodes"),
        P("feat", None),
        P("feat"),
        P("feat", None),
    )
    return jax.shard_map(
        shards,
        mesh=mesh,
        in_specs=placed,
        out_specs=(P("feat", "nodes"), P("feat"), P("feat", None)),
        check_vma=False,
    )
```

```python
import functools
import math

import jax
import jax.numpy as jnp
from jax import lax
from jax.experimental import pallas as pl
from jax.experimental.pallas import tpu as pltpu
from jax.sharding import PartitionSpec as P

F32 = jnp.float32
BF16 = jnp.bfloat16
NT = (((1,), (1,)), ((), ()))
NN = (((1,), (0,)), ((), ()))
BLK = 128
ORDER = (0, 2, 1, 3)
MIB = 1 << 20


def params(mib):
    return pltpu.CompilerParams(vmem_limit_bytes=mib * MIB)


def cost(flops, nbytes):
    return pl.CostEstimate(flops=flops, bytes_accessed=nbytes, transcendentals=0)


def dot(a, b, dims):
    return lax.dot_general(a, b, dims, preferred_element_type=F32)


def in_hbm(x):
    return pltpu.with_memory_space_constraint(x, pltpu.HBM)


def pick_kernel(chunk, table, features, out, held, sems):
    slots = out.shape[0]
    load = pltpu.make_async_copy(features.at[:, pl.ds(chunk * BLK, BLK)], held, sems.at[0])
    load.start()
    load.wait()

    @pl.loop(0, slots, unroll=8)
    def _(k):
        rows = pl.ds(pl.multiple_of(table[k] * BLK, BLK), BLK)
        pltpu.make_async_copy(held.at[rows], out.at[k], sems.at[1]).start()

    pltpu.make_async_copy(out, out, sems.at[1]).wait()


def pick(features, table, chunk):
    slots = table.shape[0]
    return pl.pallas_call(
        functools.partial(pick_kernel, chunk),
        grid_spec=pltpu.PrefetchScalarGridSpec(
            num_scalar_prefetch=1,
            grid=(),
            in_specs=[pl.BlockSpec(memory_space=pltpu.HBM)],
            out_specs=pl.BlockSpec(memory_space=pltpu.HBM),
            scratch_shapes=[
                pltpu.VMEM((features.shape[0], BLK), BF16),
                pltpu.SemaphoreType.DMA((2,)),
            ],
        ),
        out_shape=pltpu.HBM((slots, BLK, BLK), BF16),
        compiler_params=params(63),
        cost_estimate=cost(0, 4 * MIB),
        name="pick",
    )(table, in_hbm(features))


def agg_kernel(which, chunk, nfeat, src, counts, me, arrived, tiles_hbm, features, *refs):
    outs, (tiles, own, sems, *held) = refs[: len(which)], refs[len(which) :]
    group, per = tiles.shape[1:3]
    moves = []
    if held:
        moves.append(pltpu.make_async_copy(arrived, held[0], sems.at[2 * len(which)]))
        arrived = held[0]
    firsts = [lax.rem(me[0] + k, nfeat) * group for k in which]
    pairs = []
    for i, first in enumerate(firsts):
        rows = pl.ds(pl.multiple_of(first * BLK, BLK), group * BLK)
        tiles_move = pltpu.make_async_copy(
            tiles_hbm.at[pl.ds(first, group)], tiles.at[i], sems.at[2 * i]
        )
        own_move = pltpu.make_async_copy(
            features.at[rows, pl.ds(chunk * BLK, BLK)], own.at[i], sems.at[2 * i + 1]
        )
        pairs.append((tiles_move, own_move))
    for move in moves + [move for pair in pairs for move in pair]:
        move.start()
    for move in moves:
        move.wait()
    for i, (first, out) in enumerate(zip(firsts, outs)):
        for move in pairs[i]:
            move.wait()
        for b in range(group):
            rows, weights = [], []
            for t in range(per):
                slot = src[(first + b) * per + t]
                live = lax.rem(slot, 2) < counts[lax.div(slot, 2)]
                rows.append(arrived[slot])
                weights.append(tiles[i, b, t] * jnp.where(live, 1.0, 0.0).astype(BF16))
            total = dot(jnp.concatenate(weights, 1), jnp.concatenate(rows, 0), NN)
            at = pl.ds(b * BLK, BLK)
            out[at, :] = (own[i, at, :].astype(F32) + total).astype(BF16)


def aggregate(src, counts, me, arrived, tiles, features, chunk, nfeat, which):
    nblocks, per = tiles.shape[:2]
    group = nblocks // nfeat
    piece = jax.ShapeDtypeStruct((group * BLK, BLK), BF16)
    hbm = pl.BlockSpec(memory_space=pltpu.HBM)
    vmem = pl.BlockSpec(memory_space=pltpu.VMEM)
    load = chunk == 0
    return pl.pallas_call(
        functools.partial(agg_kernel, which, chunk, nfeat),
        grid_spec=pltpu.PrefetchScalarGridSpec(
            num_scalar_prefetch=3,
            grid=(),
            in_specs=[pl.BlockSpec(memory_space=pl.ANY) if load else vmem, hbm, hbm],
            out_specs=[vmem] * len(which),
            scratch_shapes=[
                pltpu.VMEM((len(which), group, per, BLK, BLK), BF16),
                pltpu.VMEM((len(which), group * BLK, BLK), BF16),
                pltpu.SemaphoreType.DMA((1 + 2 * len(which),)),
            ]
            + [pltpu.VMEM(arrived.shape, BF16)] * load,
        ),
        out_shape=[piece] * len(which),
        compiler_params=params(14),
        cost_estimate=cost(len(which) * group * per * 2 * BLK**3, 8 * MIB),
        name="aggregate",
    )(src, counts, me, arrived, in_hbm(tiles), in_hbm(features))


def assemble_kernel(me, *refs):
    flats, (weights, second_t, second, bias, consts) = refs[:4], refs[4:]
    hid, grades = second.shape
    width = flats[0].shape[1]
    consts[...] = jnp.zeros_like(consts)
    for i, k in enumerate(ORDER):
        weights[:, i * width : (i + 1) * width] = flats[i][pl.ds(0, hid), :]
        owner = lax.rem(me[0] + len(ORDER) - k, len(ORDER))
        lanes = pl.ds(pl.multiple_of(owner * width, width), width)
        tail = flats[i][pl.ds(hid, 2 * grades), :].astype(F32)
        consts[pl.ds(0, grades), lanes] = tail[:grades]
        b = (tail[grades : grades + 1] + tail[grades + 1 : grades + 2]) + tail[
            grades + 2 : grades + 3
        ]
        consts[pl.ds(grades, 8), lanes] = jnp.broadcast_to(b, (8, width))
    second_t[...] = consts[pl.ds(0, grades), :].astype(BF16)
    turned = consts[...].T
    second[...] = turned[:, :grades].astype(BF16)
    bias[...] = turned[:, grades : grades + 1]


def assemble(me, flats, hid, grades):
    vmem = pl.BlockSpec(memory_space=pltpu.VMEM)
    return pl.pallas_call(
        assemble_kernel,
        grid_spec=pltpu.PrefetchScalarGridSpec(
            num_scalar_prefetch=1,
            grid=(),
            in_specs=[vmem] * 4,
            out_specs=[vmem] * 4,
            scratch_shapes=[pltpu.VMEM((BLK, hid), F32)],
        ),
        out_shape=[
            jax.ShapeDtypeStruct((hid, hid), BF16),
            jax.ShapeDtypeStruct((grades, hid), BF16),
            jax.ShapeDtypeStruct((hid, grades), BF16),
            jax.ShapeDtypeStruct((hid, 1), F32),
        ],
        compiler_params=params(16),
        cost_estimate=cost(0, 5 * MIB),
        name="assemble",
    )(me, *flats)


def dense_kernel(nfeat, *refs):
    pieces, (weights, bias, second, hidden, proj) = refs[: 2 * nfeat], refs[2 * nfeat :]
    order = [pieces[i * nfeat + k][...] for k in range(nfeat) for i in range(2)]
    pre = dot(weights[...], jnp.concatenate(order, 1), NT)
    hid = jnp.maximum(pre + bias[...], 0.0).astype(BF16)
    hidden[...] = hid
    out = dot(second[...], hid, NN)
    for b in range(proj.shape[0]):
        proj[b] = out[:, b * BLK : (b + 1) * BLK]


def dense(pieces, weights, bias, second):
    nodes, nfeat = pieces[0].shape[0], len(pieces) // 2
    hid, width = weights.shape
    grades = second.shape[0]
    step = 512
    return pl.pallas_call(
        functools.partial(dense_kernel, nfeat),
        grid=(nodes // step,),
        in_specs=[pl.BlockSpec((step, BLK), lambda g: (g, 0))] * (2 * nfeat)
        + [
            pl.BlockSpec((hid, width), lambda g: (0, 0)),
            pl.BlockSpec((hid, 1), lambda g: (0, 0)),
            pl.BlockSpec((grades, hid), lambda g: (0, 0)),
        ],
        out_specs=[
            pl.BlockSpec((hid, step), lambda g: (0, g)),
            pl.BlockSpec((step // BLK, grades, BLK), lambda g: (g, 0, 0)),
        ],
        out_shape=[
            jax.ShapeDtypeStruct((hid, nodes), BF16),
            jax.ShapeDtypeStruct((nodes // BLK, grades, BLK), F32),
        ],
        compiler_params=params(20),
        cost_estimate=cost(2 * nodes * hid * width, 7 * MIB),
        name="dense",
    )(*pieces, weights, bias, second)


def spread_kernel(table, me, p0, p1, p2, p3, whole, out):
    nfeat, group = 4, p0.shape[0]
    for k, piece in enumerate((p0, p1, p2, p3)):
        owner = lax.rem(me[0] + nfeat - k, nfeat)
        whole[pl.ds(owner * group, group)] = piece[...]

    @pl.loop(0, out.shape[0], unroll=8)
    def _(k):
        out[k] = whole[table[k]].astype(BF16)


def spread(table, me, pieces):
    group, grades, _ = pieces[0].shape
    slots = table.shape[0]
    vmem = pl.BlockSpec(memory_space=pltpu.VMEM)
    return pl.pallas_call(
        spread_kernel,
        grid_spec=pltpu.PrefetchScalarGridSpec(
            num_scalar_prefetch=2,
            grid=(),
            in_specs=[vmem] * 4,
            out_specs=[vmem] * 2,
        ),
        out_shape=[
            jax.ShapeDtypeStruct((group * 4, grades, BLK), F32),
            jax.ShapeDtypeStruct((slots, grades, BLK), BF16),
        ],
        compiler_params=params(4),
        cost_estimate=cost(0, MIB),
        name="spread",
    )(table, me, *pieces)


def logits_kernel(
    scale, src, counts, me, arrived, own, labels, tiles, dlog_out, slots_out, field, grad_b, sums
):
    nblocks, per = tiles.shape[:2]
    grades = arrived.shape[1]
    mine = dlog_out.shape[0]

    def live_of(slot):
        return jnp.where(lax.rem(slot, 2) < counts[lax.div(slot, 2)], 1.0, 0.0)

    @pl.loop(0, nblocks, unroll=16)
    def _(b):
        rows, weights = [], []
        for t in range(per):
            slot = src[b * per + t]
            rows.append(arrived[slot] * live_of(slot).astype(BF16))
            weights.append(tiles[b, t])
        field[b] = own[b] + dot(
            jnp.concatenate(rows, 1), jnp.concatenate(weights, 1), NT
        )

    expo = jnp.exp(field[...])
    probs = expo / jnp.sum(expo, axis=1, keepdims=True)
    grade = lax.broadcasted_iota(jnp.int32, field.shape, 1)
    onehot = jnp.where(labels[...] == grade, 1.0, 0.0)
    dlog = (probs - onehot) * scale
    field[...] = dlog
    grad_b[...] = dlog.astype(BF16)
    dlog_out[...] = field[pl.ds(me[0] * mine, mine)]
    sums[...] = jnp.zeros_like(sums)

    @pl.loop(0, nblocks, unroll=16)
    def _(b):
        back = dot(grad_b[b], jnp.concatenate([tiles[b, t] for t in range(per)], 1), NN)
        for t in range(per):
            slot = src[b * per + t]
            sums[slot] += back[:, t * BLK : (t + 1) * BLK] * live_of(slot)

    slots_out[...] = sums[...].astype(BF16)


def logits_back(src, counts, me, arrived, own, labels, tiles, scale, nfeat):
    nblocks, per = tiles.shape[:2]
    grades = arrived.shape[1]
    vmem = pl.BlockSpec(memory_space=pltpu.VMEM)
    return pl.pallas_call(
        functools.partial(logits_kernel, scale),
        grid_spec=pltpu.PrefetchScalarGridSpec(
            num_scalar_prefetch=3,
            grid=(),
            in_specs=[vmem] * 4,
            out_specs=[vmem] * 2,
            scratch_shapes=[
                pltpu.VMEM((nblocks, grades, BLK), F32),
                pltpu.VMEM((nblocks, grades, BLK), BF16),
                pltpu.VMEM(arrived.shape, F32),
            ],
        ),
        out_shape=[
            jax.ShapeDtypeStruct((nblocks // nfeat, grades, BLK), F32),
            jax.ShapeDtypeStruct(arrived.shape, BF16),
        ],
        compiler_params=params(8),
        cost_estimate=cost(nblocks * per * 2 * 64 * BLK**2, 6 * MIB),
        name="logits",
    )(src, counts, me, arrived, own, labels, tiles)


def small_kernel(table, me, returned, dlog, hidden, second, dpre_out, small, total, dproj):
    group, grades, _ = dlog.shape
    width = hidden.shape[0]

    @pl.when(pl.program_id(0) == 0)
    def _():
        total[pl.ds(0, group)] = dlog[...]

        @pl.loop(0, returned.shape[0], unroll=8)
        def _(k):
            at = table[k] - me[0] * group
            at = jnp.where((at >= 0) & (at < group), at, group)
            total[at] += returned[k].astype(F32)

        for b in range(group):
            dproj[:, b * BLK : (b + 1) * BLK] = total[b].astype(BF16)

    active = hidden[...]
    dproj_b = dproj[...]
    dpre = jnp.where(active > 0, dot(second[...], dproj_b, NN), 0.0)
    dpre_out[...] = dpre.astype(BF16)
    small[pl.ds(0, grades), :] = dot(dproj_b, active, NT)
    part = dpre[:, :BLK]
    for i in range(1, dpre.shape[1] // BLK):
        part += dpre[:, i * BLK : (i + 1) * BLK]
    small[pl.ds(grades, 8), :] = jnp.broadcast_to(
        jnp.sum(part.T, axis=0, keepdims=True), (8, width)
    )


def small_gradients(table, me, returned, dlog, hidden, second, steps):
    hid, nodes = hidden.shape
    group, grades, _ = dlog.shape
    width = hid // steps
    whole3 = lambda g, t, m: (0, 0, 0)
    return pl.pallas_call(
        small_kernel,
        grid_spec=pltpu.PrefetchScalarGridSpec(
            num_scalar_prefetch=2,
            grid=(steps,),
            in_specs=[
                pl.BlockSpec(returned.shape, whole3),
                pl.BlockSpec(dlog.shape, whole3),
                pl.BlockSpec((width, nodes), lambda g, t, m: (g, 0)),
                pl.BlockSpec((width, grades), lambda g, t, m: (g, 0)),
            ],
            out_specs=[
                pl.BlockSpec((width, nodes), lambda g, t, m: (g, 0)),
                pl.BlockSpec((grades + 8, width), lambda g, t, m: (0, g)),
            ],
            scratch_shapes=[
                pltpu.VMEM((group + 1, grades, BLK), F32),
                pltpu.VMEM((grades, nodes), BF16),
            ],
        ),
        out_shape=[
            pltpu.HBM((hid, nodes), BF16),
            jax.ShapeDtypeStruct((grades + 8, hid), F32),
        ],
        compiler_params=params(16),
        cost_estimate=cost(2 * nodes * hid * 256, 4 * MIB),
        name="small_gradients",
    )(table, me, returned, dlog, hidden, second)


def big_kernel(me, side, dpre, *refs):
    pieces, out = refs[:-1], refs[-1]
    nfeat = len(pieces) // 2
    rows = dpre[...].reshape(-1, dpre.shape[-1])
    for i, k in enumerate(ORDER):
        owner = lax.rem(me[0] + nfeat - k, nfeat)
        both = jnp.concatenate([pieces[i][...], pieces[nfeat + i][...]], 1)
        grad = dot(rows, both, NN).astype(BF16)
        out[:, owner] = grad.reshape(out.shape[0], out.shape[2], out.shape[3])


def big_gradient(me, side, dpre, pieces, parts):
    nfeat = len(pieces) // 2
    hid, nodes = dpre.shape
    cols = hid // parts
    vmem = pl.BlockSpec(memory_space=pltpu.VMEM)
    return pl.pallas_call(
        big_kernel,
        grid_spec=pltpu.PrefetchScalarGridSpec(
            num_scalar_prefetch=2,
            grid=(1,),
            in_specs=[
                pl.BlockSpec((parts // 2, 1, cols, nodes), lambda g, m, s: (0, s[0], 0, 0))
            ]
            + [vmem] * (2 * nfeat),
            out_specs=pl.BlockSpec(
                (parts // 2, nfeat, cols, 2 * BLK), lambda g, m, s: (0, 0, 0, 0)
            ),
        ),
        out_shape=jax.ShapeDtypeStruct((parts // 2, nfeat, cols, 2 * BLK), BF16),
        compiler_params=params(16),
        cost_estimate=cost(nodes * hid * hid, 4 * MIB),
        name="big_gradient",
    )(me, side, in_hbm(dpre.reshape(parts // 2, 2, cols, nodes)), *pieces)


def join_kernel(side, a, b, small, other, out):
    width = a.shape[3]
    more = out.shape[2] - a.shape[2]
    both = small[...] + other[...]
    near = both.astype(BF16).astype(F32)
    rest = both - near
    second = jnp.concatenate(
        [near[more : more + 1], rest[more : more + 1], rest[: more - 2]], 0
    )
    kept = jnp.where(side[0] == 0, near[:more], second)
    for f in range(a.shape[1]):
        share = kept[:, f * width : (f + 1) * width]
        for p in range(a.shape[0]):
            grad = a[p, f].astype(F32) + b[p, f].astype(F32)
            out[p, f] = jnp.concatenate([grad, share], 0).astype(BF16)


def join(side, a, b, small, other):
    steps = 2
    lead, nfeat, rows, width = a.shape
    more = small.shape[0] - 8
    spec = lambda n: pl.BlockSpec((lead // steps, nfeat, n, width), lambda g, s: (g, 0, 0, 0))
    whole = pl.BlockSpec(small.shape, lambda g, s: (0, 0))
    return pl.pallas_call(
        join_kernel,
        grid_spec=pltpu.PrefetchScalarGridSpec(
            num_scalar_prefetch=1,
            grid=(steps,),
            in_specs=[spec(rows), spec(rows), whole, whole],
            out_specs=spec(rows + more),
        ),
        out_shape=pltpu.HBM((lead, nfeat, rows + more, width), BF16),
        compiler_params=params(12),
        cost_estimate=cost(a.size, 4 * MIB),
        name="join",
    )(side, a, b, small, other)


def total_kernel(arrived, out, small, acc):
    g = pl.program_id(0)
    rows = out.shape[0]

    @pl.when(g == 0)
    def _():
        acc[...] = jnp.zeros_like(acc)

    total = arrived[0].astype(F32)
    for i in range(1, arrived.shape[0]):
        total += arrived[i].astype(F32)
    acc[...] += total

    @pl.when(g == pl.num_programs(0) - 1)
    def _():
        out[...] = acc[pl.ds(0, rows), :]
        small[...] = acc[pl.ds(rows, small.shape[0]), :]


def total(arrived, rows):
    n, full, width = arrived.shape
    step = n // 4
    shapes = [(rows, width), (full - rows, width)]
    return pl.pallas_call(
        total_kernel,
        grid=(n // step,),
        in_specs=[pl.BlockSpec((step, full, width), lambda g: (g, 0, 0))],
        out_specs=[pl.BlockSpec(shape, lambda g: (0, 0)) for shape in shapes],
        out_shape=[jax.ShapeDtypeStruct(shape, F32) for shape in shapes],
        scratch_shapes=[pltpu.VMEM((full, width), F32)],
        compiler_params=params(8),
        cost_estimate=cost(0, 2 * MIB),
        name="total",
    )(arrived)


def finish_kernel(side, a, b, second, bias):
    first = side[0] == 0
    near = jnp.where(first, a[...], b[...])
    rest = jnp.where(first, b[...], a[...])
    second[...] = near + jnp.concatenate([rest[2:], jnp.zeros_like(rest[:2])], 0)
    bias[...] = rest[:1] + rest[1:2]


def finish(side, a, b):
    vmem = pl.BlockSpec(memory_space=pltpu.VMEM)
    return pl.pallas_call(
        finish_kernel,
        grid_spec=pltpu.PrefetchScalarGridSpec(
            num_scalar_prefetch=1,
            grid=(),
            in_specs=[vmem] * 2,
            out_specs=[vmem] * 2,
        ),
        out_shape=[
            jax.ShapeDtypeStruct(a.shape, F32),
            jax.ShapeDtypeStruct((1, a.shape[1]), F32),
        ],
        compiler_params=params(2),
        cost_estimate=cost(0, MIB // 8),
        name="finish",
    )(side, a, b)


def shards(features, pair_count, send_blocks, tile_src, tiles, labels, w_first, b_first, w_second):
    nblocks = tile_src.shape[0]
    parts = lax.axis_size("nodes")
    nfeat = lax.axis_size("feat")
    slots = send_blocks.shape[2]
    grades = w_second.shape[1]
    hid = w_first.shape[1]
    axis = lax.axis_index("feat").astype(jnp.int32)
    me = axis.reshape(1)
    table = send_blocks.reshape(parts * slots)
    src = tile_src.reshape(-1)
    counts = pair_count.reshape(-1)

    def ahead(x, k):
        return lax.ppermute(x, "feat", [(i, (i + k) % nfeat) for i in range(nfeat)])

    def nearby(x):
        return lax.ppermute(x, "nodes", [(i, i ^ 1) for i in range(parts)])

    def swap(x):
        shaped = x.reshape(parts, slots, *x.shape[1:])
        moved = lax.all_to_all(shaped, "nodes", split_axis=0, concat_axis=0, tiled=True)
        return moved.reshape(x.shape)

    arrived = [swap(pick(features, table, 0))]
    send = pick(features, table, 1)

    high = lax.reduce_precision(b_first, 8, 7)
    middle = lax.reduce_precision(b_first - high, 8, 7)
    split = jnp.stack([high, middle, (b_first - high) - middle]).astype(BF16)
    flat = jnp.concatenate(
        [w_first.T, w_second.T, jnp.pad(split, ((0, grades - 3), (0, 0)))], 0
    )
    flats = [ahead(flat, k) for k in (2, 1, 3)]
    send, flats, arrived = lax.optimization_barrier((send, flats, arrived))
    arrived.append(swap(send))
    others = (2, 1, 3)
    make = functools.partial(aggregate, src, counts, me)
    *sent, own = make(arrived[0], tiles, features, 0, nfeat, others + (0,))
    first = [own] + [ahead(piece, k) for k, piece in zip(others, sent)]
    core = (lax.axis_index("nodes").astype(jnp.int32) % 2).reshape(1)
    flats, here, there, first[0] = lax.optimization_barrier(
        (flats, core, 1 - core, first[0])
    )
    weights, second_t, second, bias = assemble(me, [flat] + flats, hid, grades)
    arrived[1], weights, second_t, bias, second, first = lax.optimization_barrier(
        (arrived[1], weights, second_t, bias, second, first)
    )
    sent = make(arrived[1], tiles, features, 1, nfeat, others)
    last = list(make(arrived[1], tiles, features, 1, nfeat, (0,)))
    last += [ahead(piece, k) for k, piece in zip(others, sent)]
    hidden, proj = dense(first + last, weights, bias, second_t)

    projs = [proj] + [ahead(proj, k) for k in range(1, nfeat)]
    own, send = spread(table, me, projs)
    scale = 1.0 / math.sqrt(nblocks * BLK * parts)
    dlog, slotsum = logits_back(
        src, counts, me, swap(send), own, labels.reshape(nblocks, 1, BLK), tiles, scale, nfeat
    )
    dpre, small = small_gradients(table, me, swap(slotsum), dlog, hidden, second, 2)
    away = nearby(big_gradient(me, there, dpre, first + last, parts))
    big = big_gradient(me, here, dpre, first + last, parts)
    big = join(here, big, away, small, nearby(small))
    moved = lax.all_to_all(
        big.reshape(parts // 2 * nfeat, *big.shape[2:]),
        ("nodes", "feat"),
        split_axis=0,
        concat_axis=0,
        axis_index_groups=[
            [p * nfeat + f for p in range(c, parts, 2) for f in range(nfeat)] for c in range(2)
        ],
        tiled=True,
    )
    grad_first, rest = total(moved, hid // parts)
    grad_second, grad_bias = finish(here, rest, nearby(rest))
    return grad_first.T, grad_bias.reshape(-1), grad_second.T


def solution(mesh):
    placed = (
        P("nodes", "feat"),
        P("nodes", None),
        P("nodes", None, None),
        P("nodes", None),
        P("nodes", None, None, None),
        P("nodes"),
        P("feat", None),
        P("feat"),
        P("feat", None),
    )
    return jax.shard_map(
        shards,
        mesh=mesh,
        in_specs=placed,
        out_specs=(P("feat", "nodes"), P("feat"), P("feat", None)),
        check_vma=False,
    )
```
